32 devices in a mesh: dp: 8 (over z, y), tensor: 4 (over x, core).
Axes of the slice: x: 2, y: 2, z: 4, core: 2. Of those that a mesh axis runs over, the one named last changes fastest.
Arguments:
- token_ids: int32 [8192], P('dp'), may hold values from 0 to 31999
- lengths: int32 [32], P('dp'), may hold values from 0 to 1024, as said below
- time_steps: int32 [32], P('dp'), may hold values from 0 to 999
- embed_table: bfloat16 [32000, 256], P(('dp', 'tensor')), may hold values from -6 to 6
- input_weight: bfloat16 [256, 1024], P('dp'), may hold values from -0.375 to 0.375
- time_weight: bfloat16 [256, 4096], P('dp'), may hold values from -0.375 to 0.375
- project_weight: bfloat16 [1024, 3072], P('dp', 'tensor'), may hold values from -0.1875 to 0.1875
- output_weight: bfloat16 [1024, 1024], P('tensor', 'dp'), may hold values from -1.5 to 1.5
- up_weight: bfloat16 [1024, 4096], P('dp', 'tensor'), may hold values from -0.25 to 0.25
- down_weight: bfloat16 [4096, 1024], P('tensor', 'dp'), may hold values from -0.125 to 0.125
- cotangent: bfloat16 [8192, 1024], P('dp'), may hold values from -6 to 6
Outputs:
- block_out: bfloat16 [8192, 1024], P('dp')
- grad_table: float32 [32000, 256], P(('dp', 'tensor'))
- grad_input: float32 [256, 1024], P('dp')
- grad_time: float32 [256, 4096], P('dp')
- grad_project: float32 [1024, 3072], P('dp', 'tensor')
- grad_output: float32 [1024, 1024], P('tensor', 'dp')
- grad_up: float32 [1024, 4096], P('dp', 'tensor')
- grad_down: float32 [4096, 1024], P('tensor', 'dp')
The draws below stay inside these ranges and needn't reach their ends.
Inputs may be any that keep to these rules, and one draw needn't show every extreme that they name: The 4 lengths of each pack, in order, fill its 1024 rows exactly; a length may be zero; in every draw some pack is a single document of 1024 rows.
All inputs are finite; a program needn't handle non-finite values.
Results may differ from the reference program's by a relative error of at most 0.017.
Values may be sent and summed in bfloat16 or wider, within the bound.
No kernel may reach another device: no remote copies, remote signals or barrier semaphores. Data moves between devices by JAX's collectives and lax.ppermute only.
A program may use at most 256 MiB of HBM per device.

```python
import math
import jax
import jax.numpy as jnp
import numpy as np
from jax import lax

D = 1024
HEADS = 16
HD = 64
FF = 4096
EMB = 256
VOCAB = 32000
ROWS = 1024
DOCS = 4
TOKENS = 8192
SEQS = 32
N_DP = 8


def draw_lengths(key, part):
    key = jax.random.fold_in(key, 11)
    cut_key, full_key = jax.random.split(key)
    groups = SEQS // DOCS
    drawn = jax.random.randint(cut_key, (groups, DOCS - 1), 0, ROWS + 1)
    cuts = jnp.sort(drawn * drawn // ROWS, axis=1).astype(jnp.int32)
    bounds = jnp.concatenate([jnp.zeros((groups, 1), jnp.int32), cuts, jnp.full((groups, 1), ROWS, jnp.int32)], axis=1)
    spans = bounds[:, 1:] - bounds[:, :-1]
    chosen = jax.random.randint(full_key, (), 0, groups)
    single = jnp.where(jnp.arange(DOCS) == 0, ROWS, 0).astype(jnp.int32)
    spans = jnp.where((jnp.arange(groups) == chosen)[:, None], single[None, :], spans)
    return spans.reshape(-1).astype(jnp.int32)


def set_ends(entries, key, low, top_value):
    longest = entries.shape.index(max(entries.shape))
    spots = []
    for shift in (0, 1):
        where = [jax.random.randint(jax.random.fold_in(key, axis), (), 0, length) for axis, length in enumerate(entries.shape)]
        where[longest] = (where[longest] + shift) % entries.shape[longest]
        spots.append(tuple(where))
    return entries.at[spots[0]].set(low).at[spots[1]].set(top_value)


def with_spikes(values, stream_key, source, target, parts, factor):
    owner, partner = [(jnp.arange(values.shape[dim]) // (values.shape[dim] // parts)).reshape([-1 if axis == dim else 1 for axis in range(values.ndim)]) for dim in (source, target)]
    chosen = jax.random.permutation(stream_key, parts)[partner]
    strong = (owner == chosen) | (owner == (partner + parts // 2) % parts)
    return jnp.where(strong, factor * values, values)


def shard_levels(stream_key, extent, cuts, least, high):
    gain, own = 1.0, jax.random.fold_in(stream_key, 6)
    for dim, blocks in cuts:
        heights = jnp.exp(jax.random.uniform(jax.random.fold_in(own, dim), (blocks,), jnp.float32, least / len(cuts), high / len(cuts)))
        gain = gain * jnp.repeat(heights, extent[dim] // blocks).reshape([-1 if axis == dim else 1 for axis in range(len(extent))])
    return gain


def rank_bounds(number_of, slope):
    portions = [(1 << 20) // math.isqrt(standing ** slope) + 1 for standing in range(1, number_of + 1)]
    spread = 1 + sum(portions) // (1 << 30)
    return np.cumsum(np.array([max(1, weight // spread) for weight in portions]))


def skewed_ids(rng, shape, amount, skew):
    grid = rank_bounds(amount, skew)
    lot = jax.random.randint(jax.random.fold_in(rng, 1), shape, 0, int(grid[amount - 1]))
    rank = jnp.searchsorted(jnp.asarray(grid, jnp.int32), lot, side="right")
    return jax.random.permutation(jax.random.fold_in(rng, 2), amount)[rank].astype(jnp.int32)


def noise(stream_key, dims, scale, reach, cuts=(), held_as=jnp.bfloat16):
    values = scale * jax.random.normal(stream_key, dims, jnp.float32)
    if cuts:
        values = values * shard_levels(stream_key, dims, cuts, -0.22, 0.18)
    return jnp.clip(values, -reach, reach).astype(held_as)


def bell_draw_with(key, shape, deviation, most, cuts, heavy, kind=jnp.bfloat16):
    array = deviation * jax.random.normal(key, shape, jnp.float32)
    if cuts:
        array = array * shard_levels(key, shape, cuts, -0.22, 0.18)
    return jnp.clip(with_spikes(array, jax.random.fold_in(key, 3), *heavy), -most, most).astype(kind)


def setup_inputs(seed: int = 0) -> dict:
    streams_of = jax.random.split(jax.random.key(seed), 12)
    token_ids = set_ends(skewed_ids(streams_of[0], (TOKENS,), VOCAB, 2), jax.random.fold_in(streams_of[0], 3), 0, VOCAB - 1).astype(jnp.int32)
    lengths = draw_lengths(jax.random.fold_in(streams_of[11], 71), 0)
    time_steps = set_ends(jax.random.randint(streams_of[2], (SEQS,), 0, 1000), jax.random.fold_in(streams_of[2], 1), 0, 999).astype(jnp.int32)
    embed_table = noise(streams_of[3], (VOCAB, EMB), 1.0, 6.0, ((0, 32),))
    input_weight = noise(streams_of[4], (EMB, D), EMB ** -0.5, 0.375, ((0, 8),))
    time_weight = noise(streams_of[5], (EMB, 4 * D), EMB ** -0.5, 0.375, ((0, 8),))
    project_weight = noise(streams_of[6], (D, 3 * D), D ** -0.5, 0.1875, ((0, 8), (1, 4)))
    output_weight = noise(streams_of[7], (D, D), (D * 16 // ROWS) ** -0.5, 1.5, ((0, 4), (1, 8)))
    up_weight = noise(streams_of[8], (D, FF), (D // 2) ** -0.5, 0.25, ((0, 8), (1, 4)))
    down_weight = noise(streams_of[9], (FF, D), (FF // 2) ** -0.5, 0.125, ((0, 4), (1, 8)))
    cotangent = bell_draw_with(streams_of[10], (TOKENS, D), 1.0, 6.0, ((0, 8),), (0, 1, 8, 2.0))
    return {"token_ids": token_ids, "lengths": lengths, "time_steps": time_steps, "embed_table": embed_table, "input_weight": input_weight, "time_weight": time_weight, "project_weight": project_weight, "output_weight": output_weight, "up_weight": up_weight, "down_weight": down_weight, "cotangent": cotangent}


@jax.custom_vjp
def low(v):
    return lax.optimization_barrier(v.astype(jnp.bfloat16)).astype(jnp.float32)

@jax.custom_vjp
def low_back(v):
    return v

def low_keep(v):
    return (low(v), None)

def low_pass(kept, grad):
    return (grad,)

def back_keep(v):
    return (v, None)

def back_low(kept, grad):
    return (low(grad),)
low.defvjp(low_keep, low_pass)
low_back.defvjp(back_keep, back_low)

def matmul(left, right):
    return jnp.dot(left, right, precision=lax.Precision.HIGHEST)

def normalize(table_rows):
    return table_rows * lax.rsqrt(lax.optimization_barrier(jnp.mean(table_rows * table_rows, axis=1, keepdims=True)) + 1e-06)

def layer_norm(value, scale, shift):
    centred = value - lax.optimization_barrier(jnp.mean(value, axis=-1, keepdims=True))
    return centred * lax.rsqrt(lax.optimization_barrier(jnp.mean(centred * centred, axis=-1, keepdims=True)) + 1e-05) * (1.0 + scale) + shift

def time_features(step_index, width):
    half = width // 2
    frequency = jnp.exp(-math.log(10000.0) * jnp.arange(half).astype(jnp.float32) / half)
    angles = step_index.astype(jnp.float32)[:, None] * frequency[None, :]
    return jnp.concatenate([jnp.sin(angles), jnp.cos(angles)], axis=1)

def pack_forward(params, pack):
    normed, input_weight, time_weight, project_weight, output_weight, up_weight, down_weight = params
    pack_ids, pack_lengths, pack_steps = pack
    ends = jnp.cumsum(pack_lengths).astype(jnp.int32)
    position = jnp.arange(ROWS, dtype=jnp.int32)
    document = lax.optimization_barrier(jnp.sum((position[:, None] >= ends[None, :]).astype(jnp.int32), axis=1))
    same_doc = document[:, None] == document[None, :]
    embed = low_back(jnp.take(normed, pack_ids, axis=0))
    stream_zero = low_back(matmul(embed, input_weight))
    features = low(time_features(pack_steps, EMB))
    row_mods = jnp.take(matmul(features, time_weight), document, axis=0)
    scale_one, shift_one, scale_two, shift_two = jnp.split(row_mods, 4, axis=1)
    hidden_one = low(layer_norm(stream_zero, scale_one, shift_one))
    projected = low_back(low(matmul(hidden_one, project_weight))).reshape(ROWS, HEADS, 3, HD)
    query = jnp.transpose(projected[:, :, 0], (1, 0, 2))
    keys = jnp.transpose(projected[:, :, 1], (1, 0, 2))
    values = jnp.transpose(projected[:, :, 2], (1, 0, 2))
    factor = 1.0 / math.sqrt(HD)

    def attend(head):
        head_query, head_keys, head_values = head
        scores = low_back(matmul(head_query, head_keys.T) * factor)
        scores = jnp.where(same_doc, scores, -1e+30)
        peak = lax.optimization_barrier(jnp.max(scores, axis=1, keepdims=True))
        expo = jnp.exp(scores - peak)
        probs = expo / lax.optimization_barrier(jnp.sum(expo, axis=1, keepdims=True))
        return matmul(low(probs), head_values)
    attended = lax.map(jax.checkpoint(attend), (query, keys, values))
    attended = low_back(low(jnp.transpose(attended, (1, 0, 2)).reshape(ROWS, D)))
    stream_one = stream_zero + low_back(matmul(attended, output_weight))
    hidden_two = low(layer_norm(stream_one, scale_two, shift_two))
    upward = low_back(matmul(hidden_two, up_weight))
    activated = low(jax.nn.gelu(upward, approximate=False))
    return stream_one + low_back(matmul(activated, down_weight))

def forward(params, token_ids, lengths, time_steps):
    normed = low(normalize(params[0]))
    inner = (normed,) + tuple(params[1:])
    packs = (token_ids.reshape(N_DP, ROWS), lengths.reshape(N_DP, DOCS), time_steps.reshape(N_DP, DOCS))

    def one_pack(pack):
        return pack_forward(inner, pack)
    return lax.map(jax.checkpoint(one_pack), packs)

def reference(token_ids, lengths, time_steps, embed_table, input_weight, time_weight, project_weight, output_weight, up_weight, down_weight, cotangent):
    params = tuple((arg.astype(jnp.float32) for arg in (embed_table, input_weight, time_weight, project_weight, output_weight, up_weight, down_weight)))

    def wrapped(*inputs):
        return forward(inputs, token_ids, lengths, time_steps)
    result, pullback = jax.vjp(wrapped, *params)
    grads = pullback(cotangent.astype(jnp.float32).reshape(N_DP, ROWS, D))
    block_out = result.reshape(TOKENS, D).astype(jnp.bfloat16)
    return (block_out, grads[0], grads[1], grads[2], grads[3], grads[4], grads[5], grads[6])
```

```python
import math

import jax
import jax.numpy as jnp
from jax import lax
from jax.sharding import PartitionSpec as P

HD = 64
EMB = 256

table_eps = 1e-06
norm_eps = 1e-05
bf16 = jnp.bfloat16
f32 = jnp.float32


def dot(left, right, dims=((1,), (0,))):
    return lax.dot_general(left, right, (dims, ((), ())), preferred_element_type=f32)


SWAP_CORE = [(0, 1), (1, 0), (2, 3), (3, 2)]
SWAP_X = [(0, 2), (2, 0), (1, 3), (3, 1)]


def swap_core(value):
    return lax.ppermute(value, "tensor", SWAP_CORE)


def swap_x(value):
    return lax.ppermute(value, "tensor", SWAP_X)


class Direct:
    def __init__(self, count):
        self.count, self.chain = count, count // 2
        me = lax.axis_index("dp")
        z, y = me // 2, me % 2
        self.places = [
            ((z - dz) % self.chain) * 2 + (y ^ dy) for dy in range(2) for dz in range(self.chain)
        ]

    def step(self, value, dz, dy):
        pairs = [
            (z * 2 + y, ((z + dz) % self.chain) * 2 + (y ^ dy))
            for z in range(self.chain)
            for y in range(2)
        ]
        return lax.ppermute(value, "dp", pairs)

    def spread(self, value):
        near = [value] + [self.step(value, dz, 0) for dz in range(1, self.chain)]
        return near + [self.step(value, dz, 1) for dz in range(self.chain)]

    def spread_small(self, value):
        both = jnp.stack([value, self.step(value, 0, 1)])
        rings = [both] + [self.step(both, dz, 0) for dz in range(1, self.chain)]
        return [ring[dy] for dy in range(2) for ring in rings]

    def collect(self, values):
        arrived = [values[0]]
        for k in range(1, self.count):
            dy, dz = divmod(k, self.chain)
            arrived.append(self.step(values[k], -dz, dy))
        return arrived

    def gather(self, block, axis):
        near = jnp.concatenate(
            [block] + [self.step(block, dz, 0) for dz in range(1, self.chain)], axis=axis
        )
        return jnp.concatenate([near, self.step(near, 0, 1)], axis=axis)

    def scatter(self, whole, axis):
        near, far = jnp.split(whole, 2, axis=axis)
        near = near + self.step(far.astype(bf16), 0, 1).astype(f32)
        blocks = jnp.split(near, self.chain, axis=axis)
        total = blocks[0]
        for dz in range(1, self.chain):
            total = total + self.step(blocks[dz].astype(bf16), -dz, 0).astype(f32)
        return total


class Plain:
    def __init__(self, count):
        self.count = count
        self.places = list(range(count))

    def spread(self, value):
        return list(lax.all_gather(value, "dp"))

    spread_small = spread

    def collect(self, values):
        stacked = jnp.stack(values).astype(f32)
        return [lax.psum_scatter(stacked, "dp", scatter_dimension=0, tiled=False)]

    def gather(self, block, axis):
        return lax.all_gather(block, "dp", axis=axis, tiled=True)

    def scatter(self, whole, axis):
        return lax.psum_scatter(whole, "dp", scatter_dimension=axis, tiled=True)


def block_order(value, places, axis):
    size = value.shape[axis] // len(places)
    return jnp.concatenate(
        [lax.dynamic_slice_in_dim(value, place * size, size, axis) for place in places], axis=axis
    )


def split_two(value):
    high = value.astype(bf16)
    return high, (value - high.astype(f32)).astype(bf16)


def fold(value, width):
    return jnp.concatenate(jnp.split(value, value.shape[1] // width, axis=1), axis=0)


def unfold(value, count):
    return jnp.concatenate(jnp.split(value, count, axis=0), axis=1)


def norm_parts(value):
    centred = value - jnp.mean(value, axis=-1, keepdims=True)
    inverse = lax.rsqrt(jnp.mean(centred * centred, axis=-1, keepdims=True) + norm_eps)
    return centred * inverse, inverse


def norm_back(grad, normal, inverse, scale):
    inner = grad * (1.0 + scale)
    return inverse * (
        inner
        - jnp.mean(inner, axis=-1, keepdims=True)
        - normal * jnp.mean(inner * normal, axis=-1, keepdims=True)
    )


def per_device(
    token_ids,
    lengths,
    time_steps,
    embed_table,
    input_weight,
    time_weight,
    project_weight,
    output_weight,
    up_weight,
    down_weight,
    cotangent,
):
    rows = token_ids.shape[0]
    half, quarter = rows // 2, rows // 4
    count = lax.axis_size("dp")
    groups = lax.axis_size("tensor")
    me = lax.axis_index("dp")
    place = lax.axis_index("tensor")
    x, c = place // 2, place % 2
    width = cotangent.shape[1]
    docs = lengths.shape[0]
    shard = embed_table.shape[0]
    emb_rows = input_weight.shape[0]
    direct = count % 2 == 0 and count <= 8 and (width // count) % 128 == 0
    dp = Direct(count) if direct else Plain(count)
    places = dp.places
    inverse_places = [
        sum(jnp.where(jnp.int32(places[k]) == a, k, 0) for k in range(count)) for a in range(count)
    ]

    table = embed_table.astype(f32)
    rscale = lax.rsqrt(jnp.mean(table * table, axis=1, keepdims=True) + table_eps)
    normed = (table * rscale).astype(bf16)
    pair = jnp.concatenate([normed, swap_x(normed)], axis=0)
    shards = jnp.concatenate([pair, swap_core(pair)], axis=0)
    owners = [x * 2 + c, (1 - x) * 2 + c, x * 2 + 1 - c, (1 - x) * 2 + 1 - c]
    vocab = jnp.concatenate(
        [(me * groups + owner) * shard + jnp.arange(shard, dtype=jnp.int32) for owner in owners]
    )

    my_ids = lax.dynamic_slice_in_dim(token_ids, (c * 2 + x) * quarter, quarter)
    heard = dp.spread_small(jnp.concatenate([my_ids, time_steps]))
    ids = [message[:quarter] for message in heard]
    steps = jnp.concatenate([message[quarter:] for message in heard])
    feature = me * emb_rows + jnp.arange(emb_rows, dtype=jnp.int32)
    part = EMB // 2
    frequency = jnp.exp(-math.log(10000.0) * (feature % part).astype(f32) / part)
    angles = steps.astype(f32)[:, None] * frequency[None, :]
    features = jnp.where(feature[None, :] < part, jnp.sin(angles), jnp.cos(angles)).astype(bf16)

    packed_one = jnp.concatenate(
        [project_weight, fold(input_weight, EMB), unfold(output_weight, 2)], axis=1
    ) if direct else None
    if direct:
        whole_one = dp.gather(packed_one, 0)
        head_width = project_weight.shape[1]
        project = whole_one[:, :head_width]
        per = width // count
        input_rel = [
            unfold(whole_one[k * per : (k + 1) * per, head_width : head_width + EMB], width // EMB)
            for k in range(count)
        ]
        output = jnp.concatenate(
            [
                fold(whole_one[k * per : (k + 1) * per, head_width + EMB :], per)
                for k in range(count)
            ],
            axis=1,
        )
        input_rows = block_order(jnp.concatenate(input_rel, axis=0), inverse_places, 0)
        input_full = block_order(input_rows, places, 1)
    else:
        project = dp.gather(project_weight, 0)
        input_full = dp.gather(input_weight, 0)
        output = dp.gather(output_weight, 1)
    down = dp.gather(down_weight, 1)
    up = dp.gather(up_weight, 0)

    time_part = lax.dynamic_slice_in_dim(time_weight, place * width, width, 1)
    messages = []
    for k in range(count):
        onehot = (ids[k][:, None] == vocab[None, :]).astype(bf16)
        found = dot(onehot, shards).astype(bf16)
        mods = dot(features[k * docs : (k + 1) * docs], time_part)
        high, low = split_two(mods)
        messages.append(
            jnp.concatenate([found, fold(jnp.concatenate([high, low], axis=0), EMB)], axis=0)
        )
    arrived = sum(message.astype(f32) for message in dp.collect(messages))
    embed_quarter = arrived[:quarter].astype(bf16)
    mods = unfold(arrived[quarter:], width // EMB)
    mods = mods[:docs] + mods[docs:]
    mods = block_order(mods, places, 1)
    high, low = split_two(mods)
    mine = jnp.concatenate(
        [embed_quarter, fold(jnp.concatenate([high, low], axis=0), EMB)], axis=0
    )
    other = swap_x(mine)
    both = jnp.stack([jnp.where(x == 0, mine, other), jnp.where(x == 0, other, mine)])
    far = swap_core(both)
    embed = jnp.concatenate(
        [both[0, :quarter], far[0, :quarter], both[1, :quarter], far[1, :quarter]], axis=0
    )
    blocks = []
    for at in range(2):
        first = jnp.where(c == 0, both[at, quarter:], far[at, quarter:])
        second = jnp.where(c == 0, far[at, quarter:], both[at, quarter:])
        blocks += [unfold(first, width // EMB), unfold(second, width // EMB)]
    position = jnp.concatenate(
        [
            start + jnp.arange(quarter, dtype=jnp.int32)
            for start in (c * half, (1 - c) * half, c * half + quarter, (1 - c) * half + quarter)
        ]
    )
    ends = jnp.cumsum(lengths)
    document = jnp.sum((position[:, None] >= ends[None, :]).astype(jnp.int32), axis=1)
    member = document[:, None] == jnp.arange(docs, dtype=jnp.int32)[None, :]
    member = member.astype(bf16)
    member_two = jnp.concatenate([member, member], axis=1)

    def own(value):
        return jnp.concatenate([value[:quarter], value[half : half + quarter]], axis=0)

    member_own = own(member)
    member_two_own = own(member_two)

    stream_zero = dot(embed, input_full)
    normal_one, inverse_one = norm_parts(stream_zero)
    scale_one = dot(member_two, blocks[0])
    hidden_one = (normal_one * (1.0 + scale_one) + dot(member_two, blocks[1])).astype(bf16)
    stream_zero = own(stream_zero)
    normal_one, inverse_one = norm_parts(stream_zero)

    projected = dot(hidden_one, project).astype(bf16)
    heads = projected.shape[1] // (3 * HD)
    split = projected.reshape(rows, heads, 3, HD)
    query = jnp.transpose(split[:, :, 0], (1, 0, 2)) * jnp.asarray(1.0 / math.sqrt(HD), bf16)
    keys = jnp.transpose(split[:, :, 1], (1, 0, 2))
    values = jnp.transpose(split[:, :, 2], (1, 0, 2))
    same = (document[:, None] == document[None, :])[None]

    def batched(left, right, spec):
        return jnp.einsum(spec, left, right, preferred_element_type=f32)

    scores = jnp.where(same, batched(query, keys, "hqd,hkd->hqk"), -1e30)
    peak = jnp.max(scores, axis=2, keepdims=True)
    expo = jnp.exp(scores - peak)
    total = jnp.sum(expo, axis=2, keepdims=True)
    probs = (expo / total).astype(bf16)
    attended = (
        jnp.transpose(batched(probs, values, "hqk,hkd->hqd"), (1, 0, 2))
        .reshape(rows, heads * HD)
        .astype(bf16)
    )

    def reduce_chunk(partial):
        mine = partial[:quarter] + swap_core(partial[quarter:].astype(bf16)).astype(f32)
        mine = mine.astype(bf16)
        return mine.astype(f32) + swap_x(mine).astype(f32)

    cot = cotangent.reshape(4, quarter, width)
    cot = jnp.where(
        c == 0,
        jnp.concatenate([cot[0], cot[2], cot[1], cot[3]], axis=0),
        jnp.concatenate([cot[2], cot[0], cot[3], cot[1]], axis=0),
    )
    if direct:
        cot = block_order(cot, places, 1)
    attention = [
        reduce_chunk(dot(attended[at * half : (at + 1) * half], output)) for at in range(2)
    ]
    stream_one, normals, inverses, scales, hidden_two = [], [], [], [], []
    for at in range(2):
        stream = stream_zero[at * quarter : (at + 1) * quarter] + attention[at]
        normal, inverse = norm_parts(stream)
        members = member_two_own[at * quarter : (at + 1) * quarter]
        scale = dot(members, blocks[2])
        hidden = (normal * (1.0 + scale) + dot(members, blocks[3])).astype(bf16)
        hidden_two.append(jnp.concatenate([hidden, swap_core(hidden)], axis=0))
        stream_one.append(stream)
        normals.append(normal)
        inverses.append(inverse)
        scales.append(scale)
    activated, grad_upward, grad_two, branch = [], [], [], []
    for at in range(2):
        upward = dot(hidden_two[at], up)
        phi = 0.5 * (1.0 + lax.erf(upward * math.sqrt(0.5)))
        active = (upward * phi).astype(bf16)
        slope = phi + upward * (math.sqrt(0.5 / math.pi) * jnp.exp(-0.5 * upward * upward))
        grad_active = dot(cot[at * half : (at + 1) * half], down, ((1,), (1,)))
        grad_up_rows = (grad_active * slope).astype(bf16)
        activated.append(active)
        grad_upward.append(grad_up_rows)
        grad_two.append(reduce_chunk(dot(grad_up_rows, up, ((1,), (1,)))))
    for at in range(2):
        branch.append(reduce_chunk(dot(activated[at], down)))
    activated = jnp.concatenate(activated, axis=0)
    grad_upward = jnp.concatenate(grad_upward, axis=0)
    hidden_two = jnp.concatenate(hidden_two, axis=0)
    grad_down = dot(activated, cot, ((0,), (0,)))
    grad_up = dot(hidden_two, grad_upward, ((0,), (0,)))
    summed_down = dp.scatter(grad_down, 1)
    summed_up = dp.scatter(grad_up, 0)

    out_blocks = []
    for at in range(2):
        block = (stream_one[at] + branch[at]).astype(bf16)
        out_blocks += [block, swap_core(block)]
    block_out = jnp.where(
        c == 0,
        jnp.concatenate([out_blocks[b] for b in (0, 2, 1, 3)], axis=0),
        jnp.concatenate([out_blocks[b] for b in (1, 3, 0, 2)], axis=0),
    )
    if direct:
        block_out = block_order(block_out, inverse_places, 1)

    grad_one, grad_attn, grad_scale_two, grad_shift_two = [], [], 0.0, 0.0
    for at in range(2):
        grad = grad_two[at]
        back = norm_back(grad, normals[at], inverses[at], scales[at])
        stream = cot[at * half : at * half + quarter].astype(f32) + back
        low = stream.astype(bf16)
        grad_attn += [low, swap_core(low)]
        grad_one.append(stream)
        members = member_own[at * quarter : (at + 1) * quarter]
        grad_scale_two += dot(members, (grad * normals[at]).astype(bf16), ((0,), (0,)))
        grad_shift_two += dot(members, grad.astype(bf16), ((0,), (0,)))
    grad_attn = jnp.concatenate(grad_attn, axis=0)
    grad_output = dot(attended, grad_attn, ((0,), (0,)))
    grad_attended = dot(grad_attn, output, ((1,), (1,))).astype(bf16)
    grad_heads = jnp.transpose(grad_attended.reshape(rows, heads, HD), (1, 0, 2))
    attended_heads = jnp.transpose(attended.reshape(rows, heads, HD), (1, 0, 2))
    inner = jnp.sum(
        grad_heads.astype(f32) * attended_heads.astype(f32), axis=2, keepdims=True
    )
    grad_probs = batched(grad_heads, values, "hqd,hkd->hqk")
    grad_scores = (probs.astype(f32) * (grad_probs - inner)).astype(bf16)
    grad_query = batched(grad_scores, keys, "hqk,hkd->hqd") * (1.0 / math.sqrt(HD))
    grad_keys = batched(grad_scores, query, "hqk,hqd->hkd")
    grad_values = batched(probs, grad_heads, "hqk,hqd->hkd")
    grad_projected = (
        jnp.transpose(jnp.stack([grad_query, grad_keys, grad_values], axis=2), (1, 0, 2, 3))
        .reshape(rows, heads * 3 * HD)
        .astype(bf16)
    )
    grad_hidden_one = [
        reduce_chunk(dot(grad_projected[at * half : (at + 1) * half], project, ((1,), (1,))))
        for at in range(2)
    ]
    grad_project = dot(hidden_one, grad_projected, ((0,), (0,)))
    if direct:
        per = width // count
        grad_output = jnp.concatenate(
            [unfold(grad_output[:, k * per : (k + 1) * per], 2) for k in range(count)], axis=0
        )
        summed_one = dp.scatter(jnp.concatenate([grad_project, grad_output], axis=1), 0)
        summed_project = summed_one[:, : grad_project.shape[1]]
        summed_output = fold(summed_one[:, grad_project.shape[1] :], per)
    else:
        summed_project = dp.scatter(grad_project, 0)
        summed_output = dp.scatter(grad_output, 1)

    grad = jnp.concatenate(grad_hidden_one, axis=0)
    back = norm_back(grad, normal_one, inverse_one, own(scale_one))
    grad_zero = (back + jnp.concatenate(grad_one, axis=0)).astype(bf16)
    grad_scale_one = dot(member_own, (grad * normal_one).astype(bf16), ((0,), (0,)))
    grad_shift_one = dot(member_own, grad.astype(bf16), ((0,), (0,)))
    grad_embed = dot(grad_zero, input_full, ((1,), (1,))).astype(bf16)
    grad_embed = jnp.where(x == 0, grad_embed[:quarter], grad_embed[quarter:])
    grad_mods = jnp.concatenate(
        [grad_scale_one, grad_shift_one, grad_scale_two, grad_shift_two], axis=0
    )
    grad_mods = block_order(grad_mods, inverse_places, 1)
    grad_mods = grad_mods + swap_core(grad_mods)
    mod_part = lax.dynamic_slice_in_dim(grad_mods, place * docs, docs, 0).astype(bf16)
    grad_input = dot(own(embed), grad_zero, ((0,), (0,)))
    grad_input = block_order(grad_input, inverse_places, 1)
    columns = width // groups
    mine = lax.dynamic_slice_in_dim(grad_input, place * columns, columns, 1)
    partner = lax.dynamic_slice_in_dim(grad_input, (x * 2 + 1 - c) * columns, columns, 1)
    mine = (mine + swap_core(partner.astype(bf16)).astype(f32)).astype(bf16)
    for_places = [lax.dynamic_slice_in_dim(mine, p * emb_rows, emb_rows, 0) for p in places]
    to_all = jnp.concatenate([grad_embed, fold(mod_part, EMB)], axis=0)
    if direct:
        arrived = []
        for k in range(count):
            dy, dz = divmod(k, dp.chain)
            message = jnp.concatenate([to_all, for_places[(-dz) % dp.chain + dy * dp.chain]], axis=0)
            arrived.append(message if k == 0 else dp.step(message, dz, dy))
        extra = arrived[0].shape[0] - emb_rows
        input_part = sum(message[extra:].astype(f32) for message in arrived)
    else:
        arrived = dp.spread(to_all)
        input_part = dp.collect([block.astype(f32) for block in for_places])[0]
        extra = to_all.shape[0]
    grad_tokens = jnp.concatenate([message[:quarter] for message in arrived], axis=0)
    all_mods = jnp.concatenate(
        [unfold(message[quarter:extra], width // EMB) for message in arrived], axis=0
    )
    time_grad = dot(features, all_mods, ((0,), (0,)))
    small = jnp.concatenate([time_grad, input_part], axis=1)
    other = swap_x(small)
    both = jnp.stack([jnp.where(x == 0, small, other), jnp.where(x == 0, other, small)])
    far = swap_core(both)
    pieces = []
    for at in range(2):
        pieces += [jnp.where(c == 0, both[at], far[at]), jnp.where(c == 0, far[at], both[at])]
    summed_time = jnp.concatenate([piece[:, :width] for piece in pieces], axis=1)
    summed_input = jnp.concatenate([piece[:, width:] for piece in pieces], axis=1)

    all_ids = jnp.concatenate(ids)

    def table_part(at):
        names = vocab[at * 2 * shard : (at + 1) * 2 * shard]
        onehot = (names[:, None] == all_ids[None, :]).astype(bf16)
        return dot(onehot, grad_tokens)

    far = swap_core(table_part(1).astype(bf16))
    near = table_part(0) + far.astype(f32)
    grad_normed = near[:shard] + swap_x(near[shard:].astype(bf16)).astype(f32)
    grad_table = rscale * grad_normed - table * (
        rscale * rscale * rscale * jnp.mean(grad_normed * table, axis=1, keepdims=True)
    )
    return (
        block_out,
        grad_table,
        summed_input,
        summed_time,
        summed_project,
        summed_output,
        summed_up,
        summed_down,
    )


def solution(mesh):
    return jax.shard_map(
        per_device,
        mesh=mesh,
        in_specs=(
            P("dp"),
            P("dp"),
            P("dp"),
            P(("dp", "tensor"), None),
            P("dp", None),
            P("dp", None),
            P("dp", "tensor"),
            P("tensor", "dp"),
            P("dp", "tensor"),
            P("tensor", "dp"),
            P("dp", None),
        ),
        out_specs=(
            P("dp", None),
            P(("dp", "tensor"), None),
            P("dp", None),
            P("dp", None),
            P("dp", "tensor"),
            P("tensor", "dp"),
            P("dp", "tensor"),
            P("tensor", "dp"),
        ),
        check_vma=False,
    )
```

```python
import functools
import math

import jax
import jax.numpy as jnp
from jax import lax
from jax.experimental import pallas as pl
from jax.experimental.pallas import tpu as pltpu
from jax.sharding import PartitionSpec as P

HD = 64
EMB = 256

table_eps = 1e-06
norm_eps = 1e-05
bf16 = jnp.bfloat16
f32 = jnp.float32


def dot(left, right, dims=((1,), (0,))):
    return lax.dot_general(left, right, (dims, ((), ())), preferred_element_type=f32)


def after(value, *others):
    return lax.optimization_barrier((value,) + others)[0]


SWAP_CORE = [(0, 1), (1, 0), (2, 3), (3, 2)]
SWAP_X = [(0, 2), (2, 0), (1, 3), (3, 1)]


def swap_core(value):
    return lax.ppermute(value, "tensor", SWAP_CORE)


def swap_x(value):
    return lax.ppermute(value, "tensor", SWAP_X)


class Direct:
    def __init__(self, count):
        self.count, self.chain = count, count // 2
        me = lax.axis_index("dp")
        z, y = me // 2, me % 2
        self.places = [
            ((z - dz) % self.chain) * 2 + (y ^ dy) for dy in range(2) for dz in range(self.chain)
        ]

    def step(self, value, dz, dy):
        pairs = [
            (z * 2 + y, ((z + dz) % self.chain) * 2 + (y ^ dy))
            for z in range(self.chain)
            for y in range(2)
        ]
        return lax.ppermute(value, "dp", pairs)

    def spread(self, value):
        near = [value] + [self.step(value, dz, 0) for dz in range(1, self.chain)]
        return near + [self.step(value, dz, 1) for dz in range(self.chain)]

    def spread_small(self, value):
        both = jnp.stack([value, self.step(value, 0, 1)])
        rings = [both] + [self.step(both, dz, 0) for dz in range(1, self.chain)]
        return [ring[dy] for dy in range(2) for ring in rings]

    def collect(self, values):
        arrived = [values[0]]
        for k in range(1, self.count):
            dy, dz = divmod(k, self.chain)
            arrived.append(self.step(values[k], -dz, dy))
        return arrived

    def reverse(self, arrived):
        return [
            arrived[dy * self.chain + -dz % self.chain]
            for dy in range(2)
            for dz in range(self.chain)
        ]

    def gather_near(self, block, axis):
        return jnp.concatenate(
            [block] + [self.step(block, dz, 0) for dz in range(1, self.chain)], axis=axis
        )

    def gather_far(self, near, axis):
        return jnp.concatenate([near, self.step(near, 0, 1)], axis=axis)

    def scatter_far(self, whole, axis):
        near, far = jnp.split(whole, 2, axis=axis)
        return near, self.step(far.astype(bf16), 0, 1)

    def scatter_near(self, near, far, axis):
        blocks = jnp.split(near + far.astype(f32), self.chain, axis=axis)
        total = blocks[0]
        for dz in range(1, self.chain):
            total = total + self.step(blocks[dz].astype(bf16), -dz, 0).astype(f32)
        return total


class Plain:
    def __init__(self, count):
        self.count = count
        self.places = list(range(count))

    def spread(self, value):
        return list(lax.all_gather(value, "dp"))

    spread_small = spread

    def collect(self, values):
        stacked = jnp.stack(values).astype(f32)
        return [lax.psum_scatter(stacked, "dp", scatter_dimension=0, tiled=False)]

    def gather_near(self, block, axis):
        return lax.all_gather(block, "dp", axis=axis, tiled=True)

    def gather_far(self, near, axis):
        return near

    def scatter_far(self, whole, axis):
        return whole, None

    def scatter_near(self, near, far, axis):
        return lax.psum_scatter(near, "dp", scatter_dimension=axis, tiled=True)


def block_order(value, places, axis):
    size = value.shape[axis] // len(places)
    return jnp.concatenate(
        [lax.dynamic_slice_in_dim(value, place * size, size, axis) for place in places], axis=axis
    )


def split_two(value):
    high = value.astype(bf16)
    return high, (value - high.astype(f32)).astype(bf16)


def fold(value, width):
    return jnp.concatenate(jnp.split(value, value.shape[1] // width, axis=1), axis=0)


def unfold(value, count):
    return jnp.concatenate(jnp.split(value, count, axis=0), axis=1)


def permute_kernel(row_places, column_places, source, target):
    rows = source.shape[0] // row_places.shape[0]
    columns = source.shape[1] // column_places.shape[0]
    for i in range(row_places.shape[0]):
        for j in range(column_places.shape[0]):
            first = pl.multiple_of(row_places[i] * rows, rows)
            second = pl.multiple_of(column_places[j] * columns, columns)
            target[i * rows : (i + 1) * rows, j * columns : (j + 1) * columns] = source[
                pl.ds(first, rows), pl.ds(second, columns)
            ]


def permute(value, row_places, column_places):
    lists = [jnp.stack([jnp.int32(p) for p in places]) for places in (row_places, column_places)]
    return pl.pallas_call(
        permute_kernel,
        out_shape=jax.ShapeDtypeStruct(value.shape, value.dtype),
        in_specs=[pl.BlockSpec(memory_space=pltpu.SMEM)] * 2
        + [pl.BlockSpec(memory_space=pltpu.VMEM)],
        out_specs=pl.BlockSpec(memory_space=pltpu.VMEM),
        compiler_params=pltpu.CompilerParams(vmem_limit_bytes=32 << 20),
        name="permute",
    )(*lists, value)


ROWS_OF_BOTH = ((1,), (1,))
COLUMNS_OF_BOTH = ((0,), (0,))


def attention_kernel(heads, same_row, same_column, query, keys, values, attended, logsum):
    same = same_row[...] == same_column[...]
    q, k, v = query[...], keys[...], values[...]
    head = lax.broadcasted_iota(jnp.int32, q.shape, 1) // HD
    total_out = jnp.zeros(q.shape, f32)
    for h in range(heads):
        scores = dot(jnp.where(head == h, q, jnp.zeros_like(q)), k, ROWS_OF_BOTH)
        scores = jnp.where(same, scores, -1e30)
        peak = jnp.max(scores, axis=1, keepdims=True)
        expo = jnp.exp(scores - peak)
        total = jnp.sum(expo, axis=1, keepdims=True)
        total_out = jnp.where(head == h, dot(expo.astype(bf16), v) / total, total_out)
        logsum[:, h : h + 1] = peak + jnp.log(total)
    attended[...] = total_out.astype(bf16)


def attention(document, query, keys, values):
    rows, width = query.shape
    heads = width // HD
    block = min(512, rows)
    part = pl.BlockSpec((block, width), lambda i: (i, 0))
    whole = pl.BlockSpec((rows, width), lambda i: (0, 0))
    return pl.pallas_call(
        functools.partial(attention_kernel, heads),
        grid=(rows // block,),
        in_specs=[
            pl.BlockSpec((block, 1), lambda i: (i, 0)),
            pl.BlockSpec((1, rows), lambda i: (0, 0)),
            part,
            whole,
            whole,
        ],
        out_specs=[part, pl.BlockSpec((block, heads), lambda i: (i, 0))],
        out_shape=[
            jax.ShapeDtypeStruct((rows, width), bf16),
            jax.ShapeDtypeStruct((rows, heads), f32),
        ],
        compiler_params=pltpu.CompilerParams(vmem_limit_bytes=48 << 20),
        cost_estimate=pl.CostEstimate(
            flops=4 * rows * rows * width * 4, bytes_accessed=8 * rows * width, transcendentals=0
        ),
        name="attention",
    )(document[:, None], document[None, :], query, keys, values)


def attention_back_kernel(
    heads,
    count,
    same_row,
    same_column,
    query,
    keys,
    values,
    grad_attended,
    attended,
    logsum,
    grad_query,
    grad_keys,
    grad_values,
    sum_keys,
    sum_values,
):
    at = pl.program_id(0)
    same = same_row[...] == same_column[...]
    q, k, v, g = query[...], keys[...], values[...], grad_attended[...]
    head = lax.broadcasted_iota(jnp.int32, q.shape, 1) // HD
    product = g.astype(f32) * attended[...].astype(f32)

    @pl.when(at == 0)
    def _():
        sum_keys[...] = jnp.zeros_like(sum_keys)
        sum_values[...] = jnp.zeros_like(sum_values)

    out = jnp.zeros(q.shape, f32)
    for h in range(heads):
        here = head == h
        q_head = jnp.where(here, q, jnp.zeros_like(q))
        g_head = jnp.where(here, g, jnp.zeros_like(g))
        scores = jnp.where(same, dot(q_head, k, ROWS_OF_BOTH), -1e30)
        probs = jnp.exp(scores - logsum[:, h : h + 1])
        inner = jnp.sum(jnp.where(here, product, 0.0), axis=1, keepdims=True)
        grad_scores = probs * (dot(g_head, v, ROWS_OF_BOTH) - inner)
        grad_scores = grad_scores.astype(bf16)
        out = jnp.where(here, dot(grad_scores, k), out)
        sum_keys[...] += dot(grad_scores, q_head, COLUMNS_OF_BOTH)
        sum_values[...] += dot(probs.astype(bf16), g_head, COLUMNS_OF_BOTH)
    grad_query[...] = (out * (1.0 / math.sqrt(HD))).astype(bf16)

    @pl.when(at == count - 1)
    def _():
        grad_keys[...] = sum_keys[...].astype(bf16)
        grad_values[...] = sum_values[...].astype(bf16)


def attention_back(document, query, keys, values, grad_attended, attended, logsum):
    rows, width = query.shape
    heads = width // HD
    block = min(512, rows)
    part = pl.BlockSpec((block, width), lambda i: (i, 0))
    whole = pl.BlockSpec((rows, width), lambda i: (0, 0))
    return pl.pallas_call(
        functools.partial(attention_back_kernel, heads, rows // block),
        grid=(rows // block,),
        in_specs=[
            pl.BlockSpec((block, 1), lambda i: (i, 0)),
            pl.BlockSpec((1, rows), lambda i: (0, 0)),
            part,
            whole,
            whole,
            part,
            part,
            pl.BlockSpec((block, heads), lambda i: (i, 0)),
        ],
        out_specs=[part, whole, whole],
        out_shape=[jax.ShapeDtypeStruct((rows, width), bf16)] * 3,
        scratch_shapes=[pltpu.VMEM((rows, width), f32)] * 2,
        compiler_params=pltpu.CompilerParams(vmem_limit_bytes=48 << 20),
        cost_estimate=pl.CostEstimate(
            flops=10 * rows * rows * width * 4, bytes_accessed=16 * rows * width, transcendentals=0
        ),
        name="attention_back",
    )(document[:, None], document[None, :], query, keys, values, grad_attended, attended, logsum)


def norm_parts(value):
    centred = value - jnp.mean(value, axis=-1, keepdims=True)
    inverse = lax.rsqrt(jnp.mean(centred * centred, axis=-1, keepdims=True) + norm_eps)
    return centred * inverse, inverse


def norm_back(grad, normal, inverse, scale):
    inner = grad * (1.0 + scale)
    return inverse * (
        inner
        - jnp.mean(inner, axis=-1, keepdims=True)
        - normal * jnp.mean(inner * normal, axis=-1, keepdims=True)
    )


def per_device(
    token_ids,
    lengths,
    time_steps,
    embed_table,
    input_weight,
    time_weight,
    project_weight,
    output_weight,
    up_weight,
    down_weight,
    cotangent,
):
    rows = token_ids.shape[0]
    half, quarter = rows // 2, rows // 4
    count = lax.axis_size("dp")
    groups = lax.axis_size("tensor")
    me = lax.axis_index("dp")
    place = lax.axis_index("tensor")
    x, c = place // 2, place % 2
    width = cotangent.shape[1]
    docs = lengths.shape[0]
    shard = embed_table.shape[0]
    emb_rows = input_weight.shape[0]
    direct = count % 2 == 0 and count <= 8 and (width // count) % 128 == 0
    dp = Direct(count) if direct else Plain(count)
    places = dp.places
    inverse_places = [
        sum(jnp.where(jnp.int32(places[k]) == a, k, 0) for k in range(count)) for a in range(count)
    ]

    order, back_order = (places, inverse_places) if direct else ([0], [0])

    table = embed_table.astype(f32)
    rscale = lax.rsqrt(jnp.mean(table * table, axis=1, keepdims=True) + table_eps)
    normed = (table * rscale).astype(bf16)
    my_ids = lax.dynamic_slice_in_dim(token_ids, (c * 2 + x) * quarter, quarter)
    heard = dp.spread_small(jnp.concatenate([my_ids, time_steps]))
    ids = [message[:quarter] for message in heard]
    steps = jnp.concatenate([message[quarter:] for message in heard])

    pair = jnp.concatenate([normed, swap_x(normed)], axis=0)
    shards = jnp.concatenate([pair, swap_core(pair)], axis=0)
    entry = jnp.arange(4 * shard, dtype=jnp.int32)
    which = entry // shard
    owner = (x ^ (which & 1)) * 2 + (c ^ (which >> 1))
    vocab = (me * groups + owner) * shard + entry % shard

    feature = me * emb_rows + jnp.arange(emb_rows, dtype=jnp.int32)
    part = EMB // 2
    frequency = jnp.exp(-math.log(10000.0) * (feature % part).astype(f32) / part)
    angles = steps.astype(f32)[:, None] * frequency[None, :]
    features = jnp.where(feature[None, :] < part, jnp.sin(angles), jnp.cos(angles)).astype(bf16)

    head_width = project_weight.shape[1]
    heads = head_width // (3 * HD)
    per = width // count
    ordered = project_weight.reshape(per, heads, 3, HD).transpose(0, 2, 1, 3)
    ordered = ordered.reshape(per, head_width)
    project_near = dp.gather_near(after(ordered, steps), 0)
    columns = width // groups
    input_part = lax.dynamic_slice_in_dim(input_weight, place * columns, columns, 1)

    time_part = lax.dynamic_slice_in_dim(time_weight, place * width, width, 1)
    messages = []
    for k in range(count):
        onehot = (ids[k][:, None] == vocab[None, :]).astype(bf16)
        found = dot(onehot, shards).astype(bf16)
        mods = dot(features[k * docs : (k + 1) * docs], time_part)
        high, low = split_two(mods)
        small = fold(jnp.concatenate([high, low], axis=0), EMB)
        if direct:
            small = jnp.concatenate([small, fold(input_part, EMB)], axis=0)
        messages.append(jnp.concatenate([found, small], axis=0))
    arrived = dp.collect(messages)
    extra = quarter + 8 * docs
    if direct:
        input_rel = jnp.concatenate([message[extra:] for message in dp.reverse(arrived)], axis=0)
    else:
        input_rel = lax.all_gather(input_part, "dp", axis=0, tiled=True)
    arrived = sum(message[:extra].astype(f32) for message in arrived)
    project_far = dp.gather_far(after(project_near, messages[-1]), 0)
    output_near = dp.gather_near(after(output_weight, arrived), 1)
    up_near = dp.gather_near(after(up_weight, arrived), 0)
    embed_quarter = arrived[:quarter].astype(bf16)
    mods = unfold(arrived[quarter:], width // EMB)
    mods = mods[:docs] + mods[docs:]
    if direct:
        mods = block_order(mods, places, 1)
    high, low = split_two(mods)
    small = fold(jnp.concatenate([high, low], axis=0), EMB)
    mine = jnp.concatenate([embed_quarter, small, input_rel], axis=0)
    other = swap_x(mine)
    both = jnp.stack([jnp.where(x == 0, mine, other), jnp.where(x == 0, other, mine)])
    far = swap_core(both)
    embed = jnp.concatenate(
        [both[0, :quarter], far[0, :quarter], both[1, :quarter], far[1, :quarter]], axis=0
    )
    ordered = []
    for at in range(2):
        ordered.append(jnp.where(c == 0, both[at, quarter:], far[at, quarter:]))
        ordered.append(jnp.where(c == 0, far[at, quarter:], both[at, quarter:]))
    blocks = [unfold(block[: 8 * docs], width // EMB) for block in ordered]
    input_full = jnp.concatenate([block[8 * docs :] for block in ordered], axis=1)
    if direct:
        input_full = permute(input_full, inverse_places, places)
    position = jnp.concatenate(
        [
            start + jnp.arange(quarter, dtype=jnp.int32)
            for start in (c * half, (1 - c) * half, c * half + quarter, (1 - c) * half + quarter)
        ]
    )
    ends = jnp.cumsum(lengths)
    document = jnp.sum((position[:, None] >= ends[None, :]).astype(jnp.int32), axis=1)
    member = document[:, None] == jnp.arange(docs, dtype=jnp.int32)[None, :]
    member = member.astype(bf16)
    member_two = jnp.concatenate([member, member], axis=1)

    def own(value):
        return jnp.concatenate([value[:quarter], value[half : half + quarter]], axis=0)

    member_own = own(member)
    member_two_own = own(member_two)

    stream_zero = dot(embed, input_full)
    normal_one, inverse_one = norm_parts(stream_zero)
    scale_one = dot(member_two, blocks[0])
    hidden_one = (normal_one * (1.0 + scale_one) + dot(member_two, blocks[1])).astype(bf16)
    stream_zero = own(stream_zero)
    normal_one, inverse_one = norm_parts(stream_zero)

    projected = dot(hidden_one, project_far).astype(bf16)
    third = heads * HD
    query = projected[:, :third] * jnp.asarray(1.0 / math.sqrt(HD), bf16)
    keys = projected[:, third : 2 * third]
    values = projected[:, 2 * third :]
    down_near = dp.gather_near(after(down_weight, projected), 1)
    output = dp.gather_far(after(output_near, projected), 1)
    attended, logsum = attention(document, query, keys, values)
    up = dp.gather_far(after(up_near, projected), 0)

    def reduce_chunk(partial):
        mine = partial[:quarter] + swap_core(partial[quarter:].astype(bf16)).astype(f32)
        mine = mine.astype(bf16)
        return mine.astype(f32) + swap_x(mine).astype(f32)

    row_places = [2 * c, 2 * (1 - c), 2 * c + 1, 2 * (1 - c) + 1]
    cot = permute(after(cotangent, steps), row_places, order)
    attention_sum = [
        reduce_chunk(dot(attended[at * half : (at + 1) * half], output)) for at in range(2)
    ]
    stream_one, normals, inverses, scales, hidden_two = [], [], [], [], []
    for at in range(2):
        stream = stream_zero[at * quarter : (at + 1) * quarter] + attention_sum[at]
        normal, inverse = norm_parts(stream)
        members = member_two_own[at * quarter : (at + 1) * quarter]
        scale = dot(members, blocks[2])
        hidden = (normal * (1.0 + scale) + dot(members, blocks[3])).astype(bf16)
        hidden_two.append(jnp.concatenate([hidden, swap_core(hidden)], axis=0))
        stream_one.append(stream)
        normals.append(normal)
        inverses.append(inverse)
        scales.append(scale)
    down = dp.gather_far(after(down_near, attention_sum[0]), 1)
    activated, grad_upward, grad_two, branch = [], [], [], []
    for at in range(2):
        upward = dot(hidden_two[at], up)
        phi = 0.5 * (1.0 + lax.erf(upward * math.sqrt(0.5)))
        active = (upward * phi).astype(bf16)
        slope = phi + upward * (math.sqrt(0.5 / math.pi) * jnp.exp(-0.5 * upward * upward))
        grad_active = dot(cot[at * half : (at + 1) * half], down, ROWS_OF_BOTH)
        grad_up_rows = (grad_active * slope).astype(bf16)
        activated.append(active)
        grad_upward.append(grad_up_rows)
        grad_two.append(reduce_chunk(dot(grad_up_rows, up, ROWS_OF_BOTH)))
    activated = jnp.concatenate(activated, axis=0)
    grad_upward = jnp.concatenate(grad_upward, axis=0)
    hidden_two = jnp.concatenate(hidden_two, axis=0)
    grad_down = dot(activated, cot, COLUMNS_OF_BOTH)
    grad_up = dot(hidden_two, grad_upward, COLUMNS_OF_BOTH)
    down_mine, down_far = dp.scatter_far(grad_down, 1)
    branch_sent = dot(activated, down)

    grad_one, grad_attn, grad_scale_two, grad_shift_two = [], [], 0.0, 0.0
    for at in range(2):
        grad = grad_two[at]
        back = norm_back(grad, normals[at], inverses[at], scales[at])
        stream = cot[at * half : at * half + quarter].astype(f32) + back
        low = stream.astype(bf16)
        grad_attn += [low, swap_core(low)]
        grad_one.append(stream)
        members = member_own[at * quarter : (at + 1) * quarter]
        grad_scale_two += dot(members, (grad * normals[at]).astype(bf16), COLUMNS_OF_BOTH)
        grad_shift_two += dot(members, grad.astype(bf16), COLUMNS_OF_BOTH)
    grad_attn = jnp.concatenate(grad_attn, axis=0)
    if direct:
        summed_down = dp.scatter_near(down_mine, after(down_far, grad_one[0]), 1)
        up_mine, up_far = dp.scatter_far(after(grad_up, down_far, grad_one[0]), 0)
    else:
        summed_down = dp.scatter_near(down_mine, None, 1)
        up_mine, up_far = dp.scatter_far(grad_up, 0)
    grad_output = dot(attended, grad_attn, COLUMNS_OF_BOTH)
    grad_attended = dot(grad_attn, output, ROWS_OF_BOTH).astype(bf16)
    two = 2 * HD
    grad_parts = []
    for at in range(0, third, two):
        lanes = slice(at, at + two)
        grad_parts.append(
            attention_back(
                document,
                query[:, lanes],
                keys[:, lanes],
                values[:, lanes],
                grad_attended[:, lanes],
                attended[:, lanes],
                logsum[:, at // HD : at // HD + 2],
            )
        )
    grad_projected = jnp.concatenate(
        [parts[which] for which in range(3) for parts in grad_parts], axis=1
    )
    if direct:
        summed_up = dp.scatter_near(up_mine, after(up_far, grad_projected), 0)
    else:
        summed_up = dp.scatter_near(up_mine, None, 0)
    grad_hidden_one = [
        reduce_chunk(dot(grad_projected[at * half : (at + 1) * half], project_far, ROWS_OF_BOTH))
        for at in range(2)
    ]
    grad_project = dot(hidden_one, grad_projected, COLUMNS_OF_BOTH)
    if direct:
        grad_output = jnp.concatenate(
            [unfold(grad_output[:, k * per : (k + 1) * per], 2) for k in range(count)], axis=0
        )
        one_mine, one_far = dp.scatter_far(
            jnp.concatenate([grad_project, grad_output], axis=1), 0
        )
        summed_one = dp.scatter_near(one_mine, one_far, 0)
        summed_project = summed_one[:, :head_width]
        summed_output = fold(summed_one[:, head_width:], per)
    else:
        summed_project = dp.scatter_near(grad_project, None, 0)
        summed_output = dp.scatter_near(grad_output, None, 1)
    summed_project = (
        summed_project.reshape(per, 3, heads, HD).transpose(0, 2, 1, 3).reshape(per, head_width)
    )

    branch_sent = after(branch_sent, grad_hidden_one[1])
    out_blocks = []
    for at in range(2):
        branch = reduce_chunk(branch_sent[at * half : (at + 1) * half])
        block = (stream_one[at] + branch).astype(bf16)
        out_blocks += [block, swap_core(block)]
    back_places = [c, 2 + c, 1 - c, 3 - c]
    block_out = permute(jnp.concatenate(out_blocks, axis=0), back_places, back_order)

    grad = jnp.concatenate(grad_hidden_one, axis=0)
    back = norm_back(grad, normal_one, inverse_one, own(scale_one))
    grad_zero = (back + jnp.concatenate(grad_one, axis=0)).astype(bf16)
    grad_scale_one = dot(member_own, (grad * normal_one).astype(bf16), COLUMNS_OF_BOTH)
    grad_shift_one = dot(member_own, grad.astype(bf16), COLUMNS_OF_BOTH)
    grad_embed = dot(grad_zero, input_full, ROWS_OF_BOTH).astype(bf16)
    grad_embed = jnp.where(x == 0, grad_embed[:quarter], grad_embed[quarter:])
    grad_mods = jnp.concatenate(
        [grad_scale_one, grad_shift_one, grad_scale_two, grad_shift_two], axis=0
    )
    if direct:
        grad_mods = block_order(grad_mods, inverse_places, 1)
    grad_mods = grad_mods + swap_core(grad_mods)
    mod_part = lax.dynamic_slice_in_dim(grad_mods, place * docs, docs, 0).astype(bf16)
    grad_input = dot(own(embed), grad_zero, COLUMNS_OF_BOTH)
    if direct:
        grad_input = permute(grad_input, [0], inverse_places)
    mine = lax.dynamic_slice_in_dim(grad_input, place * columns, columns, 1)
    partner = lax.dynamic_slice_in_dim(grad_input, (x * 2 + 1 - c) * columns, columns, 1)
    mine = (mine + swap_core(partner.astype(bf16)).astype(f32)).astype(bf16)
    for_places = [lax.dynamic_slice_in_dim(mine, p * emb_rows, emb_rows, 0) for p in places]
    to_all = jnp.concatenate([grad_embed, fold(mod_part, EMB)], axis=0)
    if direct:
        arrived = []
        for k in range(count):
            dy, dz = divmod(k, dp.chain)
            message = jnp.concatenate([to_all, for_places[(-dz) % dp.chain + dy * dp.chain]], axis=0)
            arrived.append(message if k == 0 else dp.step(message, dz, dy))
        extra = arrived[0].shape[0] - emb_rows
        input_part = sum(message[extra:].astype(f32) for message in arrived)
    else:
        arrived = dp.spread(to_all)
        input_part = dp.collect([block.astype(f32) for block in for_places])[0]
        extra = to_all.shape[0]
    grad_tokens = jnp.concatenate([message[:quarter] for message in arrived], axis=0)
    all_mods = jnp.concatenate(
        [unfold(message[quarter:extra], width // EMB) for message in arrived], axis=0
    )
    time_grad = dot(features, all_mods, COLUMNS_OF_BOTH)
    small = jnp.concatenate([time_grad, input_part], axis=1)
    other = swap_x(small)
    both = jnp.stack([jnp.where(x == 0, small, other), jnp.where(x == 0, other, small)])
    far = swap_core(both)
    pieces = []
    for at in range(2):
        pieces += [jnp.where(c == 0, both[at], far[at]), jnp.where(c == 0, far[at], both[at])]
    summed_time = jnp.concatenate([piece[:, :width] for piece in pieces], axis=1)
    summed_input = jnp.concatenate([piece[:, width:] for piece in pieces], axis=1)

    all_ids = jnp.concatenate(ids)

    def table_part(at):
        names = vocab[at * 2 * shard : (at + 1) * 2 * shard]
        onehot = (names[:, None] == all_ids[None, :]).astype(bf16)
        return dot(onehot, grad_tokens)

    far = swap_core(table_part(1).astype(bf16))
    near = table_part(0) + far.astype(f32)
    grad_normed = near[:shard] + swap_x(near[shard:].astype(bf16)).astype(f32)
    grad_table = rscale * grad_normed - table * (
        rscale * rscale * rscale * jnp.mean(grad_normed * table, axis=1, keepdims=True)
    )
    return (
        block_out,
        grad_table,
        summed_input,
        summed_time,
        summed_project,
        summed_output,
        summed_up,
        summed_down,
    )


def solution(mesh):
    return jax.shard_map(
        per_device,
        mesh=mesh,
        in_specs=(
            P("dp"),
            P("dp"),
            P("dp"),
            P(("dp", "tensor"), None),
            P("dp", None),
            P("dp", None),
            P("dp", "tensor"),
            P("tensor", "dp"),
            P("dp", "tensor"),
            P("tensor", "dp"),
            P("dp", None),
        ),
        out_specs=(
            P("dp", None),
            P(("dp", "tensor"), None),
            P("dp", None),
            P("dp", None),
            P("dp", "tensor"),
            P("tensor", "dp"),
            P("dp", "tensor"),
            P("tensor", "dp"),
        ),
        check_vma=False,
    )
```

```python
import functools
import math

import jax
import jax.numpy as jnp
from jax import lax
from jax.experimental import pallas as pl
from jax.experimental.pallas import tpu as pltpu
from jax.sharding import PartitionSpec as P

HD = 64
EMB = 256

table_eps = 1e-06
norm_eps = 1e-05
bf16 = jnp.bfloat16
f32 = jnp.float32


def dot(left, right, dims=((1,), (0,))):
    return lax.dot_general(left, right, (dims, ((), ())), preferred_element_type=f32)


def after(value, *others):
    return lax.optimization_barrier((value,) + others)[0]


SWAP_CORE = [(0, 1), (1, 0), (2, 3), (3, 2)]
SWAP_X = [(0, 2), (2, 0), (1, 3), (3, 1)]


def swap_core(value):
    return lax.ppermute(value, "tensor", SWAP_CORE)


def swap_x(value):
    return lax.ppermute(value, "tensor", SWAP_X)


ROWS_OF_BOTH = ((1,), (1,))
COLUMNS_OF_BOTH = ((0,), (0,))
ORDER = (0, 4, 2, 6, 1, 5, 3, 7)


class Direct:
    def __init__(self, count):
        self.count = count
        self.me = lax.axis_index("dp")
        self.places = [self.me ^ v for v in ORDER]
        self.inverse = [
            sum(jnp.where(self.places[k] == a, k, 0) for k in range(count)) for a in range(count)
        ]

    def swap(self, value, v):
        return lax.ppermute(value, "dp", [(i, i ^ v) for i in range(self.count)])

    def spread_small(self, value):
        value = value[None]
        for v in (4, 2, 1):
            value = jnp.concatenate([value, self.swap(value, v)], axis=0)
        return value


class Plain:
    def __init__(self, count):
        self.count = count
        self.me = lax.axis_index("dp")
        self.places = self.inverse = list(range(count))

    def spread_small(self, value):
        return lax.all_gather(value, "dp")


def picked(value, places, axis):
    size = value.shape[axis] // len(ORDER)
    return jnp.concatenate(
        [lax.slice_in_dim(value, p * size, (p + 1) * size, axis=axis) for p in places], axis=axis
    )


def split_two(value):
    high = value.astype(bf16)
    return high, (value - high.astype(f32)).astype(bf16)


def fold(value, width):
    return jnp.concatenate(jnp.split(value, value.shape[1] // width, axis=1), axis=0)


def unfold(value, count):
    return jnp.concatenate(jnp.split(value, count, axis=0), axis=1)


def permute_kernel(row_places, column_places, source, target):
    rows = source.shape[0] // row_places.shape[0]
    columns = source.shape[1] // column_places.shape[0]
    for i in range(row_places.shape[0]):
        for j in range(column_places.shape[0]):
            first = pl.multiple_of(row_places[i] * rows, rows)
            second = pl.multiple_of(column_places[j] * columns, columns)
            target[i * rows : (i + 1) * rows, j * columns : (j + 1) * columns] = source[
                pl.ds(first, rows), pl.ds(second, columns)
            ]


def permute(value, row_places, column_places):
    lists = [jnp.stack([jnp.int32(p) for p in places]) for places in (row_places, column_places)]
    return pl.pallas_call(
        permute_kernel,
        out_shape=jax.ShapeDtypeStruct(value.shape, value.dtype),
        in_specs=[pl.BlockSpec(memory_space=pltpu.SMEM)] * 2
        + [pl.BlockSpec(memory_space=pltpu.VMEM)],
        out_specs=pl.BlockSpec(memory_space=pltpu.VMEM),
        compiler_params=pltpu.CompilerParams(vmem_limit_bytes=32 << 20),
        name="permute",
    )(*lists, value)


def attention_kernel(heads, same_row, same_column, query, keys, values, attended, logsum):
    same = same_row[...] == same_column[...]
    q, k, v = query[...], keys[...], values[...]
    head = lax.broadcasted_iota(jnp.int32, q.shape, 1) // HD
    total_out = jnp.zeros(q.shape, f32)
    for h in range(heads):
        scores = dot(jnp.where(head == h, q, jnp.zeros_like(q)), k, ROWS_OF_BOTH)
        scores = jnp.where(same, scores, -1e30)
        peak = jnp.max(scores, axis=1, keepdims=True)
        expo = jnp.exp(scores - peak)
        total = jnp.sum(expo, axis=1, keepdims=True)
        total_out = jnp.where(head == h, dot(expo.astype(bf16), v) / total, total_out)
        logsum[:, h : h + 1] = peak + jnp.log(total)
    attended[...] = total_out.astype(bf16)


def attention(document, query, keys, values):
    rows, width = query.shape
    heads = width // HD
    block = min(512, rows)
    part = pl.BlockSpec((block, width), lambda i: (i, 0))
    whole = pl.BlockSpec((rows, width), lambda i: (0, 0))
    return pl.pallas_call(
        functools.partial(attention_kernel, heads),
        grid=(rows // block,),
        in_specs=[
            pl.BlockSpec((block, 1), lambda i: (i, 0)),
            pl.BlockSpec((1, rows), lambda i: (0, 0)),
            part,
            whole,
            whole,
        ],
        out_specs=[part, pl.BlockSpec((block, heads), lambda i: (i, 0))],
        out_shape=[
            jax.ShapeDtypeStruct((rows, width), bf16),
            jax.ShapeDtypeStruct((rows, heads), f32),
        ],
        compiler_params=pltpu.CompilerParams(vmem_limit_bytes=48 << 20),
        cost_estimate=pl.CostEstimate(
            flops=4 * rows * rows * width * 4, bytes_accessed=8 * rows * width, transcendentals=0
        ),
        name="attention",
    )(document[:, None], document[None, :], query, keys, values)


def attention_back_kernel(
    count,
    same_row,
    same_column,
    query,
    keys,
    values,
    grad_attended,
    attended,
    logsum,
    grad_projected,
    sum_keys,
    sum_values,
):
    pair, at = pl.program_id(0), pl.program_id(1)
    same = same_row[...] == same_column[...]
    q, k, v, g = query[...], keys[...], values[...], grad_attended[...]
    rows, lanes = q.shape
    head = lax.broadcasted_iota(jnp.int32, q.shape, 1) // HD
    product = g.astype(f32) * attended[...].astype(f32)
    logs = logsum[...]
    lane = lax.broadcasted_iota(jnp.int32, logs.shape, 1)

    @pl.when(at == 0)
    def _():
        sum_keys[...] = jnp.zeros_like(sum_keys)
        sum_values[...] = jnp.zeros_like(sum_values)

    out = jnp.zeros(q.shape, f32)
    for h in range(lanes // HD):
        here = head == h
        q_head = jnp.where(here, q, jnp.zeros_like(q))
        g_head = jnp.where(here, g, jnp.zeros_like(g))
        log = jnp.sum(jnp.where(lane == pair * (lanes // HD) + h, logs, 0.0), 1, keepdims=True)
        scores = jnp.where(same, dot(q_head, k, ROWS_OF_BOTH), -1e30)
        probs = jnp.exp(scores - log)
        inner = jnp.sum(jnp.where(here, product, 0.0), axis=1, keepdims=True)
        grad_scores = probs * (dot(g_head, v, ROWS_OF_BOTH) - inner)
        grad_scores = grad_scores.astype(bf16)
        out = jnp.where(here, dot(grad_scores, k), out)
        sum_keys[...] += dot(grad_scores, q_head, COLUMNS_OF_BOTH)
        sum_values[...] += dot(probs.astype(bf16), g_head, COLUMNS_OF_BOTH)
    third = grad_projected.shape[1] // 3
    first = pl.multiple_of(at * rows, rows)
    grad_projected[pl.ds(first, rows), pl.ds(pl.multiple_of(pair * lanes, lanes), lanes)] = (
        out * (1.0 / math.sqrt(HD))
    ).astype(bf16)

    @pl.when(at == count - 1)
    def _():
        for which, total in ((1, sum_keys), (2, sum_values)):
            start = pl.multiple_of(which * third + pair * lanes, lanes)
            grad_projected[:, pl.ds(start, lanes)] = total[...].astype(bf16)


def attention_back(document, query, keys, values, grad_attended, attended, logsum):
    rows, width = query.shape
    heads = width // HD
    block, lanes = min(512, rows), 2 * HD
    part = pl.BlockSpec((block, lanes), lambda p, i: (i, p))
    whole = pl.BlockSpec((rows, lanes), lambda p, i: (0, p))
    return pl.pallas_call(
        functools.partial(attention_back_kernel, rows // block),
        grid=(width // lanes, rows // block),
        in_specs=[
            pl.BlockSpec((block, 1), lambda p, i: (i, 0)),
            pl.BlockSpec((1, rows), lambda p, i: (0, 0)),
            part,
            whole,
            whole,
            part,
            part,
            pl.BlockSpec((block, heads), lambda p, i: (i, 0)),
        ],
        out_specs=pl.BlockSpec((rows, 3 * width), lambda p, i: (0, 0)),
        out_shape=jax.ShapeDtypeStruct((rows, 3 * width), bf16),
        scratch_shapes=[pltpu.VMEM((rows, lanes), f32)] * 2,
        compiler_params=pltpu.CompilerParams(vmem_limit_bytes=48 << 20),
        cost_estimate=pl.CostEstimate(
            flops=10 * rows * rows * width * 4, bytes_accessed=16 * rows * width, transcendentals=0
        ),
        name="attention_back",
    )(document[:, None], document[None, :], query, keys, values, grad_attended, attended, logsum)


def vmem(shape, index=None):
    if index is None:
        return pl.BlockSpec(shape, lambda *_: (0,) * len(shape))
    return pl.BlockSpec(shape, index)


def estimate(flops, moved):
    return pl.CostEstimate(flops=flops, bytes_accessed=moved, transcendentals=0)


def finish_kernel(direct, docs, places, *refs):
    *arrived, target = refs
    rows = arrived[0].shape[0] - 8 * docs
    total = arrived[0][:rows].astype(f32)
    high = arrived[0][rows : rows + 4 * docs].astype(f32)
    low = arrived[0][rows + 4 * docs :].astype(f32)
    for ref in arrived[1:]:
        total += ref[:rows].astype(f32)
        high += ref[rows : rows + 4 * docs].astype(f32)
        low += ref[rows + 4 * docs :].astype(f32)
    target[:rows] = total.astype(bf16)
    mods = high + low
    if direct:
        lanes = mods.shape[1] // 2
        blocks = [
            mods[(a // 2) * docs : (a // 2 + 1) * docs, (a % 2) * lanes : (a % 2 + 1) * lanes]
            for a in range(8)
        ]
        ordered = []
        for p in range(8):
            block = jnp.zeros_like(blocks[0])
            for a in range(8):
                block = jnp.where(places[p] == a, blocks[a], block)
            ordered.append(block)
        mods = jnp.concatenate(
            [jnp.concatenate(ordered[2 * q : 2 * q + 2], axis=1) for q in range(4)], axis=0
        )
    first = mods.astype(bf16)
    target[rows:] = jnp.concatenate(
        [first, (mods - first.astype(f32)).astype(bf16)], axis=0
    )


def finish(direct, docs, places, arrived):
    return pl.pallas_call(
        functools.partial(finish_kernel, direct, docs),
        in_specs=[pl.BlockSpec(memory_space=pltpu.SMEM)]
        + [pl.BlockSpec(memory_space=pltpu.VMEM)] * len(arrived),
        out_specs=pl.BlockSpec(memory_space=pltpu.VMEM),
        out_shape=jax.ShapeDtypeStruct(arrived[0].shape, bf16),
        name="finish",
    )(jnp.stack([jnp.int32(p) for p in places]), *arrived)


def row_mods(document, folded, docs):
    lane = lax.broadcasted_iota(jnp.int32, (document.shape[0], 8 * docs), 1)
    return jnp.concatenate(
        [
            dot((lane % (4 * docs) == document + q * docs).astype(bf16), folded)
            for q in range(4)
        ],
        axis=1,
    )


def normal_of(value):
    centred = value - jnp.mean(value, axis=-1, keepdims=True)
    inverse = lax.rsqrt(jnp.mean(centred * centred, axis=-1, keepdims=True) + norm_eps)
    return centred * inverse, inverse


def front_kernel(docs, document, both, far, weight, project, scale, shift, *outs):
    hidden, query, keys, values, stream = outs
    at = pl.program_id(0)
    rows = hidden.shape[0]
    embed = jnp.where(at % 2 == 0, both[0, :rows], far[0, :rows])
    value = dot(embed, weight[...])

    @pl.when(at % 2 == 0)
    def _():
        stream[...] = value

    normal, _ = normal_of(value)
    which = document[...]
    scaled = normal * (1.0 + row_mods(which, scale[...], docs)) + row_mods(which, shift[...], docs)
    low = scaled.astype(bf16)
    hidden[...] = low
    projected = dot(low, project[...]).astype(bf16)
    third = projected.shape[1] // 3
    query[...] = projected[:, :third] * jnp.asarray(1.0 / math.sqrt(HD), bf16)
    keys[...] = projected[:, third : 2 * third]
    values[...] = projected[:, 2 * third :]


def front(docs, document, both, far, weight, project, scale, shift):
    emb, width = weight.shape
    rows = document.shape[0]
    quarter = rows // 4
    third = project.shape[1] // 3
    message = both.shape[1]
    part = vmem((quarter, third), lambda i: (i, 0))
    return pl.pallas_call(
        functools.partial(front_kernel, docs),
        grid=(4,),
        in_specs=[
            vmem((quarter, 1), lambda i: (i, 0)),
            vmem((1, message, emb), lambda i: (i // 2, 0, 0)),
            vmem((1, message, emb), lambda i: (i // 2, 0, 0)),
            vmem(weight.shape),
            vmem(project.shape),
            vmem(scale.shape),
            vmem(shift.shape),
        ],
        out_specs=[
            vmem((quarter, width), lambda i: (i, 0)),
            part,
            part,
            part,
            vmem((quarter, width), lambda i: (i // 2, 0)),
        ],
        out_shape=[jax.ShapeDtypeStruct((rows, width), bf16)]
        + [jax.ShapeDtypeStruct((rows, third), bf16)] * 3
        + [jax.ShapeDtypeStruct((rows // 2, width), f32)],
        compiler_params=pltpu.CompilerParams(vmem_limit_bytes=48 << 20),
        cost_estimate=estimate(2 * rows * width * (emb + 3 * third), 8 * rows * width),
        name="front",
    )(document, both, far, weight, project, scale, shift)


def unpack_kernel(places, near, far, project, output, weight):
    group = near.shape[0] // 4
    emb = weight.shape[0] // 8
    depth = project.shape[0] // 8
    columns = project.shape[1]
    for k in range(8):
        source = near if k < 4 else far
        begin = k % 4 * group
        project[k * depth : (k + 1) * depth] = source[begin : begin + depth, :columns]
        for j in range(2):
            output[j * depth : (j + 1) * depth, k * depth : (k + 1) * depth] = source[
                begin : begin + depth, columns + j * depth : columns + (j + 1) * depth
            ]
        small = source[begin + depth : begin + group]
        half = small.shape[1] // 2
        first = pl.multiple_of(places[k] * emb, emb)
        weight[pl.ds(first, emb // 2)] = small[:, :half]
        weight[pl.ds(pl.multiple_of(first + emb // 2, emb // 2), emb // 2)] = small[:, half:]


def unpack(places, near, far, columns, emb):
    width = near.shape[1]
    return pl.pallas_call(
        unpack_kernel,
        in_specs=[pl.BlockSpec(memory_space=pltpu.SMEM)]
        + [pl.BlockSpec(memory_space=pltpu.VMEM)] * 2,
        out_specs=[pl.BlockSpec(memory_space=pltpu.VMEM)] * 3,
        out_shape=[
            jax.ShapeDtypeStruct((width, columns), bf16),
            jax.ShapeDtypeStruct((width - columns, width), bf16),
            jax.ShapeDtypeStruct((emb, width // 2), bf16),
        ],
        compiler_params=pltpu.CompilerParams(vmem_limit_bytes=32 << 20),
        name="unpack",
    )(jnp.stack([jnp.int32(p) for p in places]), near, far)


def second_norm_kernel(docs, document, stream_zero, mine, other, scale, shift, stream, hidden):
    value = stream_zero[...] + (mine[...].astype(f32) + other[...].astype(f32))
    stream[...] = value
    normal, _ = normal_of(value)
    which = document[...]
    hidden[...] = (
        normal * (1.0 + row_mods(which, scale[...], docs)) + row_mods(which, shift[...], docs)
    ).astype(bf16)


def second_norm(docs, at, document, stream_zero, mine, other, scale, shift):
    quarter, width = mine.shape
    whole = vmem((quarter, width))
    return pl.pallas_call(
        functools.partial(second_norm_kernel, docs),
        grid=(1,),
        in_specs=[
            vmem((quarter, 1), lambda i: (2 * at, 0)),
            vmem((quarter, width), lambda i: (at, 0)),
            whole,
            whole,
            vmem(scale.shape),
            vmem(shift.shape),
        ],
        out_specs=[whole, whole],
        out_shape=[
            jax.ShapeDtypeStruct((quarter, width), f32),
            jax.ShapeDtypeStruct((quarter, width), bf16),
        ],
        compiler_params=pltpu.CompilerParams(vmem_limit_bytes=32 << 20),
        cost_estimate=estimate(2 * quarter * width * 128, 12 * quarter * width),
        name="second_norm",
    )(document, stream_zero, mine, other, scale, shift)


def back_through_norm(docs, grad, value, which, scale):
    normal, inverse = normal_of(value)
    inner = grad * (1.0 + row_mods(which, scale, docs))
    back = inverse * (
        inner
        - jnp.mean(inner, axis=-1, keepdims=True)
        - normal * jnp.mean(inner * normal, axis=-1, keepdims=True)
    )
    lane = lax.broadcasted_iota(jnp.int32, (which.shape[0], 8), 1)
    member = (lane == which).astype(bf16)
    by_scale = dot(member, (grad * normal).astype(bf16), COLUMNS_OF_BOTH)
    by_shift = dot(member, grad.astype(bf16), COLUMNS_OF_BOTH)
    return back, by_scale, by_shift


def second_back_kernel(
    docs, document, stream, mine, other, scale, cotangent, stream_grad, low, by_scale, by_shift
):
    grad = mine[...].astype(f32) + other[...].astype(f32)
    back, by_scale[...], by_shift[...] = back_through_norm(
        docs, grad, stream[...], document[...], scale[...]
    )
    total = cotangent[...].astype(f32) + back
    stream_grad[...] = total
    low[...] = total.astype(bf16)


def second_back(docs, at, document, stream, mine, other, scale, cotangent):
    quarter, width = mine.shape
    whole = vmem((quarter, width))
    sums = vmem((8, width))
    return pl.pallas_call(
        functools.partial(second_back_kernel, docs),
        grid=(1,),
        in_specs=[
            vmem((quarter, 1), lambda i: (2 * at, 0)),
            whole,
            whole,
            whole,
            vmem(scale.shape),
            vmem((quarter, width), lambda i: (2 * at, 0)),
        ],
        out_specs=[whole, whole, sums, sums],
        out_shape=[
            jax.ShapeDtypeStruct((quarter, width), f32),
            jax.ShapeDtypeStruct((quarter, width), bf16),
            jax.ShapeDtypeStruct((8, width), f32),
            jax.ShapeDtypeStruct((8, width), f32),
        ],
        compiler_params=pltpu.CompilerParams(vmem_limit_bytes=32 << 20),
        cost_estimate=estimate(2 * quarter * width * 128, 16 * quarter * width),
        name="second_back",
    )(document, stream, mine, other, scale, cotangent)


def first_back_kernel(
    docs, document, stream, mine, other, scale, above, weight, embed, grad_embed, grad_weight,
    by_scale, by_shift,
):
    grad = mine[...].astype(f32) + other[...].astype(f32)
    back, by_scale[...], by_shift[...] = back_through_norm(
        docs, grad, stream[...], document[...], scale[...]
    )
    low = (back + above[...]).astype(bf16)
    grad_embed[...] = dot(low, weight[...], ROWS_OF_BOTH).astype(bf16)
    grad_weight[...] = dot(embed[0, : low.shape[0]], low, COLUMNS_OF_BOTH)


def first_back(docs, at, document, stream, mine, other, scale, above, weight, both):
    quarter, width = mine.shape
    emb = weight.shape[0]
    whole = vmem((quarter, width))
    sums = vmem((8, width))
    return pl.pallas_call(
        functools.partial(first_back_kernel, docs),
        grid=(1,),
        in_specs=[
            vmem((quarter, 1), lambda i: (2 * at, 0)),
            vmem((quarter, width), lambda i: (at, 0)),
            whole,
            whole,
            vmem(scale.shape),
            whole,
            vmem(weight.shape),
            vmem((1,) + both.shape[1:], lambda i: (at, 0, 0)),
        ],
        out_specs=[vmem((quarter, emb)), vmem((emb, width)), sums, sums],
        out_shape=[
            jax.ShapeDtypeStruct((quarter, emb), bf16),
            jax.ShapeDtypeStruct((emb, width), f32),
            jax.ShapeDtypeStruct((8, width), f32),
            jax.ShapeDtypeStruct((8, width), f32),
        ],
        compiler_params=pltpu.CompilerParams(vmem_limit_bytes=32 << 20),
        cost_estimate=estimate(4 * quarter * width * 256, 16 * quarter * width),
        name="first_back",
    )(document, stream, mine, other, scale, above, weight, both)


def scalars(values):
    return jnp.stack([jnp.int32(value) for value in values])


SMEM_SPEC = pl.BlockSpec(memory_space=pltpu.SMEM)
VMEM_SPEC = pl.BlockSpec(memory_space=pltpu.VMEM)


def local_sums_kernel(docs, spots, *refs):
    weights, mods, (own, other) = refs[:2], refs[2:10], refs[10:]
    emb = weights[0].shape[0]
    per = weights[0].shape[1] // 8
    for target, column in ((own, spots[8]), (other, spots[9])):
        for j in range(2):
            start = pl.multiple_of(spots[column * 2 + j] * per, per)
            lanes = slice(j * per, (j + 1) * per)
            block = weights[0][:, pl.ds(start, per)] + weights[1][:, pl.ds(start, per)]
            target[:emb, lanes] = block.astype(target.dtype)
        for q in range(4):
            halves = []
            for j in range(2):
                start = pl.multiple_of(spots[2 * q + j] * per, per)
                total = jnp.zeros((8, per), f32)
                for which in range(4):
                    both = (
                        mods[2 * which][:, pl.ds(start, per)]
                        + mods[2 * which + 1][:, pl.ds(start, per)]
                    )
                    total = jnp.where(column == which, both, total)
                halves.append(total)
            block = jnp.concatenate(halves, axis=1)
            target[emb + q * 8 : emb + (q + 1) * 8] = block.astype(target.dtype)


def local_sums(docs, spots, weights, mods):
    emb = weights[0].shape[0]
    return pl.pallas_call(
        functools.partial(local_sums_kernel, docs),
        in_specs=[SMEM_SPEC] + [VMEM_SPEC] * 10,
        out_specs=[VMEM_SPEC] * 2,
        out_shape=[
            jax.ShapeDtypeStruct((emb + 32, emb), f32),
            jax.ShapeDtypeStruct((emb + 32, emb), bf16),
        ],
        compiler_params=pltpu.CompilerParams(vmem_limit_bytes=32 << 20),
        name="local_sums",
    )(spots, *weights, *mods)


def outgoing_kernel(spots, own, other, first, second, *messages):
    emb = own.shape[1]
    total = own[...] + other[...].astype(f32)
    rows = jnp.where(spots[0] == 0, first[...], second[...])
    mods = total[emb:].astype(bf16)
    piece = emb // 8
    for k, message in enumerate(messages):
        message[: rows.shape[0]] = rows
        message[rows.shape[0] : rows.shape[0] + mods.shape[0]] = mods
    base = rows.shape[0] + mods.shape[0]
    for place in range(8):
        low = total[place * piece : (place + 1) * piece].astype(bf16)
        for k, message in enumerate(messages):
            for j in range(2):

                @pl.when(spots[1 + 2 * k + j] == place)
                def _(message=message, j=j, low=low):
                    message[base + j * piece : base + (j + 1) * piece] = low


def outgoing(spots, own, other, first, second):
    emb = own.shape[1]
    rows = first.shape[0] + own.shape[0] - emb + 2 * (emb // 8)
    return pl.pallas_call(
        outgoing_kernel,
        in_specs=[SMEM_SPEC] + [VMEM_SPEC] * 4,
        out_specs=[VMEM_SPEC] * 4,
        out_shape=[jax.ShapeDtypeStruct((rows, emb), bf16)] * 4,
        name="outgoing",
    )(spots, own, other, first, second)


def relay_kernel(share, piece, *refs):
    *arrived, message, keep = refs
    for k, ref in enumerate(arrived):
        message[k * share : (k + 1) * share] = ref[:share]
    for j, target in ((0, keep), (1, message)):
        begin = share + j * piece
        total = sum(ref[begin : begin + piece].astype(f32) for ref in arrived)
        if j:
            message[4 * share :] = total.astype(bf16)
        else:
            keep[...] = total


def relay(share, piece, arrived):
    emb = arrived[0].shape[1]
    return pl.pallas_call(
        functools.partial(relay_kernel, share, piece),
        in_specs=[VMEM_SPEC] * 4,
        out_specs=[VMEM_SPEC] * 2,
        out_shape=[
            jax.ShapeDtypeStruct((4 * share + piece, emb), bf16),
            jax.ShapeDtypeStruct((piece, emb), f32),
        ],
        name="relay",
    )(*arrived)


def landed_kernel(docs, share, rows, features, near, far, keep, tokens, small):
    width = small.shape[1] - keep.shape[1]
    emb = keep.shape[1]
    total = jnp.zeros((features.shape[1], width), f32)
    for k in range(8):
        source, begin = (near, far)[k // 4], k % 4 * share
        tokens[k * rows : (k + 1) * rows] = source[begin : begin + rows]
        mods = jnp.concatenate(
            [source[begin + rows + q * 8 : begin + rows + q * 8 + 8] for q in range(4)], axis=1
        )
        total += dot(features[k * 8 : (k + 1) * 8], mods, COLUMNS_OF_BOTH)
    small[:, :width] = total
    small[:, width:] = keep[...] + far[4 * share :].astype(f32)


def landed(docs, share, rows, width, features, near, far, keep):
    emb = keep.shape[1]
    return pl.pallas_call(
        functools.partial(landed_kernel, docs, share, rows),
        in_specs=[VMEM_SPEC] * 4,
        out_specs=[VMEM_SPEC] * 2,
        out_shape=[
            jax.ShapeDtypeStruct((8 * rows, emb), bf16),
            jax.ShapeDtypeStruct((features.shape[1], width + emb), f32),
        ],
        name="landed",
    )(features, near, far, keep)


def per_device(
    token_ids,
    lengths,
    time_steps,
    embed_table,
    input_weight,
    time_weight,
    project_weight,
    output_weight,
    up_weight,
    down_weight,
    cotangent,
):
    rows = token_ids.shape[0]
    half, quarter = rows // 2, rows // 4
    count = lax.axis_size("dp")
    groups = lax.axis_size("tensor")
    me = lax.axis_index("dp")
    place = lax.axis_index("tensor")
    x, c = place // 2, place % 2
    width = cotangent.shape[1]
    docs = lengths.shape[0]
    shard = embed_table.shape[0]
    emb_rows = input_weight.shape[0]
    head_width = project_weight.shape[1]
    heads = head_width // (3 * HD)
    third = heads * HD
    per = width // count
    columns = width // groups
    direct = count == len(ORDER) and per == 128 and 2 * per == third
    dp = Direct(count) if direct else Plain(count)
    order, back_order = (dp.places, dp.inverse) if direct else ([0], [0])

    my_ids = lax.dynamic_slice_in_dim(token_ids, (c * 2 + x) * quarter, quarter)
    heard = dp.spread_small(jnp.concatenate([my_ids, time_steps]))

    table = embed_table.astype(f32)
    rscale = lax.rsqrt(jnp.mean(table * table, axis=1, keepdims=True) + table_eps)
    normed = (table * rscale).astype(bf16)
    pair = jnp.concatenate([normed, swap_x(normed)], axis=0)
    shards = jnp.concatenate([pair, swap_core(pair)], axis=0)
    entry = jnp.arange(4 * shard, dtype=jnp.int32)
    which = entry // shard
    owner = (x ^ (which & 1)) * 2 + (c ^ (which >> 1))
    vocab = (me * groups + owner) * shard + entry % shard

    feature = me * emb_rows + jnp.arange(emb_rows, dtype=jnp.int32)
    part = EMB // 2
    frequency = jnp.exp(-math.log(10000.0) * (feature % part).astype(f32) / part)
    angles = heard[:, quarter:].astype(f32)[:, :, None] * frequency[None, None, :]
    features = jnp.where(feature[None, None, :] < part, jnp.sin(angles), jnp.cos(angles))
    features = features.astype(bf16)

    ordered = project_weight.reshape(per, heads, 3, HD).transpose(0, 2, 1, 3)
    ordered = ordered.reshape(per, head_width)
    input_half = lax.dynamic_slice_in_dim(input_weight, c * (width // 2), width // 2, 1)
    if direct:
        packed = jnp.concatenate(
            [
                jnp.concatenate([ordered, unfold(output_weight, 2)], axis=1),
                unfold(input_half, 2),
            ],
            axis=0,
        )
        packed = jnp.concatenate([packed, dp.swap(packed, 4)], axis=0)
        packed = jnp.concatenate([packed, dp.swap(packed, 2)], axis=0)

    time_part = lax.dynamic_slice_in_dim(time_weight, place * width, width, 1)

    found_mods = dot(features.reshape(count * docs, emb_rows), time_part)
    found_mods = found_mods.reshape(count, docs, 4, EMB).transpose(0, 2, 1, 3)
    found_mods = jnp.concatenate(split_two(found_mods.reshape(count, 4 * docs, EMB)), axis=1)

    def look_up(begin, end):
        names = heard[begin:end, :quarter].reshape(-1)
        onehot = (names[:, None] == vocab[None, :]).astype(bf16)
        found = dot(onehot, shards).astype(bf16).reshape(end - begin, quarter, EMB)
        return jnp.concatenate([found, found_mods[begin:end]], axis=1)

    if direct:
        crossed = dp.swap(look_up(4, 8), 1)
        near = look_up(0, 4).astype(f32) + crossed.astype(f32)
        mods = near[:, quarter : quarter + 4 * docs] + near[:, quarter + 4 * docs :]
        near = jnp.concatenate([near[:, :quarter].astype(bf16), *split_two(mods)], axis=1)
        up_near = after(up_weight, packed)
        up_z2 = dp.swap(up_near, 4)
        packed_far = dp.swap(after(packed, crossed), 1)
        arrived = [near[0]] + [dp.swap(near[k], ORDER[k]) for k in (1, 2, 3)]
    else:
        messages = look_up(0, count).astype(f32)
        total = lax.psum_scatter(messages, "dp", scatter_dimension=0, tiled=False)
        mods = total[quarter : quarter + 4 * docs] + total[quarter + 4 * docs :]
        arrived = [jnp.concatenate([total[:quarter].astype(bf16), *split_two(mods)], axis=0)]
    mine = finish(direct, docs, dp.places[:8], arrived)
    other = swap_x(mine)
    both = jnp.stack([jnp.where(x == 0, mine, other), jnp.where(x == 0, other, mine)])
    far = swap_core(both)
    own_mods, far_mods = both[:, quarter:], far[:, quarter:]
    scale_one, scale_two = jnp.where(c == 0, own_mods, far_mods)
    shift_one, shift_two = jnp.where(c == 0, far_mods, own_mods)

    if direct:
        project, output, input_half = unpack(dp.places, packed, packed_far, head_width, EMB)
        input_other = swap_core(input_half)
        input_full = jnp.concatenate(
            [
                jnp.where(c == 0, input_half, input_other),
                jnp.where(c == 0, input_other, input_half),
            ],
            axis=1,
        )
        input_full = permute(input_full, [0], order)
        up_near = jnp.concatenate([up_near, after(up_z2, mine)], axis=0)
        up_z1 = dp.swap(up_near, 2)
        down_near = after(down_weight, mine)
        down_z2 = dp.swap(down_near, 4)
    else:
        project = lax.all_gather(ordered, "dp", axis=0, tiled=True)
        output = lax.all_gather(output_weight, "dp", axis=1, tiled=True)
        input_full = lax.all_gather(input_weight, "dp", axis=0, tiled=True)
        up = lax.all_gather(up_weight, "dp", axis=0, tiled=True)
        down = lax.all_gather(down_weight, "dp", axis=1, tiled=True)

    position = jnp.concatenate(
        [
            start + jnp.arange(quarter, dtype=jnp.int32)
            for start in (c * half, (1 - c) * half, c * half + quarter, (1 - c) * half + quarter)
        ]
    )
    ends = jnp.cumsum(lengths)
    document = jnp.sum((position[:, None] >= ends[None, :]).astype(jnp.int32), axis=1)
    row_places = [2 * c, 2 * (1 - c), 2 * c + 1, 2 * (1 - c) + 1]
    cot = permute(after(cotangent, heard), row_places, order)

    hidden_one, query, keys, values, stream_zero = front(
        docs, document[:, None], both, far, input_full, project, scale_one, shift_one
    )
    if direct:
        up_near = jnp.concatenate([up_near, after(up_z1, query)], axis=0)
        up_far = dp.swap(up_near, 1)
        down_near = jnp.concatenate([down_near, after(down_z2, query)], axis=1)
        down_y = dp.swap(down_near, 1)
    attended, logsum = attention(document, query, keys, values)

    def reduce_core(partial):
        other = swap_core(partial[quarter:].astype(bf16))
        return (partial[:quarter] + other.astype(f32)).astype(bf16)

    stream_one, hidden_two = [], []
    sums = [reduce_core(dot(attended[at * half : (at + 1) * half], output)) for at in range(2)]
    crossed = [swap_x(part) for part in sums]
    for at in range(2):
        stream, hidden = second_norm(
            docs, at, document[:, None], stream_zero, sums[at], crossed[at], scale_two, shift_two
        )
        hidden_two.append(jnp.concatenate([hidden, swap_core(hidden)], axis=0))
        stream_one.append(stream)
    if direct:
        down_near = jnp.concatenate([down_near, after(down_y, crossed[0])], axis=1)
        down_z = dp.swap(down_near, 2)
        up = jnp.concatenate([up_near, after(up_far, crossed[0])], axis=0)
        down = jnp.concatenate(
            [
                down_near[:, : 2 * per],
                down_z[:, : 2 * per],
                down_near[:, 2 * per :],
                down_z[:, 2 * per :],
            ],
            axis=1,
        )
    uppers = [dot(hidden_two[at], up) for at in range(2)]
    activated, grad_upward, grad_two = [], [], []
    for at in range(2):
        upward = uppers[at]
        phi = 0.5 * (1.0 + lax.erf(upward * math.sqrt(0.5)))
        active = (upward * phi).astype(bf16)
        slope = phi + upward * (math.sqrt(0.5 / math.pi) * jnp.exp(-0.5 * upward * upward))
        grad_active = dot(cot[at * half : (at + 1) * half], down, ROWS_OF_BOTH)
        grad_up_rows = (grad_active * slope).astype(bf16)
        activated.append(active)
        grad_upward.append(grad_up_rows)
        grad_two.append(reduce_core(dot(grad_up_rows, up, ROWS_OF_BOTH)))
    crossed = [swap_x(part) for part in grad_two]
    activated = jnp.concatenate(activated, axis=0)
    grad_upward = jnp.concatenate(grad_upward, axis=0)
    hidden_two = jnp.concatenate(hidden_two, axis=0)
    grad_down = dot(activated, after(cot, *grad_two), COLUMNS_OF_BOTH)
    if direct:
        down_keep = picked(grad_down, (0, 1, 4, 5), 1)
        down_first = dp.swap(picked(grad_down, (2, 3, 6, 7), 1).astype(bf16), 2)
    grad_up = dot(hidden_two, after(grad_upward, *grad_two), COLUMNS_OF_BOTH)
    if direct:
        up_first = dp.swap(grad_up[width // 2 :].astype(bf16), 1)
    branch = dot(after(activated, *grad_two), down)

    grad_one, grad_attn, by_two = [], [], []
    for at in range(2):
        stream, low, *by = second_back(
            docs, at, document[:, None], stream_one[at], grad_two[at], crossed[at], scale_two, cot
        )
        grad_attn += [low, swap_core(low)]
        grad_one.append(stream)
        by_two.append(by)
    grad_attn = jnp.concatenate(grad_attn, axis=0)
    grad_attended = dot(grad_attn, output, ROWS_OF_BOTH).astype(bf16)
    branch_low = after(branch, grad_attended)
    branch_sums = jnp.concatenate(
        [reduce_core(branch_low[at * half : (at + 1) * half]) for at in range(2)], axis=0
    )
    branch_crossed = swap_x(branch_sums)
    if direct:
        down_first = after(down_first, grad_attended)
        down_sum = down_keep + down_first.astype(f32)
        down_second = dp.swap(down_sum[:, 2 * per :].astype(bf16), 1)
        up_first = after(up_first, grad_attended)
        up_sum = grad_up[: width // 2] + up_first.astype(f32)
        up_second = dp.swap(up_sum[2 * per :].astype(bf16), 2)
    grad_projected = attention_back(
        document, query, keys, values, grad_attended, attended, logsum
    )
    sums = [
        reduce_core(dot(grad_projected[at * half : (at + 1) * half], project, ROWS_OF_BOTH))
        for at in range(2)
    ]
    crossed = [swap_x(part) for part in sums]
    if direct:
        down_second = after(down_second, grad_projected)
        down_sum = down_sum[:, : 2 * per] + down_second.astype(f32)
        down_third = dp.swap(down_sum[:, per:].astype(bf16), 4)
        up_second = after(up_second, grad_projected)
        up_sum = up_sum[: 2 * per] + up_second.astype(f32)
        up_third = dp.swap(up_sum[per:].astype(bf16), 4)
    grad_project = dot(hidden_one, after(grad_projected, *sums), COLUMNS_OF_BOTH)
    grad_output = dot(attended, after(grad_attn, *sums), COLUMNS_OF_BOTH)
    if direct:
        grad_output = jnp.concatenate(
            [unfold(grad_output[:, k * per : (k + 1) * per], 2) for k in range(count)], axis=0
        )
        grad_packed = jnp.concatenate([grad_project, grad_output], axis=1)
        packed_first = dp.swap(grad_packed[width // 2 :].astype(bf16), 1)

    grad_embed, grad_input, by_one = [], [], []
    for at in range(2):
        rows_grad, weight_grad, *by = first_back(
            docs,
            at,
            document[:, None],
            stream_zero,
            sums[at],
            crossed[at],
            scale_one,
            grad_one[at],
            input_full,
            both,
        )
        grad_embed.append(rows_grad)
        grad_input.append(weight_grad)
        by_one.append(by)
    share = quarter + 32
    spots = scalars((list(dp.inverse) if direct else [0] * 8) + [place, x * 2 + 1 - c])
    if direct:
        mods = [by[at][which] for by in (by_one, by_two) for which in range(2) for at in range(2)]
        own_sums, other_sums = local_sums(docs, spots, grad_input, mods)
        received = swap_core(other_sums)
        spots = scalars([x] + [me ^ v ^ j for v in ORDER[:4] for j in range(2)])
        messages = outgoing(spots, own_sums, received, *grad_embed)
        arrived = [messages[0]] + [dp.swap(messages[k], ORDER[k]) for k in (1, 2, 3)]
        near, keep = relay(share, emb_rows, arrived)
        far = dp.swap(near, 1)
        features = jnp.pad(features, ((0, 0), (0, 8 - docs), (0, 0)))
        features = features.reshape(8 * count, emb_rows)
        grad_tokens, small = landed(docs, share, quarter, width, features, near, far, keep)

        packed_first = after(packed_first, near)
        packed_sum = grad_packed[: width // 2] + packed_first.astype(f32)
        packed_second = dp.swap(packed_sum[2 * per :].astype(bf16), 2)
        packed_second = after(packed_second, grad_tokens)
        packed_sum = packed_sum[: 2 * per] + packed_second.astype(f32)
        packed_third = dp.swap(packed_sum[per:].astype(bf16), 4)
    else:
        grad_embed = jnp.where(x == 0, grad_embed[0], grad_embed[1])
        mods = jnp.concatenate(
            [
                (by[0][which] + by[1][which])[:docs]
                for by in (by_one, by_two)
                for which in range(2)
            ],
            axis=0,
        )
        mods = mods + swap_core(mods)
        mods = lax.dynamic_slice_in_dim(mods, place * docs, docs, 0).astype(bf16)
        grad_input = grad_input[0] + grad_input[1]
        mine = lax.dynamic_slice_in_dim(grad_input, place * columns, columns, 1)
        partner = lax.dynamic_slice_in_dim(grad_input, (x * 2 + 1 - c) * columns, columns, 1)
        mine = mine + swap_core(partner.astype(bf16)).astype(f32)
        grad_tokens = lax.all_gather(grad_embed, "dp", axis=0, tiled=True)
        all_mods = lax.all_gather(mods, "dp", axis=0, tiled=True)
        input_part = lax.psum_scatter(mine, "dp", scatter_dimension=0, tiled=True)
        time_grad = dot(features.reshape(-1, emb_rows), all_mods, COLUMNS_OF_BOTH)
        small = jnp.concatenate([time_grad, input_part], axis=1)
    all_ids = heard[:, :quarter].reshape(-1)

    def table_part(first, last):
        onehot = (vocab[first * shard : last * shard, None] == all_ids[None, :]).astype(bf16)
        return dot(onehot, grad_tokens)

    far = swap_core(table_part(2, 4).astype(bf16))
    sent = swap_x((table_part(1, 2) + far[shard:].astype(f32)).astype(bf16))
    kept = table_part(0, 1) + far[:shard].astype(f32)
    grad_normed = kept + sent.astype(f32)
    grad_table = rscale * grad_normed - table * (
        rscale * rscale * rscale * jnp.mean(grad_normed * table, axis=1, keepdims=True)
    )

    other = swap_x(small)
    both = jnp.stack([jnp.where(x == 0, small, other), jnp.where(x == 0, other, small)])
    far = swap_core(both)
    pieces = []
    for at in range(2):
        pieces += [jnp.where(c == 0, both[at], far[at]), jnp.where(c == 0, far[at], both[at])]
    summed_time = jnp.concatenate([piece[:, :width] for piece in pieces], axis=1)
    summed_input = jnp.concatenate([piece[:, width:] for piece in pieces], axis=1)

    out_blocks = []
    for at in range(2):
        here = slice(at * quarter, (at + 1) * quarter)
        block = branch_sums[here].astype(f32) + branch_crossed[here].astype(f32)
        block = (stream_one[at] + block).astype(bf16)
        out_blocks += [block, swap_core(block)]
    back_places = [c, 2 + c, 1 - c, 3 - c]
    block_out = permute(jnp.concatenate(out_blocks, axis=0), back_places, back_order)

    if direct:
        summed_down = down_sum[:, :per] + after(down_third, grad_tokens).astype(f32)
        summed_up = up_sum[:per] + after(up_third, grad_tokens).astype(f32)
        summed_packed = packed_sum[:per] + after(packed_third, kept).astype(f32)
        summed_project = summed_packed[:, :head_width]
        summed_output = fold(summed_packed[:, head_width:], per)
    else:
        summed_down, summed_up, summed_project, summed_output = (
            lax.psum_scatter(grad, "dp", scatter_dimension=axis, tiled=True)
            for grad, axis in ((grad_down, 1), (grad_up, 0), (grad_project, 0), (grad_output, 1))
        )
    summed_project = (
        summed_project.reshape(per, 3, heads, HD).transpose(0, 2, 1, 3).reshape(per, head_width)
    )
    return (
        block_out,
        grad_table,
        summed_input,
        summed_time,
        summed_project,
        summed_output,
        summed_up,
        summed_down,
    )


def solution(mesh):
    return jax.shard_map(
        per_device,
        mesh=mesh,
        in_specs=(
            P("dp"),
            P("dp"),
            P("dp"),
            P(("dp", "tensor"), None),
            P("dp", None),
            P("dp", None),
            P("dp", "tensor"),
            P("tensor", "dp"),
            P("dp", "tensor"),
            P("tensor", "dp"),
            P("dp", None),
        ),
        out_specs=(
            P("dp", None),
            P(("dp", "tensor"), None),
            P("dp", None),
            P("dp", None),
            P("dp", "tensor"),
            P("tensor", "dp"),
            P("dp", "tensor"),
            P("tensor", "dp"),
        ),
        check_vma=False,
    )
```

```python
import functools
import math

import jax
import jax.numpy as jnp
from jax import lax
from jax.experimental import pallas as pl
from jax.experimental.pallas import tpu as pltpu
from jax.sharding import PartitionSpec as P

HD = 64
EMB = 256

table_eps = 1e-06
norm_eps = 1e-05
masked_score = -1e30
highest = lax.Precision.HIGHEST
bf16 = jnp.bfloat16
f32 = jnp.float32


def dot(left, right, dims=((1,), (0,))):
    return lax.dot_general(left, right, (dims, ((), ())), preferred_element_type=f32)


def join(*values):
    return lax.optimization_barrier(values)


def after(value, *others):
    return lax.optimization_barrier((value,) + others)[0]


SWAP_CORE = [(0, 1), (1, 0), (2, 3), (3, 2)]
SWAP_X = [(0, 2), (2, 0), (1, 3), (3, 1)]


def swap_core(value):
    return lax.ppermute(value, "tensor", SWAP_CORE)


def swap_x(value):
    return lax.ppermute(value, "tensor", SWAP_X)


ROWS_OF_BOTH = ((1,), (1,))
COLUMNS_OF_BOTH = ((0,), (0,))
ORDER = (0, 4, 2, 6, 1, 5, 3, 7)


class Direct:
    def __init__(self, count):
        self.count = count
        self.me = lax.axis_index("dp")
        self.places = [self.me ^ v for v in ORDER]
        self.inverse = [
            sum(jnp.where(self.places[k] == a, k, 0) for k in range(count)) for a in range(count)
        ]

    def swap(self, value, v):
        return lax.ppermute(value, "dp", [(i, i ^ v) for i in range(self.count)])

    def spread_small(self, value):
        value = value[None]
        for v in (4, 2, 1):
            value = jnp.concatenate([value, self.swap(value, v)], axis=0)
        return value


def picked(value, places, axis):
    size = value.shape[axis] // len(ORDER)
    return jnp.concatenate(
        [lax.slice_in_dim(value, p * size, (p + 1) * size, axis=axis) for p in places], axis=axis
    )


def split_two(value):
    high = value.astype(bf16)
    return high, (value - high.astype(f32)).astype(bf16)


def fold(value, width):
    return jnp.concatenate(jnp.split(value, value.shape[1] // width, axis=1), axis=0)


def unfold(value, count):
    return jnp.concatenate(jnp.split(value, count, axis=0), axis=1)


def permute_kernel(row_places, column_places, source, target):
    rows = source.shape[0] // row_places.shape[0]
    columns = source.shape[1] // column_places.shape[0]
    for i in range(row_places.shape[0]):
        for j in range(column_places.shape[0]):
            first = pl.multiple_of(row_places[i] * rows, rows)
            second = pl.multiple_of(column_places[j] * columns, columns)
            target[i * rows : (i + 1) * rows, j * columns : (j + 1) * columns] = source[
                pl.ds(first, rows), pl.ds(second, columns)
            ]


def permute(value, row_places, column_places):
    lists = [jnp.stack([jnp.int32(p) for p in places]) for places in (row_places, column_places)]
    return pl.pallas_call(
        permute_kernel,
        out_shape=jax.ShapeDtypeStruct(value.shape, value.dtype),
        in_specs=[pl.BlockSpec(memory_space=pltpu.SMEM)] * 2
        + [pl.BlockSpec(memory_space=pltpu.VMEM)],
        out_specs=pl.BlockSpec(memory_space=pltpu.VMEM),
        compiler_params=pltpu.CompilerParams(vmem_limit_bytes=32 << 20),
        cost_estimate=estimate(0, 0),
        name="permute",
    )(*lists, value)


def attention_kernel(heads, same_row, same_column, query, keys, values, attended, logsum):
    same = same_row[...] == same_column[...]
    q, k, v = query[...], keys[...], values[...]
    head = lax.broadcasted_iota(jnp.int32, q.shape, 1) // HD
    total_out = jnp.zeros(q.shape, f32)
    for h in range(heads):
        scores = dot(jnp.where(head == h, q, jnp.zeros_like(q)), k, ROWS_OF_BOTH)
        scores = jnp.where(same, scores, -1e30)
        peak = jnp.max(scores, axis=1, keepdims=True)
        expo = jnp.exp(scores - peak)
        total = jnp.sum(expo, axis=1, keepdims=True)
        total_out = jnp.where(head == h, dot(expo.astype(bf16), v) / total, total_out)
        logsum[:, h : h + 1] = peak + jnp.log(total)
    attended[...] = total_out.astype(bf16)


def attention(document, query, keys, values):
    rows, width = query.shape
    heads = width // HD
    block = rows // 2
    part = pl.BlockSpec((block, width), lambda i: (i, 0))
    whole = pl.BlockSpec((rows, width), lambda i: (0, 0))
    return pl.pallas_call(
        functools.partial(attention_kernel, heads),
        grid=(2,),
        in_specs=[
            pl.BlockSpec((block, 1), lambda i: (i, 0)),
            pl.BlockSpec((1, rows), lambda i: (0, 0)),
            part,
            whole,
            whole,
        ],
        out_specs=[part, pl.BlockSpec((block, heads), lambda i: (i, 0))],
        out_shape=[
            jax.ShapeDtypeStruct((rows, width), bf16),
            jax.ShapeDtypeStruct((rows, heads), f32),
        ],
        compiler_params=pltpu.CompilerParams(vmem_limit_bytes=32 << 20),
        cost_estimate=pl.CostEstimate(
            flops=4 * rows * rows * width * 4, bytes_accessed=8 * rows * width, transcendentals=0
        ),
        name="attention",
    )(document[:, None], document[None, :], query, keys, values)


def attention_back_kernel(
    count,
    same_row,
    same_column,
    query,
    keys,
    values,
    grad_attended,
    attended,
    logsum,
    grad_projected,
    sum_keys,
    sum_values,
):
    pair, at = pl.program_id(0), pl.program_id(1)
    same = same_row[...] == same_column[...]
    q, k, v, g = query[...], keys[...], values[...], grad_attended[...]
    rows, lanes = q.shape
    head = lax.broadcasted_iota(jnp.int32, q.shape, 1) // HD
    product = g.astype(f32) * attended[...].astype(f32)
    logs = logsum[...]
    lane = lax.broadcasted_iota(jnp.int32, logs.shape, 1)

    @pl.when(at == 0)
    def _():
        sum_keys[...] = jnp.zeros_like(sum_keys)
        sum_values[...] = jnp.zeros_like(sum_values)

    out = jnp.zeros(q.shape, f32)
    for h in range(lanes // HD):
        here = head == h
        q_head = jnp.where(here, q, jnp.zeros_like(q))
        g_head = jnp.where(here, g, jnp.zeros_like(g))
        log = jnp.sum(jnp.where(lane == pair * (lanes // HD) + h, logs, 0.0), 1, keepdims=True)
        scores = jnp.where(same, dot(q_head, k, ROWS_OF_BOTH), -1e30)
        probs = jnp.exp(scores - log)
        inner = jnp.sum(jnp.where(here, product, 0.0), axis=1, keepdims=True)
        grad_scores = probs * (dot(g_head, v, ROWS_OF_BOTH) - inner)
        grad_scores = grad_scores.astype(bf16)
        out = jnp.where(here, dot(grad_scores, k), out)
        sum_keys[...] += dot(grad_scores, q_head, COLUMNS_OF_BOTH)
        sum_values[...] += dot(probs.astype(bf16), g_head, COLUMNS_OF_BOTH)
    third = grad_projected.shape[1] // 3
    first = pl.multiple_of(at * rows, rows)
    grad_projected[pl.ds(first, rows), pl.ds(pl.multiple_of(pair * lanes, lanes), lanes)] = (
        out * (1.0 / math.sqrt(HD))
    ).astype(bf16)

    @pl.when(at == count - 1)
    def _():
        for which, total in ((1, sum_keys), (2, sum_values)):
            start = pl.multiple_of(which * third + pair * lanes, lanes)
            grad_projected[:, pl.ds(start, lanes)] = total[...].astype(bf16)


def attention_back(document, query, keys, values, grad_attended, attended, logsum):
    rows, width = query.shape
    heads = width // HD
    block, lanes = min(512, rows), 2 * HD
    part = pl.BlockSpec((block, lanes), lambda p, i: (i, p))
    whole = pl.BlockSpec((rows, lanes), lambda p, i: (0, p))
    return pl.pallas_call(
        functools.partial(attention_back_kernel, rows // block),
        grid=(width // lanes, rows // block),
        in_specs=[
            pl.BlockSpec((block, 1), lambda p, i: (i, 0)),
            pl.BlockSpec((1, rows), lambda p, i: (0, 0)),
            part,
            whole,
            whole,
            part,
            part,
            pl.BlockSpec((block, heads), lambda p, i: (i, 0)),
        ],
        out_specs=pl.BlockSpec((rows, 3 * width), lambda p, i: (0, 0)),
        out_shape=jax.ShapeDtypeStruct((rows, 3 * width), bf16),
        scratch_shapes=[pltpu.VMEM((rows, lanes), f32)] * 2,
        compiler_params=pltpu.CompilerParams(vmem_limit_bytes=32 << 20),
        cost_estimate=pl.CostEstimate(
            flops=10 * rows * rows * width * 4, bytes_accessed=16 * rows * width, transcendentals=0
        ),
        name="attention_back",
    )(document[:, None], document[None, :], query, keys, values, grad_attended, attended, logsum)


SMEM_SPEC = pl.BlockSpec(memory_space=pltpu.SMEM)
VMEM_SPEC = pl.BlockSpec(memory_space=pltpu.VMEM)


def scalars(values):
    return jnp.stack([jnp.int32(value) for value in values])


def vmem(shape, index=None):
    if index is None:
        return pl.BlockSpec(shape, lambda *_: (0,) * len(shape))
    return pl.BlockSpec(shape, index)


def estimate(flops, moved):
    return pl.CostEstimate(flops=flops, bytes_accessed=moved, transcendentals=0)


def finish_kernel(direct, docs, places, *refs):
    *arrived, target = refs
    rows = arrived[0].shape[0] - 8 * docs
    total = arrived[0][:rows].astype(f32)
    high = arrived[0][rows : rows + 4 * docs].astype(f32)
    low = arrived[0][rows + 4 * docs :].astype(f32)
    for ref in arrived[1:]:
        total += ref[:rows].astype(f32)
        high += ref[rows : rows + 4 * docs].astype(f32)
        low += ref[rows + 4 * docs :].astype(f32)
    target[:rows] = total.astype(bf16)
    mods = high + low
    if direct:
        lanes = mods.shape[1] // 2
        blocks = [
            mods[(a // 2) * docs : (a // 2 + 1) * docs, (a % 2) * lanes : (a % 2 + 1) * lanes]
            for a in range(8)
        ]
        ordered = []
        for p in range(8):
            block = jnp.zeros_like(blocks[0])
            for a in range(8):
                block = jnp.where(places[p] == a, blocks[a], block)
            ordered.append(block)
        mods = jnp.concatenate(
            [jnp.concatenate(ordered[2 * q : 2 * q + 2], axis=1) for q in range(4)], axis=0
        )
    first = mods.astype(bf16)
    target[rows:] = jnp.concatenate(
        [first, (mods - first.astype(f32)).astype(bf16)], axis=0
    )


def finish(direct, docs, places, arrived):
    return pl.pallas_call(
        functools.partial(finish_kernel, direct, docs),
        in_specs=[pl.BlockSpec(memory_space=pltpu.SMEM)]
        + [pl.BlockSpec(memory_space=pltpu.VMEM)] * len(arrived),
        out_specs=pl.BlockSpec(memory_space=pltpu.VMEM),
        out_shape=jax.ShapeDtypeStruct(arrived[0].shape, bf16),
        cost_estimate=estimate(0, 0),
        name="finish",
    )(jnp.stack([jnp.int32(p) for p in places]), *arrived)


def row_mods(document, folded, docs):
    lane = lax.broadcasted_iota(jnp.int32, (document.shape[0], 8 * docs), 1)
    return jnp.concatenate(
        [
            dot((lane % (4 * docs) == document + q * docs).astype(bf16), folded)
            for q in range(4)
        ],
        axis=1,
    )


def normal_of(value):
    centred = value - jnp.mean(value, axis=-1, keepdims=True)
    inverse = lax.rsqrt(jnp.mean(centred * centred, axis=-1, keepdims=True) + norm_eps)
    return centred * inverse, inverse


def front_kernel(docs, document, both, far, weight, project, scale, shift, *outs):
    hidden, query, keys, values, stream = outs
    at = pl.program_id(0)
    rows = hidden.shape[0]
    embed = jnp.where(at < 2, both[0, :rows], far[0, :rows])
    value = dot(embed, weight[...])

    @pl.when(at < 2)
    def _():
        stream[...] = value

    normal, _ = normal_of(value)
    which = document[...]
    scaled = normal * (1.0 + row_mods(which, scale[...], docs)) + row_mods(which, shift[...], docs)
    low = scaled.astype(bf16)
    hidden[...] = low
    projected = dot(low, project[...]).astype(bf16)
    third = projected.shape[1] // 3
    query[...] = projected[:, :third] * jnp.asarray(1.0 / math.sqrt(HD), bf16)
    keys[...] = projected[:, third : 2 * third]
    values[...] = projected[:, 2 * third :]


def front(docs, document, both, far, weight, project, scale, shift):
    emb, width = weight.shape
    rows = document.shape[0]
    quarter = rows // 4
    third = project.shape[1] // 3
    message = both.shape[1]
    part = vmem((quarter, third), lambda i: (i, 0))
    return pl.pallas_call(
        functools.partial(front_kernel, docs),
        grid=(4,),
        in_specs=[
            vmem((quarter, 1), lambda i: (i, 0)),
            vmem((1, message, emb), lambda i: (jnp.minimum(i, 1), 0, 0)),
            vmem((1, message, emb), lambda i: (jnp.maximum(i - 2, 0), 0, 0)),
            vmem(weight.shape),
            vmem(project.shape),
            vmem(scale.shape),
            vmem(shift.shape),
        ],
        out_specs=[
            vmem((quarter, width), lambda i: (i, 0)),
            part,
            part,
            part,
            vmem((quarter, width), lambda i: (jnp.minimum(i, 1), 0)),
        ],
        out_shape=[jax.ShapeDtypeStruct((rows, width), bf16)]
        + [jax.ShapeDtypeStruct((rows, third), bf16)] * 3
        + [jax.ShapeDtypeStruct((rows // 2, width), f32)],
        compiler_params=pltpu.CompilerParams(vmem_limit_bytes=32 << 20),
        cost_estimate=estimate(2 * rows * width * (emb + 3 * third), 8 * rows * width),
        name="front",
    )(document, both, far, weight, project, scale, shift)


def pack_first_kernel(spots, project, weight, output, target, small):
    depth, columns = project.shape
    third = columns // 3
    for head in range(third // HD):
        for which in range(3):
            target[:, which * third + head * HD : which * third + (head + 1) * HD] = project[
                :, (3 * head + which) * HD : (3 * head + which + 1) * HD
            ]
    emb = weight.shape[0]
    for q in range(depth // emb):
        start = spots[0] * (weight.shape[1] // 2) + q * depth
        small[q * emb : (q + 1) * emb, :depth] = weight[
            :, pl.ds(pl.multiple_of(start, depth), depth)
        ]
    for j in range(2):
        small[:, (1 + j) * depth : (2 + j) * depth] = output[j * depth : (j + 1) * depth]


def pack_first(spots, project, weight, output):
    depth, columns = project.shape
    return pl.pallas_call(
        pack_first_kernel,
        in_specs=[SMEM_SPEC] + [VMEM_SPEC] * 3,
        out_specs=[VMEM_SPEC] * 2,
        out_shape=[
            jax.ShapeDtypeStruct((depth, columns), bf16),
            jax.ShapeDtypeStruct((depth, 3 * depth), bf16),
        ],
        name="pack_first",
    )(spots, project, weight, output)


def pack_second_kernel(up, down, target):
    per = up.shape[0]
    target[:per] = up[...]
    for j in range(down.shape[0] // per):
        target[per:, j * per : (j + 1) * per] = down[j * per : (j + 1) * per]


def pack_second(up, down):
    per, units = up.shape
    return pl.pallas_call(
        pack_second_kernel,
        in_specs=[VMEM_SPEC] * 2,
        out_specs=VMEM_SPEC,
        out_shape=jax.ShapeDtypeStruct((2 * per, units), bf16),
        name="pack_second",
    )(up, down)


def unpack_kernel(places, gathered, near, far, project, output, weight):
    depth = project.shape[0] // 8
    emb = weight.shape[0] // 8
    for p in range(8):
        rows = slice(p * depth, (p + 1) * depth)
        project[rows] = gathered[places[p]]
        source, begin = (near, far)[p // 4], p % 4 * depth
        for j in range(2):
            output[j * depth : (j + 1) * depth, rows] = source[
                begin : begin + depth, (1 + j) * depth : (2 + j) * depth
            ]
        first = pl.multiple_of(places[p] * emb, emb)
        for q in range(depth // emb):
            weight[pl.ds(first, emb), q * depth : (q + 1) * depth] = source[
                begin + q * emb : begin + (q + 1) * emb, :depth
            ]


def unpack(places, gathered, near, far, emb):
    count, depth, columns = gathered.shape
    return pl.pallas_call(
        unpack_kernel,
        in_specs=[SMEM_SPEC] + [VMEM_SPEC] * 3,
        out_specs=[VMEM_SPEC] * 3,
        out_shape=[
            jax.ShapeDtypeStruct((count * depth, columns), bf16),
            jax.ShapeDtypeStruct((2 * depth, count * depth), bf16),
            jax.ShapeDtypeStruct((emb, depth * depth // (emb // count)), bf16),
        ],
        compiler_params=pltpu.CompilerParams(vmem_limit_bytes=32 << 20),
        cost_estimate=estimate(0, 0),
        name="unpack",
    )(places, gathered, near, far)


def spread_kernel(places, gathered, up, down):
    per = up.shape[0] // 8
    for p in range(8):
        up[p * per : (p + 1) * per] = gathered[places[p], :per]
        for j in range(down.shape[0] // per):
            down[j * per : (j + 1) * per, p * per : (p + 1) * per] = gathered[
                places[p], per:, j * per : (j + 1) * per
            ]


def spread(places, gathered):
    width = gathered.shape[2]
    return pl.pallas_call(
        spread_kernel,
        in_specs=[SMEM_SPEC, VMEM_SPEC],
        out_specs=[VMEM_SPEC] * 2,
        out_shape=[jax.ShapeDtypeStruct((width, width), bf16)] * 2,
        compiler_params=pltpu.CompilerParams(vmem_limit_bytes=32 << 20),
        cost_estimate=estimate(0, 0),
        name="spread",
    )(places, gathered)


def bundle_kernel(places, up, down, gathered):
    per = up.shape[0] // 8
    for p in range(8):
        gathered[places[p], :per] = up[p * per : (p + 1) * per]
        for j in range(down.shape[0] // per):
            gathered[places[p], per:, j * per : (j + 1) * per] = down[
                j * per : (j + 1) * per, p * per : (p + 1) * per
            ]


def bundle(places, up, down):
    width = up.shape[1]
    return pl.pallas_call(
        bundle_kernel,
        in_specs=[SMEM_SPEC] + [VMEM_SPEC] * 2,
        out_specs=VMEM_SPEC,
        out_shape=jax.ShapeDtypeStruct((8, width // 4, width), bf16),
        compiler_params=pltpu.CompilerParams(vmem_limit_bytes=32 << 20),
        cost_estimate=estimate(0, 0),
        name="bundle",
    )(places, up, down)


def second_norm_kernel(docs, document, stream_zero, mine, other, scale, shift, stream, hidden):
    value = stream_zero[...] + (mine[...].astype(f32) + other[...].astype(f32))
    stream[...] = value
    normal, _ = normal_of(value)
    which = document[...]
    hidden[...] = (
        normal * (1.0 + row_mods(which, scale[...], docs)) + row_mods(which, shift[...], docs)
    ).astype(bf16)


def second_norm(docs, document, stream_zero, mine, other, scale, shift):
    half, width = mine.shape
    block = half // 2
    part = vmem((block, width), lambda i: (i, 0))
    return pl.pallas_call(
        functools.partial(second_norm_kernel, docs),
        grid=(2,),
        in_specs=[
            vmem((block, 1), lambda i: (i, 0)),
            part,
            part,
            part,
            vmem(scale.shape),
            vmem(shift.shape),
        ],
        out_specs=[part, part],
        out_shape=[
            jax.ShapeDtypeStruct((half, width), f32),
            jax.ShapeDtypeStruct((half, width), bf16),
        ],
        compiler_params=pltpu.CompilerParams(vmem_limit_bytes=32 << 20),
        cost_estimate=estimate(2 * half * width * 128, 12 * half * width),
        name="second_norm",
    )(document, stream_zero, mine, other, scale, shift)


def add_up(target, value):
    @pl.when(pl.program_id(0) == 0)
    def _():
        target[...] = value

    @pl.when(pl.program_id(0) > 0)
    def _():
        target[...] += value


def back_through_norm(docs, grad, value, which, scale):
    normal, inverse = normal_of(value)
    inner = grad * (1.0 + row_mods(which, scale, docs))
    back = inverse * (
        inner
        - jnp.mean(inner, axis=-1, keepdims=True)
        - normal * jnp.mean(inner * normal, axis=-1, keepdims=True)
    )
    lane = lax.broadcasted_iota(jnp.int32, (which.shape[0], 8), 1)
    member = (lane == which).astype(bf16)
    by_scale = dot(member, (grad * normal).astype(bf16), COLUMNS_OF_BOTH)
    by_shift = dot(member, grad.astype(bf16), COLUMNS_OF_BOTH)
    return back, by_scale, by_shift


def second_back_kernel(
    docs, document, stream, mine, other, scale, cotangent, stream_grad, low, by_scale, by_shift
):
    grad = mine[...].astype(f32) + other[...].astype(f32)
    back, for_scale, for_shift = back_through_norm(
        docs, grad, stream[...], document[...], scale[...]
    )
    add_up(by_scale, for_scale)
    add_up(by_shift, for_shift)
    total = cotangent[...].astype(f32) + back
    stream_grad[...] = total
    low[...] = total.astype(bf16)


def second_back(docs, document, stream, mine, other, scale, cotangent):
    half, width = mine.shape
    block = half // 2
    part = vmem((block, width), lambda i: (i, 0))
    sums = vmem((8, width))
    return pl.pallas_call(
        functools.partial(second_back_kernel, docs),
        grid=(2,),
        in_specs=[
            vmem((block, 1), lambda i: (i, 0)),
            part,
            part,
            part,
            vmem(scale.shape),
            part,
        ],
        out_specs=[part, part, sums, sums],
        out_shape=[
            jax.ShapeDtypeStruct((half, width), f32),
            jax.ShapeDtypeStruct((half, width), bf16),
            jax.ShapeDtypeStruct((8, width), f32),
            jax.ShapeDtypeStruct((8, width), f32),
        ],
        compiler_params=pltpu.CompilerParams(vmem_limit_bytes=32 << 20),
        cost_estimate=estimate(2 * half * width * 128, 16 * half * width),
        name="second_back",
    )(document, stream, mine, other, scale, cotangent)


def first_back_kernel(
    docs, flag, document, both, far, weight, project, grad_projected, scale, above, own, other,
    grad_weight, by_scale, by_shift,
):
    at = pl.program_id(0)
    rows = grad_projected.shape[0]
    embed = jnp.where(at < 2, both[0, :rows], far[0, :rows])
    value = dot(embed, weight[...])
    grad = dot(grad_projected[...], project[...], ROWS_OF_BOTH)
    back, for_scale, for_shift = back_through_norm(docs, grad, value, document[...], scale[...])
    add_up(by_scale, for_scale)
    add_up(by_shift, for_shift)
    counts = jnp.where(at < 2, flag[0], 0).astype(f32)
    low = (back + counts * above[...]).astype(bf16)
    grad_embed = dot(low, weight[...], ROWS_OF_BOTH)

    @pl.when(at < 2)
    def _():
        own[...] = grad_embed

    @pl.when(at >= 2)
    def _():
        other[...] = grad_embed.astype(bf16)

    add_up(grad_weight, dot(embed, low, COLUMNS_OF_BOTH))


def first_back(docs, flag, document, both, far, weight, project, grad_projected, scale, above):
    emb, width = weight.shape
    rows = document.shape[0]
    quarter = rows // 4
    message = both.shape[1]
    sums = vmem((8, width))
    early = lambda i: (jnp.minimum(i, 1), 0)
    late = lambda i: (jnp.maximum(i - 2, 0), 0)
    return pl.pallas_call(
        functools.partial(first_back_kernel, docs),
        grid=(4,),
        in_specs=[
            SMEM_SPEC,
            vmem((quarter, 1), lambda i: (i, 0)),
            vmem((1, message, emb), lambda i: (jnp.minimum(i, 1), 0, 0)),
            vmem((1, message, emb), lambda i: (jnp.maximum(i - 2, 0), 0, 0)),
            vmem(weight.shape),
            vmem(project.shape),
            vmem((quarter, project.shape[1]), lambda i: (i, 0)),
            vmem(scale.shape),
            vmem((quarter, width), early),
        ],
        out_specs=[
            vmem((quarter, emb), early),
            vmem((quarter, emb), late),
            vmem((emb, width)),
            sums,
            sums,
        ],
        out_shape=[
            jax.ShapeDtypeStruct((rows // 2, emb), f32),
            jax.ShapeDtypeStruct((rows // 2, emb), bf16),
            jax.ShapeDtypeStruct((emb, width), f32),
            jax.ShapeDtypeStruct((8, width), f32),
            jax.ShapeDtypeStruct((8, width), f32),
        ],
        compiler_params=pltpu.CompilerParams(vmem_limit_bytes=32 << 20),
        cost_estimate=estimate(2 * rows * width * (3 * emb + project.shape[1]), 16 * rows * width),
        name="first_back",
    )(flag, document, both, far, weight, project, grad_projected, scale, above)


def local_sums_kernel(spots, weight, *refs):
    mods, (far_embed, own, other) = refs[:4], refs[4:]
    emb = weight.shape[0]
    per = weight.shape[1] // 8
    share = emb + 32
    flag = spots[9].astype(f32)
    for target, core in ((own, spots[8]), (other, 1 - spots[8])):
        for x in range(2):
            column = 2 * x + core
            base = x * share
            for j in range(2):
                start = pl.multiple_of(spots[column * 2 + j] * per, per)
                target[base : base + emb, j * per : (j + 1) * per] = weight[
                    :, pl.ds(start, per)
                ].astype(target.dtype)
            for q in range(4):
                halves = []
                for j in range(2):
                    start = pl.multiple_of(spots[2 * q + j] * per, per)
                    total = mods[2 * x][:, pl.ds(start, per)]
                    total = jnp.where(core == 0, total, mods[2 * x + 1][:, pl.ds(start, per)])
                    halves.append(total if x == 0 else total * flag)
                block = jnp.concatenate(halves, axis=1)
                target[base + emb + q * 8 : base + emb + (q + 1) * 8] = block.astype(target.dtype)
    other[2 * share :] = far_embed[...]


def local_sums(spots, weight, mods, far_embed):
    emb = weight.shape[0]
    rows = 2 * (emb + 32)
    return pl.pallas_call(
        local_sums_kernel,
        in_specs=[SMEM_SPEC] + [VMEM_SPEC] * 6,
        out_specs=[VMEM_SPEC] * 2,
        out_shape=[
            jax.ShapeDtypeStruct((rows, emb), f32),
            jax.ShapeDtypeStruct((rows + far_embed.shape[0], emb), bf16),
        ],
        compiler_params=pltpu.CompilerParams(vmem_limit_bytes=32 << 20),
        cost_estimate=estimate(0, 0),
        name="local_sums",
    )(spots, weight, *mods, far_embed)


def chip_sums_kernel(spots, own, received, own_embed, keep, send):
    share = own.shape[0] // 2
    quarter = own_embed.shape[0] // 2
    for target, x in ((keep, spots[0]), (send, 1 - spots[0])):
        start = pl.multiple_of(x * share, share)
        total = own[pl.ds(start, share)] + received[pl.ds(start, share)].astype(f32)
        target[:share] = total.astype(target.dtype)
        rows = pl.multiple_of(x * quarter, quarter)
        far = received[pl.ds(pl.multiple_of(2 * share + rows, 64), quarter)]
        total = own_embed[pl.ds(rows, quarter)] + far.astype(f32)
        target[share:] = total.astype(target.dtype)


def chip_sums(spots, own, received, own_embed):
    emb = own.shape[1]
    rows = own.shape[0] // 2 + own_embed.shape[0] // 2
    return pl.pallas_call(
        chip_sums_kernel,
        in_specs=[SMEM_SPEC] + [VMEM_SPEC] * 3,
        out_specs=[VMEM_SPEC] * 2,
        out_shape=[
            jax.ShapeDtypeStruct((rows, emb), f32),
            jax.ShapeDtypeStruct((rows, emb), bf16),
        ],
        cost_estimate=estimate(0, 0),
        name="chip_sums",
    )(spots, own, received, own_embed)


def outgoing_kernel(spots, own, other, *refs):
    *messages, low = refs
    emb = own.shape[1]
    total = (own[...] + other[...].astype(f32)).astype(bf16)
    low[...] = total[:emb]
    piece = emb // 8
    mods = total[emb : emb + 32]
    rows = total.shape[0] - emb - 32
    base = rows + 32
    for k, message in enumerate(messages):
        message[:rows] = total[emb + 32 :]
        message[rows:base] = mods
        for j in range(2):
            start = pl.multiple_of(spots[2 * k + j] * piece, piece)
            message[base + j * piece : base + (j + 1) * piece] = low[pl.ds(start, piece)]


def outgoing(spots, own, other):
    emb = own.shape[1]
    rows = own.shape[0] - emb + 2 * (emb // 8)
    return pl.pallas_call(
        outgoing_kernel,
        in_specs=[SMEM_SPEC] + [VMEM_SPEC] * 2,
        out_specs=[VMEM_SPEC] * 4,
        out_shape=[jax.ShapeDtypeStruct((rows, emb), bf16)] * 4,
        scratch_shapes=[pltpu.VMEM((emb, emb), bf16)],
        cost_estimate=estimate(0, 0),
        name="outgoing",
    )(spots, own, other)


def relay_kernel(share, piece, *refs):
    *arrived, message, keep = refs
    for k, ref in enumerate(arrived):
        message[k * share : (k + 1) * share] = ref[:share]
    for j, target in ((0, keep), (1, message)):
        begin = share + j * piece
        total = sum(ref[begin : begin + piece].astype(f32) for ref in arrived)
        if j:
            message[4 * share :] = total.astype(bf16)
        else:
            keep[...] = total


def relay(share, piece, arrived):
    emb = arrived[0].shape[1]
    return pl.pallas_call(
        functools.partial(relay_kernel, share, piece),
        in_specs=[VMEM_SPEC] * 4,
        out_specs=[VMEM_SPEC] * 2,
        out_shape=[
            jax.ShapeDtypeStruct((4 * share + piece, emb), bf16),
            jax.ShapeDtypeStruct((piece, emb), f32),
        ],
        cost_estimate=estimate(0, 0),
        name="relay",
    )(*arrived)


def landed_kernel(share, rows, features, near, far, keep, small):
    width = small.shape[1] - keep.shape[1]
    total = jnp.zeros((features.shape[1], width), f32)
    for k in range(8):
        source, begin = (near, far)[k // 4], k % 4 * share + rows
        mods = jnp.concatenate(
            [source[begin + q * 8 : begin + q * 8 + 8] for q in range(4)], axis=1
        )
        total += dot(features[k * 8 : (k + 1) * 8], mods, COLUMNS_OF_BOTH)
    small[:, :width] = total
    small[:, width:] = keep[...] + far[4 * share :].astype(f32)


def landed(docs, share, rows, width, features, near, far, keep):
    return pl.pallas_call(
        functools.partial(landed_kernel, share, rows),
        in_specs=[VMEM_SPEC] * 4,
        out_specs=VMEM_SPEC,
        out_shape=jax.ShapeDtypeStruct((features.shape[1], width + keep.shape[1]), f32),
        cost_estimate=estimate(0, 0),
        name="landed",
    )(features, near, far, keep)


def per_device(
    token_ids,
    lengths,
    time_steps,
    embed_table,
    input_weight,
    time_weight,
    project_weight,
    output_weight,
    up_weight,
    down_weight,
    cotangent,
):
    rows = token_ids.shape[0]
    half, quarter = rows // 2, rows // 4
    count = lax.axis_size("dp")
    groups = lax.axis_size("tensor")
    me = lax.axis_index("dp")
    place = lax.axis_index("tensor")
    x, c = place // 2, place % 2
    width = cotangent.shape[1]
    docs = lengths.shape[0]
    shard = embed_table.shape[0]
    emb_rows = input_weight.shape[0]
    head_width = project_weight.shape[1]
    heads = head_width // (3 * HD)
    third = heads * HD
    per = width // count
    dp = Direct(count)

    my_ids = lax.dynamic_slice_in_dim(token_ids, (c * 2 + x) * quarter, quarter)
    heard = jnp.concatenate([my_ids, time_steps])[None]
    table = embed_table.astype(f32)
    rscale = lax.rsqrt(jnp.mean(table * table, axis=1, keepdims=True) + table_eps)
    normed = (table * rscale).astype(bf16)
    crossed = swap_x(normed)
    heard = jnp.concatenate([heard, dp.swap(after(heard, normed), 4)], axis=0)

    packed, small = pack_first(scalars([c]), project_weight, input_weight, output_weight)
    packed = lax.all_gather(packed, "dp")
    small_z2 = dp.swap(small, 4)
    gathered = lax.all_gather(pack_second(up_weight, down_weight), "dp")
    heard = jnp.concatenate([heard, dp.swap(heard, 2)], axis=0)
    heard = jnp.concatenate([heard, dp.swap(heard, 1)], axis=0)

    pair = jnp.concatenate([normed, crossed], axis=0)
    shards = jnp.concatenate([pair, swap_core(pair)], axis=0)
    entry = jnp.arange(4 * shard, dtype=jnp.int32)
    which = entry // shard
    owner = (x ^ (which & 1)) * 2 + (c ^ (which >> 1))
    vocab = (me * groups + owner) * shard + entry % shard

    feature = me * emb_rows + jnp.arange(emb_rows, dtype=jnp.int32)
    part = EMB // 2
    frequency = jnp.exp(-math.log(10000.0) * (feature % part).astype(f32) / part)
    angles = heard[:, quarter:].astype(f32)[:, :, None] * frequency[None, None, :]
    features = jnp.where(feature[None, None, :] < part, jnp.sin(angles), jnp.cos(angles))
    features = features.astype(bf16)
    time_part = lax.dynamic_slice_in_dim(time_weight, place * width, width, 1)
    found_mods = dot(features.reshape(count * docs, emb_rows), time_part)
    found_mods = found_mods.reshape(count, docs, 4, EMB).transpose(0, 2, 1, 3)
    found_mods = jnp.concatenate(split_two(found_mods.reshape(count, 4 * docs, EMB)), axis=1)

    def look_up(begin, end):
        names = heard[begin:end, :quarter].reshape(-1)
        onehot = (names[:, None] == vocab[None, :]).astype(bf16)
        found = dot(onehot, shards).astype(bf16).reshape(end - begin, quarter, EMB)
        return jnp.concatenate([found, found_mods[begin:end]], axis=1)

    looked_up = look_up(4, 8)
    crossed = dp.swap(looked_up, 1)
    small = jnp.concatenate([small, after(small_z2, looked_up)], axis=0)
    small_z1 = dp.swap(small, 2)
    near = look_up(0, 4)
    crossed, small_z1 = join(crossed, small_z1)
    near = near.astype(f32) + crossed.astype(f32)
    mods = near[:, quarter : quarter + 4 * docs] + near[:, quarter + 4 * docs :]
    near = jnp.concatenate([near[:, :quarter].astype(bf16), *split_two(mods)], axis=1)

    small = jnp.concatenate([small, small_z1], axis=0)
    small_far = dp.swap(small, 1)
    arrived = [near[0]] + [dp.swap(near[k], ORDER[k]) for k in (1, 2, 3)]
    arrived[3], small_far = join(arrived[3], small_far)
    mine = finish(True, docs, dp.places, arrived)
    project, output, input_half = unpack(
        scalars(dp.places), after(packed, mine), small, small_far, EMB
    )
    input_other = swap_core(input_half)
    input_full = jnp.concatenate(
        [jnp.where(c == 0, input_half, input_other), jnp.where(c == 0, input_other, input_half)],
        axis=1,
    )
    input_full = permute(input_full, [0], dp.places)
    other = swap_x(mine)
    both = jnp.stack([jnp.where(x == 0, mine, other), jnp.where(x == 0, other, mine)])
    far = swap_core(both)
    own_mods, far_mods = both[:, quarter:], far[:, quarter:]
    scale_one, scale_two = jnp.where(c == 0, own_mods, far_mods)
    shift_one, shift_two = jnp.where(c == 0, far_mods, own_mods)

    position = jnp.arange(rows, dtype=jnp.int32) ^ (c * half)
    ends = jnp.cumsum(lengths)
    document = jnp.sum((position[:, None] >= ends[None, :]).astype(jnp.int32), axis=1)
    column = document[:, None]
    cot = permute(after(cotangent, heard), [c, 1 - c], dp.places)

    hidden_one, query, keys, values, stream_zero = front(
        docs, column, both, far, input_full, project, scale_one, shift_one
    )

    def reduce_core(own, far, weight, dims=((1,), (0,))):
        sent = swap_core(dot(far, weight, dims).astype(bf16))
        return (dot(own, weight, dims) + sent.astype(f32)).astype(bf16)

    def over_rows(left, right):
        return dot(left[0], right[0], COLUMNS_OF_BOTH) + dot(left[1], right[1], COLUMNS_OF_BOTH)

    attended, logsum = attention(document, query, keys, values)
    attention_sum = reduce_core(attended[:half], attended[half:], output)
    crossed = swap_x(attention_sum)
    crossed, cot = join(crossed, cot)
    up, down = spread(scalars(dp.places), after(gathered, attention_sum))
    stream_one, hidden = second_norm(
        docs, column, stream_zero, attention_sum, crossed, scale_two, shift_two
    )
    hidden_two = (hidden, swap_core(hidden))
    cot_two = (cot[:half], cot[half:])
    activated, grad_upward = [], []
    for at in range(2):
        upward = dot(hidden_two[at], up)
        phi = 0.5 * (1.0 + lax.erf(upward * math.sqrt(0.5)))
        activated.append((upward * phi).astype(bf16))
        slope = phi + upward * (math.sqrt(0.5 / math.pi) * jnp.exp(-0.5 * upward * upward))
        grad_active = dot(cot_two[at], down, ROWS_OF_BOTH)
        grad_upward.append((grad_active * slope).astype(bf16))
    grad_two = reduce_core(*grad_upward, up, ROWS_OF_BOTH)
    crossed = swap_x(grad_two)
    activated = [after(part, grad_two) for part in activated]
    grad_down = over_rows(activated, cot_two).astype(bf16)
    grad_up = over_rows(hidden_two, [after(part, grad_two) for part in grad_upward]).astype(bf16)
    bundled = bundle(scalars(dp.places), grad_up, grad_down)
    branch_sum = reduce_core(*activated, down)

    reduced = lax.psum_scatter(bundled, "dp", scatter_dimension=0, tiled=False)
    crossed, bundled, branch_sum = join(crossed, bundled, branch_sum)
    grad_one, low, *by_two = second_back(
        docs, column, stream_one, grad_two, crossed, scale_two, cot
    )
    grad_attn = (low, swap_core(low))
    grad_attended = jnp.concatenate(
        [dot(part, output, ROWS_OF_BOTH).astype(bf16) for part in grad_attn], axis=0
    )
    grad_projected = attention_back(
        document, query, keys, values, grad_attended, attended, logsum
    )
    flag = jnp.where(x == 0, 1, 0)
    own_embed, far_embed, grad_input, *by_one = first_back(
        docs,
        scalars([flag]),
        column,
        both,
        far,
        input_full,
        project,
        grad_projected,
        scale_one,
        grad_one,
    )
    share = quarter + 32
    own_sums, far_sums = local_sums(
        scalars(dp.inverse + [c, flag]), grad_input, [*by_one, *by_two], far_embed
    )
    received = swap_core(far_sums)
    keep, send = chip_sums(scalars([x]), own_sums, received, own_embed)
    crossed = swap_x(send)
    grad_project = dot(hidden_one, after(grad_projected, send), COLUMNS_OF_BOTH)
    grad_output = over_rows((attended[:half], attended[half:]), grad_attn)
    grad_output = jnp.concatenate(
        [unfold(grad_output[:, k * per : (k + 1) * per], 2) for k in range(count)], axis=0
    )
    grad_packed = jnp.concatenate([grad_project, grad_output], axis=1).astype(bf16)
    crossed, grad_packed = join(crossed, grad_packed)
    packed_first = dp.swap(grad_packed[width // 2 :], 1)
    branch_crossed = swap_x(after(branch_sum, crossed))
    messages = outgoing(scalars([me ^ v ^ j for v in ORDER[:4] for j in range(2)]), keep, crossed)
    arrived = [messages[0]] + [dp.swap(messages[k], ORDER[k]) for k in (1, 2, 3)]
    arrived[3], packed_first, reduced = join(arrived[3], packed_first, reduced)
    near, keep = relay(share, emb_rows, arrived)
    far = dp.swap(near, 1)
    packed_first = after(packed_first, near)
    branch_crossed = after(branch_crossed, near)
    packed_sum = grad_packed[: width // 2].astype(f32) + packed_first.astype(f32)
    packed_second = dp.swap(packed_sum[2 * per :].astype(bf16), 2)

    names = jnp.pad(heard[:, :quarter], ((0, 0), (0, share - quarter)), constant_values=-1)
    near_ids, far_ids = names[:4].reshape(-1), names[4:].reshape(-1)
    near_ids, far_ids = (
        jnp.pad(part, (0, emb_rows), constant_values=-1) for part in (near_ids, far_ids)
    )

    def table_part(first, last, tokens, names):
        onehot = (vocab[first * shard : last * shard, None] == names[None, :]).astype(bf16)
        return dot(onehot, tokens)

    near_low = table_part(0, 4, near, near_ids)
    block = branch_sum.astype(f32) + branch_crossed.astype(f32)
    block = (stream_one + block).astype(bf16)
    block_out = jnp.concatenate([block, swap_core(block)], axis=0)
    block_out = permute(block_out, [c, 1 - c], dp.inverse)
    far, packed_second, block_out, near_low = join(far, packed_second, block_out, near_low)
    theirs = near_low[2 * shard :] + table_part(2, 4, far, far_ids)
    theirs = swap_core(theirs.astype(bf16)).astype(f32)
    sent = near_low[shard : 2 * shard] + table_part(1, 2, far, far_ids)
    sent_low = (sent + theirs[shard:]).astype(bf16)
    sent = swap_x(sent_low)
    kept = near_low[:shard] + table_part(0, 1, far, far_ids) + theirs[:shard]

    features = jnp.pad(features, ((0, 0), (0, 8 - docs), (0, 0))).reshape(8 * count, emb_rows)
    small = landed(docs, share, quarter, width, features, near, far, after(keep, sent_low))
    packed_sum = packed_sum[: 2 * per] + after(packed_second, sent_low).astype(f32)
    packed_third = dp.swap(packed_sum[per:].astype(bf16), 4)
    other = swap_x(small)

    reduced = reduced.astype(f32)
    summed_up, summed_down = reduced[:per], fold(reduced[per:], per)
    summed_packed = packed_sum[:per] + after(packed_third, kept).astype(f32)
    summed_project = summed_packed[:, :head_width]
    summed_output = fold(summed_packed[:, head_width:], per)
    summed_project = (
        summed_project.reshape(per, 3, heads, HD).transpose(0, 2, 1, 3).reshape(per, head_width)
    )
    sent, kept, summed_up, summed_down = join(sent, kept, summed_up, summed_down)
    other = after(other, sent)
    both = jnp.stack([jnp.where(x == 0, small, other), jnp.where(x == 0, other, small)])
    far = swap_core(both)
    pieces = []
    for at in range(2):
        pieces += [jnp.where(c == 0, both[at], far[at]), jnp.where(c == 0, far[at], both[at])]
    summed_time = jnp.concatenate([piece[:, :width] for piece in pieces], axis=1)
    summed_input = jnp.concatenate([piece[:, width:] for piece in pieces], axis=1)
    grad_normed = kept + sent.astype(f32)
    grad_table = rscale * grad_normed - table * (
        rscale * rscale * rscale * jnp.mean(grad_normed * table, axis=1, keepdims=True)
    )
    return (
        block_out,
        grad_table,
        summed_input,
        summed_time,
        summed_project,
        summed_output,
        summed_up,
        summed_down,
    )


def normalize(table_rows):
    return table_rows * lax.rsqrt(
        jnp.mean(table_rows * table_rows, axis=1, keepdims=True) + table_eps
    )


def layer_norm(value, scale, shift):
    centred = value - jnp.mean(value, axis=-1, keepdims=True)
    return (
        centred
        * lax.rsqrt(jnp.mean(centred * centred, axis=-1, keepdims=True) + norm_eps)
        * (1.0 + scale)
        + shift
    )


def time_features(step_index, width):
    half = width // 2
    frequency = jnp.exp(-math.log(10000.0) * jnp.arange(half).astype(jnp.float32) / half)
    angles = step_index.astype(jnp.float32)[:, None] * frequency[None, :]
    return jnp.concatenate([jnp.sin(angles), jnp.cos(angles)], axis=1)


def gelu_exact(value):
    return jax.nn.gelu(value, approximate=False)


def whole_collectives(
    token_ids,
    lengths,
    time_steps,
    embed_table,
    input_weight,
    time_weight,
    project_weight,
    output_weight,
    up_weight,
    down_weight,
    cotangent,
):
    rows = token_ids.shape[0]
    groups = lax.axis_size("tensor")
    tensor_place = lax.axis_index("tensor")
    shard_rows = embed_table.shape[0]
    factor = 1.0 / math.sqrt(HD)
    normed, normed_back = jax.vjp(normalize, embed_table.astype(jnp.float32))
    normed_low = normed.astype(jnp.bfloat16)
    gathered = (
        lax.all_gather(input_weight, "dp", axis=0, tiled=True),
        lax.all_gather(time_weight, "dp", axis=0, tiled=True),
        lax.all_gather(project_weight, "dp", axis=0, tiled=True),
        lax.all_gather(output_weight, "dp", axis=1, tiled=True),
        lax.all_gather(up_weight, "dp", axis=0, tiled=True),
        lax.all_gather(down_weight, "dp", axis=1, tiled=True),
    )
    input_full, time_full, project_full, output_full, up_full, down_full = gathered

    def vocab_rows(count):
        flat_index = jnp.arange(count, dtype=jnp.int32)
        return (
            flat_index // shard_rows * groups + tensor_place
        ) * shard_rows + flat_index % shard_rows

    token_block = min(256, rows)
    piece = lax.all_gather(normed_low, "dp", axis=0, tiled=True)
    vocab = vocab_rows(piece.shape[0])
    parts = []
    for add_begin in range(0, rows, token_block):
        add_onehot = (
            token_ids[add_begin : add_begin + token_block, None] == vocab[None, :]
        ).astype(jnp.bfloat16)
        parts.append(jnp.dot(add_onehot, piece, preferred_element_type=jnp.float32))
    partial_embed = jnp.concatenate(parts, axis=0)
    embed = lax.psum(partial_embed.astype(jnp.bfloat16), "tensor")
    stream_zero = jnp.dot(embed, input_full, preferred_element_type=jnp.float32)
    ends = jnp.cumsum(lengths)
    position = jnp.arange(rows, dtype=jnp.int32)
    document = jnp.sum((position[:, None] >= ends[None, :]).astype(jnp.int32), axis=1)
    member = (document[:, None] == jnp.arange(lengths.shape[0], dtype=jnp.int32)[None, :]).astype(
        jnp.float32
    )
    features = time_features(time_steps, EMB).astype(jnp.bfloat16)
    modulation = jnp.dot(features, time_full, preferred_element_type=jnp.float32)
    row_mods = jnp.dot(member, modulation, precision=highest)
    scale_one, shift_one, scale_two, shift_two = jnp.split(row_mods, 4, axis=1)
    normed_one, norm_one_back = jax.vjp(layer_norm, stream_zero, scale_one, shift_one)
    hidden_one = normed_one.astype(jnp.bfloat16)
    projected = jnp.dot(hidden_one, project_full, preferred_element_type=jnp.float32).astype(
        jnp.bfloat16
    )
    heads_here = projected.shape[1] // (3 * HD)
    projected = projected.reshape(rows, heads_here, 3, HD)
    query = jnp.transpose(projected[:, :, 0], (1, 0, 2))
    keys = jnp.transpose(projected[:, :, 1], (1, 0, 2))
    values = jnp.transpose(projected[:, :, 2], (1, 0, 2))
    query_block = min(512, rows)

    def scores_of(begin):
        block_query = query[:, begin : begin + query_block]
        plain = (
            jnp.einsum("hqd,hkd->hqk", block_query, keys, preferred_element_type=jnp.float32)
            * factor
        )
        allowed = document[begin : begin + query_block, None] == document[None, :]
        return (jnp.where(allowed[None], plain, masked_score), block_query)

    outputs = []
    logsums = []
    kept_probs = []
    for begin in range(0, rows, query_block):
        scores, block_query = scores_of(begin)
        peak = jnp.max(scores, axis=2, keepdims=True)
        expo = jnp.exp(scores - peak)
        total = jnp.sum(expo, axis=2, keepdims=True)
        logsums.append(peak + jnp.log(total))
        probs_low = (expo / total).astype(jnp.bfloat16)
        kept_probs.append(probs_low)
        outputs.append(
            jnp.einsum("hqk,hkd->hqd", probs_low, values, preferred_element_type=jnp.float32)
        )
    attended = (
        jnp.transpose(jnp.concatenate(outputs, axis=1), (1, 0, 2))
        .reshape(rows, heads_here * HD)
        .astype(jnp.bfloat16)
    )
    attention_sum = lax.psum(
        jnp.dot(attended, output_full, preferred_element_type=jnp.float32), "tensor"
    )
    stream_one_rows = stream_zero + attention_sum
    normed_two, norm_two_back = jax.vjp(layer_norm, stream_one_rows, scale_two, shift_two)
    hidden_two = normed_two.astype(jnp.bfloat16)
    upward = jnp.dot(hidden_two, up_full, preferred_element_type=jnp.float32)
    activated, gelu_back = jax.vjp(gelu_exact, upward)
    activated_low = activated.astype(jnp.bfloat16)
    branch = lax.psum(
        jnp.dot(activated_low, down_full, preferred_element_type=jnp.float32), "tensor"
    )
    block_out = (stream_one_rows + branch).astype(jnp.bfloat16)
    grad_down = jnp.dot(activated_low.T, cotangent, preferred_element_type=jnp.float32)
    grad_active = jnp.dot(cotangent, down_full.T, preferred_element_type=jnp.float32)
    grad_upward = gelu_back(grad_active)[0].astype(jnp.bfloat16)
    grad_up = jnp.dot(hidden_two.T, grad_upward, preferred_element_type=jnp.float32)
    grad_hidden_two = lax.psum(
        jnp.dot(grad_upward, up_full.T, preferred_element_type=jnp.float32), "tensor"
    )
    grad_stream_rows, grad_scale_two, grad_shift_two = norm_two_back(grad_hidden_two)
    grad_stream_rows = grad_stream_rows + cotangent.astype(jnp.float32)
    grad_attn_rows = grad_stream_rows.astype(jnp.bfloat16)
    grad_output = jnp.dot(attended.T, grad_attn_rows, preferred_element_type=jnp.float32)
    grad_attended = jnp.dot(
        grad_attn_rows, output_full.T, preferred_element_type=jnp.float32
    ).astype(jnp.bfloat16)
    grad_attended = jnp.transpose(grad_attended.reshape(rows, heads_here, HD), (1, 0, 2))
    query_grads = []
    grad_keys = jnp.zeros(keys.shape, jnp.float32)
    grad_values = jnp.zeros(values.shape, jnp.float32)
    for number, begin in enumerate(range(0, rows, query_block)):
        scores, block_query = scores_of(begin)
        probs = jnp.exp(scores - logsums[number])
        block_grad = grad_attended[:, begin : begin + query_block]
        grad_probs = jnp.einsum(
            "hqd,hkd->hqk", block_grad, values, preferred_element_type=jnp.float32
        )
        inner = jnp.sum(probs * grad_probs, axis=2, keepdims=True)
        grad_scores = (probs * (grad_probs - inner)).astype(jnp.bfloat16)
        query_grads.append(
            jnp.einsum("hqk,hkd->hqd", grad_scores, keys, preferred_element_type=jnp.float32)
            * factor
        )
        grad_keys = (
            grad_keys
            + jnp.einsum(
                "hqk,hqd->hkd", grad_scores, block_query, preferred_element_type=jnp.float32
            )
            * factor
        )
        grad_values = grad_values + jnp.einsum(
            "hqk,hqd->hkd", kept_probs[number], block_grad, preferred_element_type=jnp.float32
        )
    grad_query = jnp.concatenate(query_grads, axis=1)
    grad_projected = jnp.stack([grad_query, grad_keys, grad_values], axis=2)
    grad_projected = (
        jnp.transpose(grad_projected, (1, 0, 2, 3))
        .reshape(rows, heads_here * 3 * HD)
        .astype(jnp.bfloat16)
    )
    grad_project = jnp.dot(hidden_one.T, grad_projected, preferred_element_type=jnp.float32)
    grad_hidden_one = lax.psum(
        jnp.dot(grad_projected, project_full.T, preferred_element_type=jnp.float32), "tensor"
    )
    grad_stream_zero, grad_scale_one, grad_shift_one = norm_one_back(grad_hidden_one)
    grad_zero_low = (grad_stream_zero + grad_stream_rows).astype(jnp.bfloat16)
    grad_rows = jnp.concatenate(
        [grad_scale_one, grad_shift_one, grad_scale_two, grad_shift_two], axis=1
    )
    partial_modulation = jnp.dot(member.T, grad_rows, precision=highest)
    grad_stream_zero = grad_zero_low
    grad_input = jnp.dot(embed.T, grad_stream_zero, preferred_element_type=jnp.float32)
    grad_embed = jnp.dot(grad_stream_zero, input_full.T, preferred_element_type=jnp.float32).astype(
        jnp.bfloat16
    )
    grad_time = jnp.dot(features.astype(jnp.float32).T, partial_modulation, precision=highest)
    every_row = shard_rows * lax.axis_size("dp")
    vocab_all = vocab_rows(every_row)
    grad_normed = jnp.zeros((every_row, EMB), jnp.float32)
    for begin in range(0, rows, token_block):
        onehot = (token_ids[begin : begin + token_block, None] == vocab_all[None, :]).astype(
            jnp.bfloat16
        )
        grad_normed = grad_normed + jnp.einsum(
            "tv,te->ve",
            onehot,
            grad_embed[begin : begin + token_block],
            preferred_element_type=jnp.float32,
        )
    (
        summed_input,
        summed_time,
        summed_project,
        summed_output,
        summed_up,
        summed_down,
        summed_table,
    ) = (
        lax.psum_scatter(grad_input, "dp", scatter_dimension=0, tiled=True),
        lax.psum_scatter(grad_time, "dp", scatter_dimension=0, tiled=True),
        lax.psum_scatter(grad_project, "dp", scatter_dimension=0, tiled=True),
        lax.psum_scatter(grad_output, "dp", scatter_dimension=1, tiled=True),
        lax.psum_scatter(grad_up, "dp", scatter_dimension=0, tiled=True),
        lax.psum_scatter(grad_down, "dp", scatter_dimension=1, tiled=True),
        lax.psum_scatter(grad_normed, "dp", scatter_dimension=0, tiled=True),
    )
    grad_table = normed_back(summed_table)[0]
    return (
        block_out,
        grad_table,
        summed_input,
        summed_time,
        summed_project,
        summed_output,
        summed_up,
        summed_down,
    )


def solution(mesh):
    count, groups = mesh.shape["dp"], mesh.shape["tensor"]
    return jax.shard_map(
        per_device if count == len(ORDER) and groups == 4 else whole_collectives,
        mesh=mesh,
        in_specs=(
            P("dp"),
            P("dp"),
            P("dp"),
            P(("dp", "tensor"), None),
            P("dp", None),
            P("dp", None),
            P("dp", "tensor"),
            P("tensor", "dp"),
            P("dp", "tensor"),
            P("tensor", "dp"),
            P("dp", None),
        ),
        out_specs=(
            P("dp", None),
            P(("dp", "tensor"), None),
            P("dp", None),
            P("dp", None),
            P("dp", "tensor"),
            P("tensor", "dp"),
            P("dp", "tensor"),
            P("tensor", "dp"),
        ),
        check_vma=False,
    )
```

```python
import functools
import math

import jax
import jax.numpy as jnp
from jax import lax
from jax.experimental import pallas as pl
from jax.experimental.pallas import tpu as pltpu
from jax.sharding import PartitionSpec as P

HD = 64
EMB = 256

table_eps = 1e-06
norm_eps = 1e-05
masked_score = -1e30
highest = lax.Precision.HIGHEST
bf16 = jnp.bfloat16
f32 = jnp.float32


def dot(left, right, dims=((1,), (0,))):
    return lax.dot_general(left, right, (dims, ((), ())), preferred_element_type=f32)


def join(*values):
    return lax.optimization_barrier(values)


def after(value, *others):
    return lax.optimization_barrier((value,) + others)[0]


SWAP_CORE = [(0, 1), (1, 0), (2, 3), (3, 2)]
SWAP_X = [(0, 2), (2, 0), (1, 3), (3, 1)]


def swap_core(value):
    return lax.ppermute(value, "tensor", SWAP_CORE)


def swap_x(value):
    return lax.ppermute(value, "tensor", SWAP_X)


ROWS_OF_BOTH = ((1,), (1,))
COLUMNS_OF_BOTH = ((0,), (0,))
ORDER = (0, 4, 2, 6, 1, 5, 3, 7)


class Direct:
    def __init__(self, count):
        self.count = count
        self.me = lax.axis_index("dp")
        self.places = [self.me ^ v for v in ORDER]
        self.inverse = [
            sum(jnp.where(self.places[k] == a, k, 0) for k in range(count)) for a in range(count)
        ]

    def swap(self, value, v):
        return lax.ppermute(value, "dp", [(i, i ^ v) for i in range(self.count)])

    def spread_small(self, value):
        value = value[None]
        for v in (4, 2, 1):
            value = jnp.concatenate([value, self.swap(value, v)], axis=0)
        return value


def picked(value, places, axis):
    size = value.shape[axis] // len(ORDER)
    return jnp.concatenate(
        [lax.slice_in_dim(value, p * size, (p + 1) * size, axis=axis) for p in places], axis=axis
    )


def split_two(value):
    high = value.astype(bf16)
    return high, (value - high.astype(f32)).astype(bf16)


def fold(value, width):
    return jnp.concatenate(jnp.split(value, value.shape[1] // width, axis=1), axis=0)


def unfold(value, count):
    return jnp.concatenate(jnp.split(value, count, axis=0), axis=1)


def permute_kernel(row_places, column_places, source, target):
    rows = source.shape[0] // row_places.shape[0]
    columns = source.shape[1] // column_places.shape[0]
    for i in range(row_places.shape[0]):
        for j in range(column_places.shape[0]):
            first = pl.multiple_of(row_places[i] * rows, rows)
            second = pl.multiple_of(column_places[j] * columns, columns)
            target[i * rows : (i + 1) * rows, j * columns : (j + 1) * columns] = source[
                pl.ds(first, rows), pl.ds(second, columns)
            ]


def permute(value, row_places, column_places):
    lists = [jnp.stack([jnp.int32(p) for p in places]) for places in (row_places, column_places)]
    return pl.pallas_call(
        permute_kernel,
        out_shape=jax.ShapeDtypeStruct(value.shape, value.dtype),
        in_specs=[pl.BlockSpec(memory_space=pltpu.SMEM)] * 2
        + [pl.BlockSpec(memory_space=pltpu.VMEM)],
        out_specs=pl.BlockSpec(memory_space=pltpu.VMEM),
        compiler_params=pltpu.CompilerParams(vmem_limit_bytes=32 << 20),
        cost_estimate=estimate(0, 0),
        name="permute",
    )(*lists, value)


def attention_kernel(heads, same_row, same_column, query, keys, values, attended, logsum):
    same = same_row[...] == same_column[...]
    q, k, v = query[...], keys[...], values[...]
    head = lax.broadcasted_iota(jnp.int32, q.shape, 1) // HD
    total_out = jnp.zeros(q.shape, f32)
    for h in range(heads):
        scores = dot(jnp.where(head == h, q, jnp.zeros_like(q)), k, ROWS_OF_BOTH)
        scores = jnp.where(same, scores, -1e30)
        peak = jnp.max(scores, axis=1, keepdims=True)
        expo = jnp.exp(scores - peak)
        total = jnp.sum(expo, axis=1, keepdims=True)
        total_out = jnp.where(head == h, dot(expo.astype(bf16), v) / total, total_out)
        logsum[:, h : h + 1] = peak + jnp.log(total)
    attended[...] = total_out.astype(bf16)


def attention(document, query, keys, values):
    rows, width = query.shape
    heads = width // HD
    block = rows // 2
    part = pl.BlockSpec((block, width), lambda i: (i, 0))
    whole = pl.BlockSpec((rows, width), lambda i: (0, 0))
    return pl.pallas_call(
        functools.partial(attention_kernel, heads),
        grid=(2,),
        in_specs=[
            pl.BlockSpec((block, 1), lambda i: (i, 0)),
            pl.BlockSpec((1, rows), lambda i: (0, 0)),
            part,
            whole,
            whole,
        ],
        out_specs=[part, pl.BlockSpec((block, heads), lambda i: (i, 0))],
        out_shape=[
            jax.ShapeDtypeStruct((rows, width), bf16),
            jax.ShapeDtypeStruct((rows, heads), f32),
        ],
        compiler_params=pltpu.CompilerParams(vmem_limit_bytes=32 << 20),
        cost_estimate=pl.CostEstimate(
            flops=4 * rows * rows * width * 4, bytes_accessed=8 * rows * width, transcendentals=0
        ),
        name="attention",
    )(document[:, None], document[None, :], query, keys, values)


def attention_back_kernel(
    count,
    same_row,
    same_column,
    query,
    keys,
    values,
    grad_attended,
    attended,
    logsum,
    grad_projected,
    sum_keys,
    sum_values,
):
    pair, at = pl.program_id(0), pl.program_id(1)
    same = same_row[...] == same_column[...]
    q, k, v, g = query[...], keys[...], values[...], grad_attended[...]
    rows, lanes = q.shape
    head = lax.broadcasted_iota(jnp.int32, q.shape, 1) // HD
    product = g.astype(f32) * attended[...].astype(f32)
    logs = logsum[...]
    lane = lax.broadcasted_iota(jnp.int32, logs.shape, 1)

    @pl.when(at == 0)
    def _():
        sum_keys[...] = jnp.zeros_like(sum_keys)
        sum_values[...] = jnp.zeros_like(sum_values)

    out = jnp.zeros(q.shape, f32)
    for h in range(lanes // HD):
        here = head == h
        q_head = jnp.where(here, q, jnp.zeros_like(q))
        g_head = jnp.where(here, g, jnp.zeros_like(g))
        log = jnp.sum(jnp.where(lane == pair * (lanes // HD) + h, logs, 0.0), 1, keepdims=True)
        scores = jnp.where(same, dot(q_head, k, ROWS_OF_BOTH), -1e30)
        probs = jnp.exp(scores - log)
        inner = jnp.sum(jnp.where(here, product, 0.0), axis=1, keepdims=True)
        grad_scores = probs * (dot(g_head, v, ROWS_OF_BOTH) - inner)
        grad_scores = grad_scores.astype(bf16)
        out = jnp.where(here, dot(grad_scores, k), out)
        sum_keys[...] += dot(grad_scores, q_head, COLUMNS_OF_BOTH)
        sum_values[...] += dot(probs.astype(bf16), g_head, COLUMNS_OF_BOTH)
    third = grad_projected.shape[1] // 3
    first = pl.multiple_of(at * rows, rows)
    grad_projected[pl.ds(first, rows), pl.ds(pl.multiple_of(pair * lanes, lanes), lanes)] = (
        out * (1.0 / math.sqrt(HD))
    ).astype(bf16)

    @pl.when(at == count - 1)
    def _():
        for which, total in ((1, sum_keys), (2, sum_values)):
            start = pl.multiple_of(which * third + pair * lanes, lanes)
            grad_projected[:, pl.ds(start, lanes)] = total[...].astype(bf16)


def attention_back(document, query, keys, values, grad_attended, attended, logsum):
    rows, width = query.shape
    heads = width // HD
    block, lanes = min(512, rows), 2 * HD
    part = pl.BlockSpec((block, lanes), lambda p, i: (i, p))
    whole = pl.BlockSpec((rows, lanes), lambda p, i: (0, p))
    return pl.pallas_call(
        functools.partial(attention_back_kernel, rows // block),
        grid=(width // lanes, rows // block),
        in_specs=[
            pl.BlockSpec((block, 1), lambda p, i: (i, 0)),
            pl.BlockSpec((1, rows), lambda p, i: (0, 0)),
            part,
            whole,
            whole,
            part,
            part,
            pl.BlockSpec((block, heads), lambda p, i: (i, 0)),
        ],
        out_specs=pl.BlockSpec((rows, 3 * width), lambda p, i: (0, 0)),
        out_shape=jax.ShapeDtypeStruct((rows, 3 * width), bf16),
        scratch_shapes=[pltpu.VMEM((rows, lanes), f32)] * 2,
        compiler_params=pltpu.CompilerParams(vmem_limit_bytes=32 << 20),
        cost_estimate=pl.CostEstimate(
            flops=10 * rows * rows * width * 4, bytes_accessed=16 * rows * width, transcendentals=0
        ),
        name="attention_back",
    )(document[:, None], document[None, :], query, keys, values, grad_attended, attended, logsum)


SMEM_SPEC = pl.BlockSpec(memory_space=pltpu.SMEM)
VMEM_SPEC = pl.BlockSpec(memory_space=pltpu.VMEM)


def scalars(values):
    return jnp.stack([jnp.int32(value) for value in values])


def vmem(shape, index=None):
    if index is None:
        return pl.BlockSpec(shape, lambda *_: (0,) * len(shape))
    return pl.BlockSpec(shape, index)


def estimate(flops, moved):
    return pl.CostEstimate(flops=flops, bytes_accessed=moved, transcendentals=0)


def finish_kernel(direct, docs, places, *refs):
    *arrived, target = refs
    rows = arrived[0].shape[0] - 8 * docs
    total = arrived[0][:rows].astype(f32)
    high = arrived[0][rows : rows + 4 * docs].astype(f32)
    low = arrived[0][rows + 4 * docs :].astype(f32)
    for ref in arrived[1:]:
        total += ref[:rows].astype(f32)
        high += ref[rows : rows + 4 * docs].astype(f32)
        low += ref[rows + 4 * docs :].astype(f32)
    target[:rows] = total.astype(bf16)
    mods = high + low
    if direct:
        lanes = mods.shape[1] // 2
        blocks = [
            mods[(a // 2) * docs : (a // 2 + 1) * docs, (a % 2) * lanes : (a % 2 + 1) * lanes]
            for a in range(8)
        ]
        ordered = []
        for p in range(8):
            block = jnp.zeros_like(blocks[0])
            for a in range(8):
                block = jnp.where(places[p] == a, blocks[a], block)
            ordered.append(block)
        mods = jnp.concatenate(
            [jnp.concatenate(ordered[2 * q : 2 * q + 2], axis=1) for q in range(4)], axis=0
        )
    first = mods.astype(bf16)
    target[rows:] = jnp.concatenate(
        [first, (mods - first.astype(f32)).astype(bf16)], axis=0
    )


def finish(direct, docs, places, arrived):
    return pl.pallas_call(
        functools.partial(finish_kernel, direct, docs),
        in_specs=[pl.BlockSpec(memory_space=pltpu.SMEM)]
        + [pl.BlockSpec(memory_space=pltpu.VMEM)] * len(arrived),
        out_specs=pl.BlockSpec(memory_space=pltpu.VMEM),
        out_shape=jax.ShapeDtypeStruct(arrived[0].shape, bf16),
        cost_estimate=estimate(0, 0),
        name="finish",
    )(jnp.stack([jnp.int32(p) for p in places]), *arrived)


def row_mods(document, folded, docs):
    lane = lax.broadcasted_iota(jnp.int32, (document.shape[0], 8 * docs), 1)
    return jnp.concatenate(
        [
            dot((lane % (4 * docs) == document + q * docs).astype(bf16), folded)
            for q in range(4)
        ],
        axis=1,
    )


def normal_of(value):
    centred = value - jnp.mean(value, axis=-1, keepdims=True)
    inverse = lax.rsqrt(jnp.mean(centred * centred, axis=-1, keepdims=True) + norm_eps)
    return centred * inverse, inverse


def front_kernel(docs, document, both, far, weight, project, scale, shift, *outs):
    hidden, query, keys, values, stream = outs
    at = pl.program_id(0)
    rows = hidden.shape[0]
    embed = jnp.where(at < 2, both[0, :rows], far[0, :rows])
    value = dot(embed, weight[...])

    @pl.when(at < 2)
    def _():
        stream[...] = value

    normal, _ = normal_of(value)
    which = document[...]
    scaled = normal * (1.0 + row_mods(which, scale[...], docs)) + row_mods(which, shift[...], docs)
    low = scaled.astype(bf16)
    hidden[...] = low
    projected = dot(low, project[...]).astype(bf16)
    third = projected.shape[1] // 3
    query[...] = projected[:, :third] * jnp.asarray(1.0 / math.sqrt(HD), bf16)
    keys[...] = projected[:, third : 2 * third]
    values[...] = projected[:, 2 * third :]


def front(docs, document, both, far, weight, project, scale, shift):
    emb, width = weight.shape
    rows = document.shape[0]
    quarter = rows // 4
    third = project.shape[1] // 3
    message = both.shape[1]
    part = vmem((quarter, third), lambda i: (i, 0))
    return pl.pallas_call(
        functools.partial(front_kernel, docs),
        grid=(4,),
        in_specs=[
            vmem((quarter, 1), lambda i: (i, 0)),
            vmem((1, message, emb), lambda i: (jnp.minimum(i, 1), 0, 0)),
            vmem((1, message, emb), lambda i: (jnp.maximum(i - 2, 0), 0, 0)),
            vmem(weight.shape),
            vmem(project.shape),
            vmem(scale.shape),
            vmem(shift.shape),
        ],
        out_specs=[
            vmem((quarter, width), lambda i: (i, 0)),
            part,
            part,
            part,
            vmem((quarter, width), lambda i: (jnp.minimum(i, 1), 0)),
        ],
        out_shape=[jax.ShapeDtypeStruct((rows, width), bf16)]
        + [jax.ShapeDtypeStruct((rows, third), bf16)] * 3
        + [jax.ShapeDtypeStruct((rows // 2, width), f32)],
        compiler_params=pltpu.CompilerParams(vmem_limit_bytes=32 << 20),
        cost_estimate=estimate(2 * rows * width * (emb + 3 * third), 8 * rows * width),
        name="front",
    )(document, both, far, weight, project, scale, shift)


def pack_first_kernel(spots, project, weight, output, target, small):
    depth, columns = project.shape
    third = columns // 3
    for head in range(third // HD):
        for which in range(3):
            target[:, which * third + head * HD : which * third + (head + 1) * HD] = project[
                :, (3 * head + which) * HD : (3 * head + which + 1) * HD
            ]
    emb = weight.shape[0]
    for q in range(depth // emb):
        start = spots[0] * (weight.shape[1] // 2) + q * depth
        small[q * emb : (q + 1) * emb, :depth] = weight[
            :, pl.ds(pl.multiple_of(start, depth), depth)
        ]
    for j in range(2):
        small[:, (1 + j) * depth : (2 + j) * depth] = output[j * depth : (j + 1) * depth]


def pack_first(spots, project, weight, output):
    depth, columns = project.shape
    return pl.pallas_call(
        pack_first_kernel,
        in_specs=[SMEM_SPEC] + [VMEM_SPEC] * 3,
        out_specs=[VMEM_SPEC] * 2,
        out_shape=[
            jax.ShapeDtypeStruct((depth, columns), bf16),
            jax.ShapeDtypeStruct((depth, 3 * depth), bf16),
        ],
        name="pack_first",
    )(spots, project, weight, output)


def pack_second_kernel(up, down, target):
    per = up.shape[0]
    target[:per] = up[...]
    target[per:] = down[...].T


def pack_second(up, down):
    per, units = up.shape
    return pl.pallas_call(
        pack_second_kernel,
        in_specs=[VMEM_SPEC] * 2,
        out_specs=VMEM_SPEC,
        out_shape=jax.ShapeDtypeStruct((2 * per, units), bf16),
        name="pack_second",
    )(up, down)


def unpack_kernel(places, gathered, near, far, project, output, weight):
    depth = project.shape[0] // 8
    emb = weight.shape[0] // 8
    for p in range(8):
        rows = slice(p * depth, (p + 1) * depth)
        project[rows] = gathered[places[p]]
        source, begin = (near, far)[p // 4], p % 4 * depth
        for j in range(2):
            output[j * depth : (j + 1) * depth, rows] = source[
                begin : begin + depth, (1 + j) * depth : (2 + j) * depth
            ]
        first = pl.multiple_of(places[p] * emb, emb)
        for q in range(depth // emb):
            weight[pl.ds(first, emb), q * depth : (q + 1) * depth] = source[
                begin + q * emb : begin + (q + 1) * emb, :depth
            ]


def unpack(places, gathered, near, far, emb):
    count, depth, columns = gathered.shape
    return pl.pallas_call(
        unpack_kernel,
        in_specs=[SMEM_SPEC] + [VMEM_SPEC] * 3,
        out_specs=[VMEM_SPEC] * 3,
        out_shape=[
            jax.ShapeDtypeStruct((count * depth, columns), bf16),
            jax.ShapeDtypeStruct((2 * depth, count * depth), bf16),
            jax.ShapeDtypeStruct((emb, depth * depth // (emb // count)), bf16),
        ],
        compiler_params=pltpu.CompilerParams(vmem_limit_bytes=32 << 20),
        cost_estimate=estimate(0, 0),
        name="unpack",
    )(places, gathered, near, far)


def spread_kernel(places, gathered, up, down):
    per = up.shape[0] // 8
    for p in range(8):
        up[p * per : (p + 1) * per] = gathered[places[p], :per]
        down[p * per : (p + 1) * per] = gathered[places[p], per:]


def spread(places, gathered):
    width = gathered.shape[2]
    return pl.pallas_call(
        spread_kernel,
        in_specs=[SMEM_SPEC, VMEM_SPEC],
        out_specs=[VMEM_SPEC] * 2,
        out_shape=[jax.ShapeDtypeStruct((width, width), bf16)] * 2,
        compiler_params=pltpu.CompilerParams(vmem_limit_bytes=32 << 20),
        cost_estimate=estimate(0, 0),
        name="spread",
    )(places, gathered)


def weight_grads_kernel(
    places, hidden, hidden_far, grad, grad_far, cotangent, active, active_far, target
):
    at = pl.program_id(0)
    half = hidden.shape[0]
    per = target.shape[1] // 2
    up = dot(hidden[...], grad[...], COLUMNS_OF_BOTH)
    up += dot(hidden_far[...], grad_far[...], COLUMNS_OF_BOTH)
    down = dot(cotangent[:half], active[...], COLUMNS_OF_BOTH)
    down += dot(cotangent[half:], active_far[...], COLUMNS_OF_BOTH)
    for j in range(2):
        place = places[2 * at + j]
        target[place, :per] = up[j * per : (j + 1) * per].astype(bf16)
        target[place, per:] = down[j * per : (j + 1) * per].astype(bf16)


def weight_grads(places, hidden, grad, cotangent, active):
    half, width = hidden[0].shape
    units = grad[0].shape[1]
    per = width // len(ORDER)
    tall = vmem((half, 2 * per), lambda i: (0, i))
    whole = vmem((half, units))
    return pl.pallas_call(
        weight_grads_kernel,
        grid=(len(ORDER) // 2,),
        in_specs=[
            SMEM_SPEC,
            tall,
            tall,
            whole,
            whole,
            vmem((2 * half, 2 * per), lambda i: (0, i)),
            whole,
            whole,
        ],
        out_specs=vmem((len(ORDER), 2 * per, units)),
        out_shape=jax.ShapeDtypeStruct((len(ORDER), 2 * per, units), bf16),
        compiler_params=pltpu.CompilerParams(vmem_limit_bytes=40 << 20),
        cost_estimate=estimate(0, 0),
        name="weight_grads",
    )(places, *hidden, *grad, cotangent, *active)


def second_norm_kernel(docs, document, stream_zero, mine, other, scale, shift, stream, hidden):
    value = stream_zero[...] + (mine[...].astype(f32) + other[...].astype(f32))
    stream[...] = value
    normal, _ = normal_of(value)
    which = document[...]
    hidden[...] = (
        normal * (1.0 + row_mods(which, scale[...], docs)) + row_mods(which, shift[...], docs)
    ).astype(bf16)


def second_norm(docs, document, stream_zero, mine, other, scale, shift):
    half, width = mine.shape
    block = half // 2
    part = vmem((block, width), lambda i: (i, 0))
    return pl.pallas_call(
        functools.partial(second_norm_kernel, docs),
        grid=(2,),
        in_specs=[
            vmem((block, 1), lambda i: (i, 0)),
            part,
            part,
            part,
            vmem(scale.shape),
            vmem(shift.shape),
        ],
        out_specs=[part, part],
        out_shape=[
            jax.ShapeDtypeStruct((half, width), f32),
            jax.ShapeDtypeStruct((half, width), bf16),
        ],
        compiler_params=pltpu.CompilerParams(vmem_limit_bytes=32 << 20),
        cost_estimate=estimate(2 * half * width * 128, 12 * half * width),
        name="second_norm",
    )(document, stream_zero, mine, other, scale, shift)


def add_up(target, value):
    @pl.when(pl.program_id(0) == 0)
    def _():
        target[...] = value

    @pl.when(pl.program_id(0) > 0)
    def _():
        target[...] += value


def back_through_norm(docs, grad, value, which, scale):
    normal, inverse = normal_of(value)
    inner = grad * (1.0 + row_mods(which, scale, docs))
    back = inverse * (
        inner
        - jnp.mean(inner, axis=-1, keepdims=True)
        - normal * jnp.mean(inner * normal, axis=-1, keepdims=True)
    )
    lane = lax.broadcasted_iota(jnp.int32, (which.shape[0], 8), 1)
    member = (lane == which).astype(bf16)
    by_scale = dot(member, (grad * normal).astype(bf16), COLUMNS_OF_BOTH)
    by_shift = dot(member, grad.astype(bf16), COLUMNS_OF_BOTH)
    return back, by_scale, by_shift


def second_back_kernel(
    docs, document, stream, mine, other, scale, cotangent, stream_grad, low, by_scale, by_shift
):
    grad = mine[...].astype(f32) + other[...].astype(f32)
    back, for_scale, for_shift = back_through_norm(
        docs, grad, stream[...], document[...], scale[...]
    )
    add_up(by_scale, for_scale)
    add_up(by_shift, for_shift)
    total = cotangent[...].astype(f32) + back
    stream_grad[...] = total
    low[...] = total.astype(bf16)


def second_back(docs, document, stream, mine, other, scale, cotangent):
    half, width = mine.shape
    block = half // 2
    part = vmem((block, width), lambda i: (i, 0))
    sums = vmem((8, width))
    return pl.pallas_call(
        functools.partial(second_back_kernel, docs),
        grid=(2,),
        in_specs=[
            vmem((block, 1), lambda i: (i, 0)),
            part,
            part,
            part,
            vmem(scale.shape),
            part,
        ],
        out_specs=[part, part, sums, sums],
        out_shape=[
            jax.ShapeDtypeStruct((half, width), f32),
            jax.ShapeDtypeStruct((half, width), bf16),
            jax.ShapeDtypeStruct((8, width), f32),
            jax.ShapeDtypeStruct((8, width), f32),
        ],
        compiler_params=pltpu.CompilerParams(vmem_limit_bytes=32 << 20),
        cost_estimate=estimate(2 * half * width * 128, 16 * half * width),
        name="second_back",
    )(document, stream, mine, other, scale, cotangent)


def first_back_kernel(
    docs, flag, document, both, far, weight, project, grad_projected, scale, above, own, other,
    grad_weight, by_scale, by_shift,
):
    at = pl.program_id(0)
    rows = grad_projected.shape[0]
    embed = jnp.where(at < 2, both[0, :rows], far[0, :rows])
    value = dot(embed, weight[...])
    grad = dot(grad_projected[...], project[...], ROWS_OF_BOTH)
    back, for_scale, for_shift = back_through_norm(docs, grad, value, document[...], scale[...])
    add_up(by_scale, for_scale)
    add_up(by_shift, for_shift)
    counts = jnp.where(at < 2, flag[0], 0).astype(f32)
    low = (back + counts * above[...]).astype(bf16)
    grad_embed = dot(low, weight[...], ROWS_OF_BOTH)

    @pl.when(at < 2)
    def _():
        own[...] = grad_embed

    @pl.when(at >= 2)
    def _():
        other[...] = grad_embed.astype(bf16)

    add_up(grad_weight, dot(embed, low, COLUMNS_OF_BOTH))


def first_back(docs, flag, document, both, far, weight, project, grad_projected, scale, above):
    emb, width = weight.shape
    rows = document.shape[0]
    quarter = rows // 4
    message = both.shape[1]
    sums = vmem((8, width))
    early = lambda i: (jnp.minimum(i, 1), 0)
    late = lambda i: (jnp.maximum(i - 2, 0), 0)
    return pl.pallas_call(
        functools.partial(first_back_kernel, docs),
        grid=(4,),
        in_specs=[
            SMEM_SPEC,
            vmem((quarter, 1), lambda i: (i, 0)),
            vmem((1, message, emb), lambda i: (jnp.minimum(i, 1), 0, 0)),
            vmem((1, message, emb), lambda i: (jnp.maximum(i - 2, 0), 0, 0)),
            vmem(weight.shape),
            vmem(project.shape),
            vmem((quarter, project.shape[1]), lambda i: (i, 0)),
            vmem(scale.shape),
            vmem((quarter, width), early),
        ],
        out_specs=[
            vmem((quarter, emb), early),
            vmem((quarter, emb), late),
            vmem((emb, width)),
            sums,
            sums,
        ],
        out_shape=[
            jax.ShapeDtypeStruct((rows // 2, emb), f32),
            jax.ShapeDtypeStruct((rows // 2, emb), bf16),
            jax.ShapeDtypeStruct((emb, width), f32),
            jax.ShapeDtypeStruct((8, width), f32),
            jax.ShapeDtypeStruct((8, width), f32),
        ],
        compiler_params=pltpu.CompilerParams(vmem_limit_bytes=32 << 20),
        cost_estimate=estimate(2 * rows * width * (3 * emb + project.shape[1]), 16 * rows * width),
        name="first_back",
    )(flag, document, both, far, weight, project, grad_projected, scale, above)


def local_sums_kernel(spots, weight, *refs):
    mods, (far_embed, own, other) = refs[:4], refs[4:]
    emb = weight.shape[0]
    per = weight.shape[1] // 8
    share = emb + 32
    flag = spots[9].astype(f32)
    for target, core in ((own, spots[8]), (other, 1 - spots[8])):
        for x in range(2):
            column = 2 * x + core
            base = x * share
            for j in range(2):
                start = pl.multiple_of(spots[column * 2 + j] * per, per)
                target[base : base + emb, j * per : (j + 1) * per] = weight[
                    :, pl.ds(start, per)
                ].astype(target.dtype)
            for q in range(4):
                halves = []
                for j in range(2):
                    start = pl.multiple_of(spots[2 * q + j] * per, per)
                    total = mods[2 * x][:, pl.ds(start, per)]
                    total = jnp.where(core == 0, total, mods[2 * x + 1][:, pl.ds(start, per)])
                    halves.append(total if x == 0 else total * flag)
                block = jnp.concatenate(halves, axis=1)
                target[base + emb + q * 8 : base + emb + (q + 1) * 8] = block.astype(target.dtype)
    other[2 * share :] = far_embed[...]


def local_sums(spots, weight, mods, far_embed):
    emb = weight.shape[0]
    rows = 2 * (emb + 32)
    return pl.pallas_call(
        local_sums_kernel,
        in_specs=[SMEM_SPEC] + [VMEM_SPEC] * 6,
        out_specs=[VMEM_SPEC] * 2,
        out_shape=[
            jax.ShapeDtypeStruct((rows, emb), f32),
            jax.ShapeDtypeStruct((rows + far_embed.shape[0], emb), bf16),
        ],
        compiler_params=pltpu.CompilerParams(vmem_limit_bytes=32 << 20),
        cost_estimate=estimate(0, 0),
        name="local_sums",
    )(spots, weight, *mods, far_embed)


def chip_sums_kernel(spots, own, received, own_embed, keep, send):
    share = own.shape[0] // 2
    quarter = own_embed.shape[0] // 2
    for target, x in ((keep, spots[0]), (send, 1 - spots[0])):
        start = pl.multiple_of(x * share, share)
        total = own[pl.ds(start, share)] + received[pl.ds(start, share)].astype(f32)
        target[:share] = total.astype(target.dtype)
        rows = pl.multiple_of(x * quarter, quarter)
        far = received[pl.ds(pl.multiple_of(2 * share + rows, 64), quarter)]
        total = own_embed[pl.ds(rows, quarter)] + far.astype(f32)
        target[share:] = total.astype(target.dtype)


def chip_sums(spots, own, received, own_embed):
    emb = own.shape[1]
    rows = own.shape[0] // 2 + own_embed.shape[0] // 2
    return pl.pallas_call(
        chip_sums_kernel,
        in_specs=[SMEM_SPEC] + [VMEM_SPEC] * 3,
        out_specs=[VMEM_SPEC] * 2,
        out_shape=[
            jax.ShapeDtypeStruct((rows, emb), f32),
            jax.ShapeDtypeStruct((rows, emb), bf16),
        ],
        cost_estimate=estimate(0, 0),
        name="chip_sums",
    )(spots, own, received, own_embed)


def outgoing_kernel(spots, own, other, *refs):
    *messages, low = refs
    emb = own.shape[1]
    total = (own[...] + other[...].astype(f32)).astype(bf16)
    low[...] = total[:emb]
    piece = emb // 8
    mods = total[emb : emb + 32]
    rows = total.shape[0] - emb - 32
    base = rows + 32
    for k, message in enumerate(messages):
        message[:rows] = total[emb + 32 :]
        message[rows:base] = mods
        for j in range(2):
            start = pl.multiple_of(spots[2 * k + j] * piece, piece)
            message[base + j * piece : base + (j + 1) * piece] = low[pl.ds(start, piece)]


def outgoing(spots, own, other):
    emb = own.shape[1]
    rows = own.shape[0] - emb + 2 * (emb // 8)
    return pl.pallas_call(
        outgoing_kernel,
        in_specs=[SMEM_SPEC] + [VMEM_SPEC] * 2,
        out_specs=[VMEM_SPEC] * 4,
        out_shape=[jax.ShapeDtypeStruct((rows, emb), bf16)] * 4,
        scratch_shapes=[pltpu.VMEM((emb, emb), bf16)],
        cost_estimate=estimate(0, 0),
        name="outgoing",
    )(spots, own, other)


def relay_kernel(share, piece, *refs):
    *arrived, message, keep = refs
    for k, ref in enumerate(arrived):
        message[k * share : (k + 1) * share] = ref[:share]
    for j, target in ((0, keep), (1, message)):
        begin = share + j * piece
        total = sum(ref[begin : begin + piece].astype(f32) for ref in arrived)
        if j:
            message[4 * share :] = total.astype(bf16)
        else:
            keep[...] = total


def relay(share, piece, arrived):
    emb = arrived[0].shape[1]
    return pl.pallas_call(
        functools.partial(relay_kernel, share, piece),
        in_specs=[VMEM_SPEC] * 4,
        out_specs=[VMEM_SPEC] * 2,
        out_shape=[
            jax.ShapeDtypeStruct((4 * share + piece, emb), bf16),
            jax.ShapeDtypeStruct((piece, emb), f32),
        ],
        cost_estimate=estimate(0, 0),
        name="relay",
    )(*arrived)


def landed_kernel(share, rows, features, near, far, keep, small):
    width = small.shape[1] - keep.shape[1]
    total = jnp.zeros((features.shape[1], width), f32)
    for k in range(8):
        source, begin = (near, far)[k // 4], k % 4 * share + rows
        mods = jnp.concatenate(
            [source[begin + q * 8 : begin + q * 8 + 8] for q in range(4)], axis=1
        )
        total += dot(features[k * 8 : (k + 1) * 8], mods, COLUMNS_OF_BOTH)
    small[:, :width] = total
    small[:, width:] = keep[...] + far[4 * share :].astype(f32)


def landed(docs, share, rows, width, features, near, far, keep):
    return pl.pallas_call(
        functools.partial(landed_kernel, share, rows),
        in_specs=[VMEM_SPEC] * 4,
        out_specs=VMEM_SPEC,
        out_shape=jax.ShapeDtypeStruct((features.shape[1], width + keep.shape[1]), f32),
        cost_estimate=estimate(0, 0),
        name="landed",
    )(features, near, far, keep)


def per_device(
    token_ids,
    lengths,
    time_steps,
    embed_table,
    input_weight,
    time_weight,
    project_weight,
    output_weight,
    up_weight,
    down_weight,
    cotangent,
):
    rows = token_ids.shape[0]
    half, quarter = rows // 2, rows // 4
    count = lax.axis_size("dp")
    groups = lax.axis_size("tensor")
    me = lax.axis_index("dp")
    place = lax.axis_index("tensor")
    x, c = place // 2, place % 2
    width = cotangent.shape[1]
    docs = lengths.shape[0]
    shard = embed_table.shape[0]
    emb_rows = input_weight.shape[0]
    head_width = project_weight.shape[1]
    heads = head_width // (3 * HD)
    third = heads * HD
    per = width // count
    dp = Direct(count)

    my_ids = lax.dynamic_slice_in_dim(token_ids, (c * 2 + x) * quarter, quarter)
    heard = jnp.concatenate([my_ids, time_steps])[None]
    table = embed_table.astype(f32)
    rscale = lax.rsqrt(jnp.mean(table * table, axis=1, keepdims=True) + table_eps)
    normed = (table * rscale).astype(bf16)
    crossed = swap_x(normed)
    heard = jnp.concatenate([heard, dp.swap(after(heard, normed), 4)], axis=0)

    packed, small = pack_first(scalars([c]), project_weight, input_weight, output_weight)
    packed = lax.all_gather(packed, "dp")
    small_z2 = dp.swap(small, 4)
    gathered = lax.all_gather(pack_second(up_weight, down_weight), "dp")
    heard = jnp.concatenate([heard, dp.swap(heard, 2)], axis=0)
    heard = jnp.concatenate([heard, dp.swap(heard, 1)], axis=0)

    pair = jnp.concatenate([normed, crossed], axis=0)
    shards = jnp.concatenate([pair, swap_core(pair)], axis=0)
    entry = jnp.arange(4 * shard, dtype=jnp.int32)
    which = entry // shard
    owner = (x ^ (which & 1)) * 2 + (c ^ (which >> 1))
    vocab = (me * groups + owner) * shard + entry % shard

    feature = me * emb_rows + jnp.arange(emb_rows, dtype=jnp.int32)
    part = EMB // 2
    frequency = jnp.exp(-math.log(10000.0) * (feature % part).astype(f32) / part)
    angles = heard[:, quarter:].astype(f32)[:, :, None] * frequency[None, None, :]
    features = jnp.where(feature[None, None, :] < part, jnp.sin(angles), jnp.cos(angles))
    features = features.astype(bf16)
    time_part = lax.dynamic_slice_in_dim(time_weight, place * width, width, 1)
    found_mods = dot(features.reshape(count * docs, emb_rows), time_part)
    found_mods = found_mods.reshape(count, docs, 4, EMB).transpose(0, 2, 1, 3)
    found_mods = jnp.concatenate(split_two(found_mods.reshape(count, 4 * docs, EMB)), axis=1)

    def look_up(begin, end):
        names = heard[begin:end, :quarter].reshape(-1)
        onehot = (names[:, None] == vocab[None, :]).astype(bf16)
        found = dot(onehot, shards).astype(bf16).reshape(end - begin, quarter, EMB)
        return jnp.concatenate([found, found_mods[begin:end]], axis=1)

    looked_up = look_up(4, 8)
    crossed = dp.swap(looked_up, 1)
    small = jnp.concatenate([small, after(small_z2, looked_up)], axis=0)
    small_z1 = dp.swap(small, 2)
    near = look_up(0, 4)
    crossed, small_z1 = join(crossed, small_z1)
    near = near.astype(f32) + crossed.astype(f32)
    mods = near[:, quarter : quarter + 4 * docs] + near[:, quarter + 4 * docs :]
    near = jnp.concatenate([near[:, :quarter].astype(bf16), *split_two(mods)], axis=1)

    small = jnp.concatenate([small, small_z1], axis=0)
    small_far = dp.swap(small, 1)
    arrived = [near[0]] + [dp.swap(near[k], ORDER[k]) for k in (1, 2, 3)]
    arrived[3], small_far = join(arrived[3], small_far)
    mine = finish(True, docs, dp.places, arrived)
    project, output, input_half = unpack(
        scalars(dp.places), after(packed, mine), small, small_far, EMB
    )
    input_other = swap_core(input_half)
    input_full = jnp.concatenate(
        [jnp.where(c == 0, input_half, input_other), jnp.where(c == 0, input_other, input_half)],
        axis=1,
    )
    input_full = permute(input_full, [0], dp.places)
    other = swap_x(mine)
    both = jnp.stack([jnp.where(x == 0, mine, other), jnp.where(x == 0, other, mine)])
    far = swap_core(both)
    own_mods, far_mods = both[:, quarter:], far[:, quarter:]
    scale_one, scale_two = jnp.where(c == 0, own_mods, far_mods)
    shift_one, shift_two = jnp.where(c == 0, far_mods, own_mods)

    position = jnp.arange(rows, dtype=jnp.int32) ^ (c * half)
    ends = jnp.cumsum(lengths)
    document = jnp.sum((position[:, None] >= ends[None, :]).astype(jnp.int32), axis=1)
    column = document[:, None]
    cot = permute(after(cotangent, heard), [c, 1 - c], dp.places)

    hidden_one, query, keys, values, stream_zero = front(
        docs, column, both, far, input_full, project, scale_one, shift_one
    )

    def reduce_core(own, far, weight, dims=((1,), (0,))):
        sent = swap_core(dot(far, weight, dims).astype(bf16))
        return (dot(own, weight, dims) + sent.astype(f32)).astype(bf16)

    def over_rows(left, right):
        return dot(left[0], right[0], COLUMNS_OF_BOTH) + dot(left[1], right[1], COLUMNS_OF_BOTH)

    attended, logsum = attention(document, query, keys, values)
    attention_sum = reduce_core(attended[:half], attended[half:], output)
    crossed = swap_x(attention_sum)
    crossed, cot = join(crossed, cot)
    up, down = spread(scalars(dp.places), after(gathered, attention_sum))
    stream_one, hidden = second_norm(
        docs, column, stream_zero, attention_sum, crossed, scale_two, shift_two
    )
    hidden_two = (hidden, swap_core(hidden))
    cot_two = (cot[:half], cot[half:])
    activated, grad_upward = [], []
    for at in range(2):
        upward = dot(hidden_two[at], up)
        phi = 0.5 * (1.0 + lax.erf(upward * math.sqrt(0.5)))
        activated.append((upward * phi).astype(bf16))
        slope = phi + upward * (math.sqrt(0.5 / math.pi) * jnp.exp(-0.5 * upward * upward))
        grad_active = dot(cot_two[at], down)
        grad_upward.append((grad_active * slope).astype(bf16))
    grad_two = reduce_core(*grad_upward, up, ROWS_OF_BOTH)
    crossed = swap_x(grad_two)
    bundled = weight_grads(
        scalars(dp.places), hidden_two, [after(part, grad_two) for part in grad_upward], cot, activated
    )
    reduced = lax.psum_scatter(bundled, "dp", scatter_dimension=0, tiled=False)
    crossed, bundled = join(crossed, bundled)
    grad_one, low, *by_two = second_back(
        docs, column, stream_one, grad_two, crossed, scale_two, cot
    )
    grad_attn = (low, swap_core(low))
    grad_attended = jnp.concatenate(
        [dot(part, output, ROWS_OF_BOTH).astype(bf16) for part in grad_attn], axis=0
    )
    grad_projected = attention_back(
        document, query, keys, values, grad_attended, attended, logsum
    )
    flag = jnp.where(x == 0, 1, 0)
    own_embed, far_embed, grad_input, *by_one = first_back(
        docs,
        scalars([flag]),
        column,
        both,
        far,
        input_full,
        project,
        grad_projected,
        scale_one,
        grad_one,
    )
    share = quarter + 32
    own_sums, far_sums = local_sums(
        scalars(dp.inverse + [c, flag]), grad_input, [*by_one, *by_two], far_embed
    )
    received = swap_core(far_sums)
    keep, send = chip_sums(scalars([x]), own_sums, received, own_embed)
    crossed = swap_x(send)
    grad_project = dot(hidden_one, after(grad_projected, send), COLUMNS_OF_BOTH)
    grad_output = over_rows((attended[:half], attended[half:]), grad_attn)
    grad_output = jnp.concatenate(
        [unfold(grad_output[:, k * per : (k + 1) * per], 2) for k in range(count)], axis=0
    )
    grad_packed = jnp.concatenate([grad_project, grad_output], axis=1).astype(bf16)
    branch_sum = reduce_core(*[after(part, send) for part in activated], down, ROWS_OF_BOTH)
    crossed, grad_packed, branch_sum = join(crossed, grad_packed, branch_sum)
    packed_first = dp.swap(grad_packed[width // 2 :], 1)
    branch_crossed = swap_x(after(branch_sum, crossed))
    messages = outgoing(scalars([me ^ v ^ j for v in ORDER[:4] for j in range(2)]), keep, crossed)
    arrived = [messages[0]] + [dp.swap(messages[k], ORDER[k]) for k in (1, 2, 3)]
    arrived[3], packed_first, reduced = join(arrived[3], packed_first, reduced)
    near, keep = relay(share, emb_rows, arrived)
    far = dp.swap(near, 1)
    packed_first = after(packed_first, near)
    branch_crossed = after(branch_crossed, near)
    packed_sum = grad_packed[: width // 2].astype(f32) + packed_first.astype(f32)
    packed_second = dp.swap(packed_sum[2 * per :].astype(bf16), 2)

    names = jnp.pad(heard[:, :quarter], ((0, 0), (0, share - quarter)), constant_values=-1)
    near_ids, far_ids = names[:4].reshape(-1), names[4:].reshape(-1)
    near_ids, far_ids = (
        jnp.pad(part, (0, emb_rows), constant_values=-1) for part in (near_ids, far_ids)
    )

    def table_part(first, last, tokens, names):
        onehot = (vocab[first * shard : last * shard, None] == names[None, :]).astype(bf16)
        return dot(onehot, tokens)

    near_low = table_part(0, 4, near, near_ids).astype(bf16)
    block = branch_sum.astype(f32) + branch_crossed.astype(f32)
    block = (stream_one + block).astype(bf16)
    block_out = jnp.concatenate([block, swap_core(block)], axis=0)
    block_out = permute(block_out, [c, 1 - c], dp.inverse)
    far, packed_second, block_out, near_low = join(far, packed_second, block_out, near_low)
    theirs = near_low[2 * shard :] + table_part(2, 4, far, far_ids)
    theirs = swap_core(theirs.astype(bf16)).astype(f32)
    sent = near_low[shard : 2 * shard] + table_part(1, 2, far, far_ids)
    sent_low = (sent + theirs[shard:]).astype(bf16)
    sent = swap_x(sent_low)
    kept = near_low[:shard] + table_part(0, 1, far, far_ids) + theirs[:shard]

    features = jnp.pad(features, ((0, 0), (0, 8 - docs), (0, 0))).reshape(8 * count, emb_rows)
    small = landed(docs, share, quarter, width, features, near, far, after(keep, sent_low))
    packed_sum = packed_sum[: 2 * per] + after(packed_second, sent_low).astype(f32)
    packed_third = dp.swap(packed_sum[per:].astype(bf16), 4)
    other = swap_x(small)

    reduced = reduced.astype(f32)
    summed_up, summed_down = reduced[:per], reduced[per:].T
    summed_packed = packed_sum[:per] + after(packed_third, kept).astype(f32)
    summed_project = summed_packed[:, :head_width]
    summed_output = fold(summed_packed[:, head_width:], per)
    summed_project = (
        summed_project.reshape(per, 3, heads, HD).transpose(0, 2, 1, 3).reshape(per, head_width)
    )
    sent, kept, summed_up, summed_down = join(sent, kept, summed_up, summed_down)
    other = after(other, sent)
    both = jnp.stack([jnp.where(x == 0, small, other), jnp.where(x == 0, other, small)])
    far = swap_core(both)
    pieces = []
    for at in range(2):
        pieces += [jnp.where(c == 0, both[at], far[at]), jnp.where(c == 0, far[at], both[at])]
    summed_time = jnp.concatenate([piece[:, :width] for piece in pieces], axis=1)
    summed_input = jnp.concatenate([piece[:, width:] for piece in pieces], axis=1)
    grad_normed = kept + sent.astype(f32)
    grad_table = rscale * grad_normed - table * (
        rscale * rscale * rscale * jnp.mean(grad_normed * table, axis=1, keepdims=True)
    )
    return (
        block_out,
        grad_table,
        summed_input,
        summed_time,
        summed_project,
        summed_output,
        summed_up,
        summed_down,
    )


def normalize(table_rows):
    return table_rows * lax.rsqrt(
        jnp.mean(table_rows * table_rows, axis=1, keepdims=True) + table_eps
    )


def layer_norm(value, scale, shift):
    centred = value - jnp.mean(value, axis=-1, keepdims=True)
    return (
        centred
        * lax.rsqrt(jnp.mean(centred * centred, axis=-1, keepdims=True) + norm_eps)
        * (1.0 + scale)
        + shift
    )


def time_features(step_index, width):
    half = width // 2
    frequency = jnp.exp(-math.log(10000.0) * jnp.arange(half).astype(jnp.float32) / half)
    angles = step_index.astype(jnp.float32)[:, None] * frequency[None, :]
    return jnp.concatenate([jnp.sin(angles), jnp.cos(angles)], axis=1)


def gelu_exact(value):
    return jax.nn.gelu(value, approximate=False)


def whole_collectives(
    token_ids,
    lengths,
    time_steps,
    embed_table,
    input_weight,
    time_weight,
    project_weight,
    output_weight,
    up_weight,
    down_weight,
    cotangent,
):
    rows = token_ids.shape[0]
    groups = lax.axis_size("tensor")
    tensor_place = lax.axis_index("tensor")
    shard_rows = embed_table.shape[0]
    factor = 1.0 / math.sqrt(HD)
    normed, normed_back = jax.vjp(normalize, embed_table.astype(jnp.float32))
    normed_low = normed.astype(jnp.bfloat16)
    gathered = (
        lax.all_gather(input_weight, "dp", axis=0, tiled=True),
        lax.all_gather(time_weight, "dp", axis=0, tiled=True),
        lax.all_gather(project_weight, "dp", axis=0, tiled=True),
        lax.all_gather(output_weight, "dp", axis=1, tiled=True),
        lax.all_gather(up_weight, "dp", axis=0, tiled=True),
        lax.all_gather(down_weight, "dp", axis=1, tiled=True),
    )
    input_full, time_full, project_full, output_full, up_full, down_full = gathered

    def vocab_rows(count):
        flat_index = jnp.arange(count, dtype=jnp.int32)
        return (
            flat_index // shard_rows * groups + tensor_place
        ) * shard_rows + flat_index % shard_rows

    token_block = min(256, rows)
    piece = lax.all_gather(normed_low, "dp", axis=0, tiled=True)
    vocab = vocab_rows(piece.shape[0])
    parts = []
    for add_begin in range(0, rows, token_block):
        add_onehot = (
            token_ids[add_begin : add_begin + token_block, None] == vocab[None, :]
        ).astype(jnp.bfloat16)
        parts.append(jnp.dot(add_onehot, piece, preferred_element_type=jnp.float32))
    partial_embed = jnp.concatenate(parts, axis=0)
    embed = lax.psum(partial_embed.astype(jnp.bfloat16), "tensor")
    stream_zero = jnp.dot(embed, input_full, preferred_element_type=jnp.float32)
    ends = jnp.cumsum(lengths)
    position = jnp.arange(rows, dtype=jnp.int32)
    document = jnp.sum((position[:, None] >= ends[None, :]).astype(jnp.int32), axis=1)
    member = (document[:, None] == jnp.arange(lengths.shape[0], dtype=jnp.int32)[None, :]).astype(
        jnp.float32
    )
    features = time_features(time_steps, EMB).astype(jnp.bfloat16)
    modulation = jnp.dot(features, time_full, preferred_element_type=jnp.float32)
    row_mods = jnp.dot(member, modulation, precision=highest)
    scale_one, shift_one, scale_two, shift_two = jnp.split(row_mods, 4, axis=1)
    normed_one, norm_one_back = jax.vjp(layer_norm, stream_zero, scale_one, shift_one)
    hidden_one = normed_one.astype(jnp.bfloat16)
    projected = jnp.dot(hidden_one, project_full, preferred_element_type=jnp.float32).astype(
        jnp.bfloat16
    )
    heads_here = projected.shape[1] // (3 * HD)
    projected = projected.reshape(rows, heads_here, 3, HD)
    query = jnp.transpose(projected[:, :, 0], (1, 0, 2))
    keys = jnp.transpose(projected[:, :, 1], (1, 0, 2))
    values = jnp.transpose(projected[:, :, 2], (1, 0, 2))
    query_block = min(512, rows)

    def scores_of(begin):
        block_query = query[:, begin : begin + query_block]
        plain = (
            jnp.einsum("hqd,hkd->hqk", block_query, keys, preferred_element_type=jnp.float32)
            * factor
        )
        allowed = document[begin : begin + query_block, None] == document[None, :]
        return (jnp.where(allowed[None], plain, masked_score), block_query)

    outputs = []
    logsums = []
    kept_probs = []
    for begin in range(0, rows, query_block):
        scores, block_query = scores_of(begin)
        peak = jnp.max(scores, axis=2, keepdims=True)
        expo = jnp.exp(scores - peak)
        total = jnp.sum(expo, axis=2, keepdims=True)
        logsums.append(peak + jnp.log(total))
        probs_low = (expo / total).astype(jnp.bfloat16)
        kept_probs.append(probs_low)
        outputs.append(
            jnp.einsum("hqk,hkd->hqd", probs_low, values, preferred_element_type=jnp.float32)
        )
    attended = (
        jnp.transpose(jnp.concatenate(outputs, axis=1), (1, 0, 2))
        .reshape(rows, heads_here * HD)
        .astype(jnp.bfloat16)
    )
    attention_sum = lax.psum(
        jnp.dot(attended, output_full, preferred_element_type=jnp.float32), "tensor"
    )
    stream_one_rows = stream_zero + attention_sum
    normed_two, norm_two_back = jax.vjp(layer_norm, stream_one_rows, scale_two, shift_two)
    hidden_two = normed_two.astype(jnp.bfloat16)
    upward = jnp.dot(hidden_two, up_full, preferred_element_type=jnp.float32)
    activated, gelu_back = jax.vjp(gelu_exact, upward)
    activated_low = activated.astype(jnp.bfloat16)
    branch = lax.psum(
        jnp.dot(activated_low, down_full, preferred_element_type=jnp.float32), "tensor"
    )
    block_out = (stream_one_rows + branch).astype(jnp.bfloat16)
    grad_down = jnp.dot(activated_low.T, cotangent, preferred_element_type=jnp.float32)
    grad_active = jnp.dot(cotangent, down_full.T, preferred_element_type=jnp.float32)
    grad_upward = gelu_back(grad_active)[0].astype(jnp.bfloat16)
    grad_up = jnp.dot(hidden_two.T, grad_upward, preferred_element_type=jnp.float32)
    grad_hidden_two = lax.psum(
        jnp.dot(grad_upward, up_full.T, preferred_element_type=jnp.float32), "tensor"
    )
    grad_stream_rows, grad_scale_two, grad_shift_two = norm_two_back(grad_hidden_two)
    grad_stream_rows = grad_stream_rows + cotangent.astype(jnp.float32)
    grad_attn_rows = grad_stream_rows.astype(jnp.bfloat16)
    grad_output = jnp.dot(attended.T, grad_attn_rows, preferred_element_type=jnp.float32)
    grad_attended = jnp.dot(
        grad_attn_rows, output_full.T, preferred_element_type=jnp.float32
    ).astype(jnp.bfloat16)
    grad_attended = jnp.transpose(grad_attended.reshape(rows, heads_here, HD), (1, 0, 2))
    query_grads = []
    grad_keys = jnp.zeros(keys.shape, jnp.float32)
    grad_values = jnp.zeros(values.shape, jnp.float32)
    for number, begin in enumerate(range(0, rows, query_block)):
        scores, block_query = scores_of(begin)
        probs = jnp.exp(scores - logsums[number])
        block_grad = grad_attended[:, begin : begin + query_block]
        grad_probs = jnp.einsum(
            "hqd,hkd->hqk", block_grad, values, preferred_element_type=jnp.float32
        )
        inner = jnp.sum(probs * grad_probs, axis=2, keepdims=True)
        grad_scores = (probs * (grad_probs - inner)).astype(jnp.bfloat16)
        query_grads.append(
            jnp.einsum("hqk,hkd->hqd", grad_scores, keys, preferred_element_type=jnp.float32)
            * factor
        )
        grad_keys = (
            grad_keys
            + jnp.einsum(
                "hqk,hqd->hkd", grad_scores, block_query, preferred_element_type=jnp.float32
            )
            * factor
        )
        grad_values = grad_values + jnp.einsum(
            "hqk,hqd->hkd", kept_probs[number], block_grad, preferred_element_type=jnp.float32
        )
    grad_query = jnp.concatenate(query_grads, axis=1)
    grad_projected = jnp.stack([grad_query, grad_keys, grad_values], axis=2)
    grad_projected = (
        jnp.transpose(grad_projected, (1, 0, 2, 3))
        .reshape(rows, heads_here * 3 * HD)
        .astype(jnp.bfloat16)
    )
    grad_project = jnp.dot(hidden_one.T, grad_projected, preferred_element_type=jnp.float32)
    grad_hidden_one = lax.psum(
        jnp.dot(grad_projected, project_full.T, preferred_element_type=jnp.float32), "tensor"
    )
    grad_stream_zero, grad_scale_one, grad_shift_one = norm_one_back(grad_hidden_one)
    grad_zero_low = (grad_stream_zero + grad_stream_rows).astype(jnp.bfloat16)
    grad_rows = jnp.concatenate(
        [grad_scale_one, grad_shift_one, grad_scale_two, grad_shift_two], axis=1
    )
    partial_modulation = jnp.dot(member.T, grad_rows, precision=highest)
    grad_stream_zero = grad_zero_low
    grad_input = jnp.dot(embed.T, grad_stream_zero, preferred_element_type=jnp.float32)
    grad_embed = jnp.dot(grad_stream_zero, input_full.T, preferred_element_type=jnp.float32).astype(
        jnp.bfloat16
    )
    grad_time = jnp.dot(features.astype(jnp.float32).T, partial_modulation, precision=highest)
    every_row = shard_rows * lax.axis_size("dp")
    vocab_all = vocab_rows(every_row)
    grad_normed = jnp.zeros((every_row, EMB), jnp.float32)
    for begin in range(0, rows, token_block):
        onehot = (token_ids[begin : begin + token_block, None] == vocab_all[None, :]).astype(
            jnp.bfloat16
        )
        grad_normed = grad_normed + jnp.einsum(
            "tv,te->ve",
            onehot,
            grad_embed[begin : begin + token_block],
            preferred_element_type=jnp.float32,
        )
    (
        summed_input,
        summed_time,
        summed_project,
        summed_output,
        summed_up,
        summed_down,
        summed_table,
    ) = (
        lax.psum_scatter(grad_input, "dp", scatter_dimension=0, tiled=True),
        lax.psum_scatter(grad_time, "dp", scatter_dimension=0, tiled=True),
        lax.psum_scatter(grad_project, "dp", scatter_dimension=0, tiled=True),
        lax.psum_scatter(grad_output, "dp", scatter_dimension=1, tiled=True),
        lax.psum_scatter(grad_up, "dp", scatter_dimension=0, tiled=True),
        lax.psum_scatter(grad_down, "dp", scatter_dimension=1, tiled=True),
        lax.psum_scatter(grad_normed, "dp", scatter_dimension=0, tiled=True),
    )
    grad_table = normed_back(summed_table)[0]
    return (
        block_out,
        grad_table,
        summed_input,
        summed_time,
        summed_project,
        summed_output,
        summed_up,
        summed_down,
    )


def solution(mesh):
    count, groups = mesh.shape["dp"], mesh.shape["tensor"]
    return jax.shard_map(
        per_device if count == len(ORDER) and groups == 4 else whole_collectives,
        mesh=mesh,
        in_specs=(
            P("dp"),
            P("dp"),
            P("dp"),
            P(("dp", "tensor"), None),
            P("dp", None),
            P("dp", None),
            P("dp", "tensor"),
            P("tensor", "dp"),
            P("dp", "tensor"),
            P("tensor", "dp"),
            P("dp", None),
        ),
        out_specs=(
            P("dp", None),
            P(("dp", "tensor"), None),
            P("dp", None),
            P("dp", None),
            P("dp", "tensor"),
            P("tensor", "dp"),
            P("dp", "tensor"),
            P("tensor", "dp"),
        ),
        check_vma=False,
    )
```

```python
import functools
import math

import jax
import jax.numpy as jnp
from jax import lax
from jax.experimental import pallas as pl
from jax.experimental.pallas import tpu as pltpu
from jax.sharding import PartitionSpec as P

HD = 64
EMB = 256

table_eps = 1e-06
norm_eps = 1e-05
masked_score = -1e30
highest = lax.Precision.HIGHEST
bf16 = jnp.bfloat16
f32 = jnp.float32


def dot(left, right, dims=((1,), (0,))):
    return lax.dot_general(left, right, (dims, ((), ())), preferred_element_type=f32)


def join(*values):
    return lax.optimization_barrier(values)


def after(value, *others):
    return lax.optimization_barrier((value,) + others)[0]


SWAP_CORE = [(0, 1), (1, 0), (2, 3), (3, 2)]
SWAP_X = [(0, 2), (2, 0), (1, 3), (3, 1)]


def swap_core(value):
    return lax.ppermute(value, "tensor", SWAP_CORE)


def swap_x(value):
    return lax.ppermute(value, "tensor", SWAP_X)


ROWS_OF_BOTH = ((1,), (1,))
COLUMNS_OF_BOTH = ((0,), (0,))
ORDER = (0, 4, 2, 6, 1, 5, 3, 7)


class Direct:
    def __init__(self, count):
        self.count = count
        self.me = lax.axis_index("dp")
        self.places = [self.me ^ v for v in ORDER]
        self.inverse = [
            sum(jnp.where(self.places[k] == a, k, 0) for k in range(count)) for a in range(count)
        ]

    def swap(self, value, v):
        return lax.ppermute(value, "dp", [(i, i ^ v) for i in range(self.count)])

    def spread_small(self, value):
        value = value[None]
        for v in (4, 2, 1):
            value = jnp.concatenate([value, self.swap(value, v)], axis=0)
        return value


def picked(value, places, axis):
    size = value.shape[axis] // len(ORDER)
    return jnp.concatenate(
        [lax.slice_in_dim(value, p * size, (p + 1) * size, axis=axis) for p in places], axis=axis
    )


def split_two(value):
    high = value.astype(bf16)
    return high, (value - high.astype(f32)).astype(bf16)


def fold(value, width):
    return jnp.concatenate(jnp.split(value, value.shape[1] // width, axis=1), axis=0)


def unfold(value, count):
    return jnp.concatenate(jnp.split(value, count, axis=0), axis=1)


def permute_kernel(row_places, column_places, source, target):
    rows = source.shape[0] // row_places.shape[0]
    columns = source.shape[1] // column_places.shape[0]
    for i in range(row_places.shape[0]):
        for j in range(column_places.shape[0]):
            first = pl.multiple_of(row_places[i] * rows, rows)
            second = pl.multiple_of(column_places[j] * columns, columns)
            target[i * rows : (i + 1) * rows, j * columns : (j + 1) * columns] = source[
                pl.ds(first, rows), pl.ds(second, columns)
            ]


def permute(value, row_places, column_places):
    lists = [jnp.stack([jnp.int32(p) for p in places]) for places in (row_places, column_places)]
    return pl.pallas_call(
        permute_kernel,
        out_shape=jax.ShapeDtypeStruct(value.shape, value.dtype),
        in_specs=[pl.BlockSpec(memory_space=pltpu.SMEM)] * 2
        + [pl.BlockSpec(memory_space=pltpu.VMEM)],
        out_specs=pl.BlockSpec(memory_space=pltpu.VMEM),
        compiler_params=pltpu.CompilerParams(vmem_limit_bytes=32 << 20),
        cost_estimate=estimate(0, 0),
        name="permute",
    )(*lists, value)


def attention_kernel(heads, same_row, same_column, query, keys, values, attended, logsum):
    same = same_row[...] == same_column[...]
    q, k, v = query[...], keys[...], values[...]
    head = lax.broadcasted_iota(jnp.int32, q.shape, 1) // HD
    total_out = jnp.zeros(q.shape, f32)
    for h in range(heads):
        scores = dot(jnp.where(head == h, q, jnp.zeros_like(q)), k, ROWS_OF_BOTH)
        scores = jnp.where(same, scores, -1e30)
        peak = jnp.max(scores, axis=1, keepdims=True)
        expo = jnp.exp(scores - peak)
        total = jnp.sum(expo, axis=1, keepdims=True)
        total_out = jnp.where(head == h, dot(expo.astype(bf16), v) / total, total_out)
        logsum[:, h : h + 1] = peak + jnp.log(total)
    attended[...] = total_out.astype(bf16)


def attention(document, query, keys, values):
    rows, width = query.shape
    heads = width // HD
    block = rows // 2
    part = pl.BlockSpec((block, width), lambda i: (i, 0))
    whole = pl.BlockSpec((rows, width), lambda i: (0, 0))
    return pl.pallas_call(
        functools.partial(attention_kernel, heads),
        grid=(2,),
        in_specs=[
            pl.BlockSpec((block, 1), lambda i: (i, 0)),
            pl.BlockSpec((1, rows), lambda i: (0, 0)),
            part,
            whole,
            whole,
        ],
        out_specs=[part, pl.BlockSpec((block, heads), lambda i: (i, 0))],
        out_shape=[
            jax.ShapeDtypeStruct((rows, width), bf16),
            jax.ShapeDtypeStruct((rows, heads), f32),
        ],
        compiler_params=pltpu.CompilerParams(vmem_limit_bytes=32 << 20),
        cost_estimate=pl.CostEstimate(
            flops=4 * rows * rows * width * 4, bytes_accessed=8 * rows * width, transcendentals=0
        ),
        name="attention",
    )(document[:, None], document[None, :], query, keys, values)


def attention_back_kernel(
    count,
    same_row,
    same_column,
    query,
    keys,
    values,
    grad_attended,
    attended,
    logsum,
    grad_projected,
    sum_keys,
    sum_values,
):
    pair, at = pl.program_id(0), pl.program_id(1)
    same = same_row[...] == same_column[...]
    q, k, v, g = query[...], keys[...], values[...], grad_attended[...]
    rows, lanes = q.shape
    head = lax.broadcasted_iota(jnp.int32, q.shape, 1) // HD
    product = g.astype(f32) * attended[...].astype(f32)
    logs = logsum[...]
    lane = lax.broadcasted_iota(jnp.int32, logs.shape, 1)

    @pl.when(at == 0)
    def _():
        sum_keys[...] = jnp.zeros_like(sum_keys)
        sum_values[...] = jnp.zeros_like(sum_values)

    out = jnp.zeros(q.shape, f32)
    for h in range(lanes // HD):
        here = head == h
        q_head = jnp.where(here, q, jnp.zeros_like(q))
        g_head = jnp.where(here, g, jnp.zeros_like(g))
        log = jnp.sum(jnp.where(lane == pair * (lanes // HD) + h, logs, 0.0), 1, keepdims=True)
        scores = jnp.where(same, dot(q_head, k, ROWS_OF_BOTH), -1e30)
        probs = jnp.exp(scores - log)
        inner = jnp.sum(jnp.where(here, product, 0.0), axis=1, keepdims=True)
        grad_scores = probs * (dot(g_head, v, ROWS_OF_BOTH) - inner)
        grad_scores = grad_scores.astype(bf16)
        out = jnp.where(here, dot(grad_scores, k), out)
        sum_keys[...] += dot(grad_scores, q_head, COLUMNS_OF_BOTH)
        sum_values[...] += dot(probs.astype(bf16), g_head, COLUMNS_OF_BOTH)
    third = grad_projected.shape[1] // 3
    first = pl.multiple_of(at * rows, rows)
    grad_projected[pl.ds(first, rows), pl.ds(pl.multiple_of(pair * lanes, lanes), lanes)] = (
        out * (1.0 / math.sqrt(HD))
    ).astype(bf16)

    @pl.when(at == count - 1)
    def _():
        for which, total in ((1, sum_keys), (2, sum_values)):
            start = pl.multiple_of(which * third + pair * lanes, lanes)
            grad_projected[:, pl.ds(start, lanes)] = total[...].astype(bf16)


def attention_back(document, query, keys, values, grad_attended, attended, logsum):
    rows, width = query.shape
    heads = width // HD
    block, lanes = min(512, rows), 2 * HD
    part = pl.BlockSpec((block, lanes), lambda p, i: (i, p))
    whole = pl.BlockSpec((rows, lanes), lambda p, i: (0, p))
    return pl.pallas_call(
        functools.partial(attention_back_kernel, rows // block),
        grid=(width // lanes, rows // block),
        in_specs=[
            pl.BlockSpec((block, 1), lambda p, i: (i, 0)),
            pl.BlockSpec((1, rows), lambda p, i: (0, 0)),
            part,
            whole,
            whole,
            part,
            part,
            pl.BlockSpec((block, heads), lambda p, i: (i, 0)),
        ],
        out_specs=pl.BlockSpec((rows, 3 * width), lambda p, i: (0, 0)),
        out_shape=jax.ShapeDtypeStruct((rows, 3 * width), bf16),
        scratch_shapes=[pltpu.VMEM((rows, lanes), f32)] * 2,
        compiler_params=pltpu.CompilerParams(vmem_limit_bytes=32 << 20),
        cost_estimate=pl.CostEstimate(
            flops=60 * rows * rows * width, bytes_accessed=16 * rows * width, transcendentals=0
        ),
        name="attention_back",
    )(document[:, None], document[None, :], query, keys, values, grad_attended, attended, logsum)


SMEM_SPEC = pl.BlockSpec(memory_space=pltpu.SMEM)
VMEM_SPEC = pl.BlockSpec(memory_space=pltpu.VMEM)


def scalars(values):
    return jnp.stack([jnp.int32(value) for value in values])


def vmem(shape, index=None):
    if index is None:
        return pl.BlockSpec(shape, lambda *_: (0,) * len(shape))
    return pl.BlockSpec(shape, index)


def estimate(flops, moved):
    return pl.CostEstimate(flops=flops, bytes_accessed=moved, transcendentals=0)


def finish_kernel(direct, docs, places, *refs):
    *arrived, target = refs
    rows = arrived[0].shape[0] - 8 * docs
    total = arrived[0][:rows].astype(f32)
    high = arrived[0][rows : rows + 4 * docs].astype(f32)
    low = arrived[0][rows + 4 * docs :].astype(f32)
    for ref in arrived[1:]:
        total += ref[:rows].astype(f32)
        high += ref[rows : rows + 4 * docs].astype(f32)
        low += ref[rows + 4 * docs :].astype(f32)
    target[:rows] = total.astype(bf16)
    mods = high + low
    if direct:
        lanes = mods.shape[1] // 2
        blocks = [
            mods[(a // 2) * docs : (a // 2 + 1) * docs, (a % 2) * lanes : (a % 2 + 1) * lanes]
            for a in range(8)
        ]
        ordered = []
        for p in range(8):
            block = jnp.zeros_like(blocks[0])
            for a in range(8):
                block = jnp.where(places[p] == a, blocks[a], block)
            ordered.append(block)
        mods = jnp.concatenate(
            [jnp.concatenate(ordered[2 * q : 2 * q + 2], axis=1) for q in range(4)], axis=0
        )
    first = mods.astype(bf16)
    target[rows:] = jnp.concatenate(
        [first, (mods - first.astype(f32)).astype(bf16)], axis=0
    )


def finish(direct, docs, places, arrived):
    return pl.pallas_call(
        functools.partial(finish_kernel, direct, docs),
        in_specs=[pl.BlockSpec(memory_space=pltpu.SMEM)]
        + [pl.BlockSpec(memory_space=pltpu.VMEM)] * len(arrived),
        out_specs=pl.BlockSpec(memory_space=pltpu.VMEM),
        out_shape=jax.ShapeDtypeStruct(arrived[0].shape, bf16),
        cost_estimate=estimate(0, 0),
        name="finish",
    )(jnp.stack([jnp.int32(p) for p in places]), *arrived)


def row_mods(document, folded, docs):
    lane = lax.broadcasted_iota(jnp.int32, (document.shape[0], 8 * docs), 1)
    return jnp.concatenate(
        [
            dot((lane % (4 * docs) == document + q * docs).astype(bf16), folded)
            for q in range(4)
        ],
        axis=1,
    )


def normal_of(value):
    centred = value - jnp.mean(value, axis=-1, keepdims=True)
    inverse = lax.rsqrt(jnp.mean(centred * centred, axis=-1, keepdims=True) + norm_eps)
    return centred * inverse, inverse


def front_kernel(docs, document, both, far, weight, project, scale, shift, *outs):
    hidden, query, keys, values, stream = outs
    at = pl.program_id(0)
    rows = hidden.shape[0]
    embed = jnp.where(at < 2, both[0, :rows], far[0, :rows])
    value = dot(embed, weight[...])

    @pl.when(at < 2)
    def _():
        stream[...] = value

    normal, _ = normal_of(value)
    which = document[...]
    scaled = normal * (1.0 + row_mods(which, scale[...], docs)) + row_mods(which, shift[...], docs)
    low = scaled.astype(bf16)
    hidden[...] = low
    projected = dot(low, project[...]).astype(bf16)
    third = projected.shape[1] // 3
    query[...] = projected[:, :third] * jnp.asarray(1.0 / math.sqrt(HD), bf16)
    keys[...] = projected[:, third : 2 * third]
    values[...] = projected[:, 2 * third :]


def front(docs, document, both, far, weight, project, scale, shift):
    emb, width = weight.shape
    rows = document.shape[0]
    quarter = rows // 4
    third = project.shape[1] // 3
    message = both.shape[1]
    part = vmem((quarter, third), lambda i: (i, 0))
    return pl.pallas_call(
        functools.partial(front_kernel, docs),
        grid=(4,),
        in_specs=[
            vmem((quarter, 1), lambda i: (i, 0)),
            vmem((1, message, emb), lambda i: (jnp.minimum(i, 1), 0, 0)),
            vmem((1, message, emb), lambda i: (jnp.maximum(i - 2, 0), 0, 0)),
            vmem(weight.shape),
            vmem(project.shape),
            vmem(scale.shape),
            vmem(shift.shape),
        ],
        out_specs=[
            vmem((quarter, width), lambda i: (i, 0)),
            part,
            part,
            part,
            vmem((quarter, width), lambda i: (jnp.minimum(i, 1), 0)),
        ],
        out_shape=[jax.ShapeDtypeStruct((rows, width), bf16)]
        + [jax.ShapeDtypeStruct((rows, third), bf16)] * 3
        + [jax.ShapeDtypeStruct((rows // 2, width), f32)],
        compiler_params=pltpu.CompilerParams(vmem_limit_bytes=32 << 20),
        cost_estimate=estimate(2 * rows * width * (emb + 3 * third), 8 * rows * width),
        name="front",
    )(document, both, far, weight, project, scale, shift)


def pack_first_kernel(spots, project, weight, output, target, small):
    depth, columns = project.shape
    third = columns // 3
    for head in range(third // HD):
        for which in range(3):
            target[:, which * third + head * HD : which * third + (head + 1) * HD] = project[
                :, (3 * head + which) * HD : (3 * head + which + 1) * HD
            ]
    emb = weight.shape[0]
    for q in range(depth // emb):
        start = spots[0] * (weight.shape[1] // 2) + q * depth
        small[q * emb : (q + 1) * emb, :depth] = weight[
            :, pl.ds(pl.multiple_of(start, depth), depth)
        ]
    for j in range(2):
        small[:, (1 + j) * depth : (2 + j) * depth] = output[j * depth : (j + 1) * depth]


def pack_first(spots, project, weight, output):
    depth, columns = project.shape
    return pl.pallas_call(
        pack_first_kernel,
        in_specs=[SMEM_SPEC] + [VMEM_SPEC] * 3,
        out_specs=[VMEM_SPEC] * 2,
        out_shape=[
            jax.ShapeDtypeStruct((depth, columns), bf16),
            jax.ShapeDtypeStruct((depth, 3 * depth), bf16),
        ],
        name="pack_first",
    )(spots, project, weight, output)


def pack_second_kernel(up, down, target):
    per = up.shape[0]
    target[:per] = up[...]
    target[per:] = down[...].T


def pack_second(up, down):
    per, units = up.shape
    return pl.pallas_call(
        pack_second_kernel,
        in_specs=[VMEM_SPEC] * 2,
        out_specs=VMEM_SPEC,
        out_shape=jax.ShapeDtypeStruct((2 * per, units), bf16),
        name="pack_second",
    )(up, down)


def unpack_kernel(places, gathered, near, far, project, output, weight):
    depth = project.shape[0] // 8
    emb = weight.shape[0] // 8
    for p in range(8):
        rows = slice(p * depth, (p + 1) * depth)
        project[rows] = gathered[places[p]]
        source, begin = (near, far)[p // 4], p % 4 * depth
        for j in range(2):
            output[j * depth : (j + 1) * depth, rows] = source[
                begin : begin + depth, (1 + j) * depth : (2 + j) * depth
            ]
        first = pl.multiple_of(places[p] * emb, emb)
        for q in range(depth // emb):
            weight[pl.ds(first, emb), q * depth : (q + 1) * depth] = source[
                begin + q * emb : begin + (q + 1) * emb, :depth
            ]


def unpack(places, gathered, near, far, emb):
    count, depth, columns = gathered.shape
    return pl.pallas_call(
        unpack_kernel,
        in_specs=[SMEM_SPEC] + [VMEM_SPEC] * 3,
        out_specs=[VMEM_SPEC] * 3,
        out_shape=[
            jax.ShapeDtypeStruct((count * depth, columns), bf16),
            jax.ShapeDtypeStruct((2 * depth, count * depth), bf16),
            jax.ShapeDtypeStruct((emb, depth * depth // (emb // count)), bf16),
        ],
        compiler_params=pltpu.CompilerParams(vmem_limit_bytes=32 << 20),
        cost_estimate=estimate(0, 0),
        name="unpack",
    )(places, gathered, near, far)


def spread_kernel(places, gathered, up, down):
    per = up.shape[0] // 8
    for p in range(8):
        up[p * per : (p + 1) * per] = gathered[places[p], :per]
        down[p * per : (p + 1) * per] = gathered[places[p], per:]


def spread(places, gathered):
    width = gathered.shape[2]
    return pl.pallas_call(
        spread_kernel,
        in_specs=[SMEM_SPEC, VMEM_SPEC],
        out_specs=[VMEM_SPEC] * 2,
        out_shape=[jax.ShapeDtypeStruct((width, width), bf16)] * 2,
        compiler_params=pltpu.CompilerParams(vmem_limit_bytes=32 << 20),
        cost_estimate=estimate(0, 0),
        name="spread",
    )(places, gathered)


def weight_grads_kernel(
    places, hidden, hidden_far, grad, grad_far, cotangent, active, active_far, target
):
    at = pl.program_id(0)
    half = hidden.shape[0]
    per = target.shape[1] // 2
    up = dot(hidden[...], grad[...], COLUMNS_OF_BOTH)
    up += dot(hidden_far[...], grad_far[...], COLUMNS_OF_BOTH)
    down = dot(cotangent[:half], active[...], COLUMNS_OF_BOTH)
    down += dot(cotangent[half:], active_far[...], COLUMNS_OF_BOTH)
    for j in range(2):
        place = places[2 * at + j]
        target[place, :per] = up[j * per : (j + 1) * per].astype(bf16)
        target[place, per:] = down[j * per : (j + 1) * per].astype(bf16)


def weight_grads(places, hidden, grad, cotangent, active):
    half, width = hidden[0].shape
    units = grad[0].shape[1]
    per = width // len(ORDER)
    tall = vmem((half, 2 * per), lambda i: (0, i))
    whole = vmem((half, units))
    return pl.pallas_call(
        weight_grads_kernel,
        grid=(len(ORDER) // 2,),
        in_specs=[
            SMEM_SPEC,
            tall,
            tall,
            whole,
            whole,
            vmem((2 * half, 2 * per), lambda i: (0, i)),
            whole,
            whole,
        ],
        out_specs=vmem((len(ORDER), 2 * per, units)),
        out_shape=jax.ShapeDtypeStruct((len(ORDER), 2 * per, units), bf16),
        compiler_params=pltpu.CompilerParams(vmem_limit_bytes=40 << 20),
        cost_estimate=estimate(0, 0),
        name="weight_grads",
    )(places, *hidden, *grad, cotangent, *active)


def second_norm_kernel(docs, document, stream_zero, mine, other, scale, shift, stream, hidden):
    value = stream_zero[...] + (mine[...].astype(f32) + other[...].astype(f32))
    stream[...] = value
    normal, _ = normal_of(value)
    which = document[...]
    hidden[...] = (
        normal * (1.0 + row_mods(which, scale[...], docs)) + row_mods(which, shift[...], docs)
    ).astype(bf16)


def second_norm(docs, document, stream_zero, mine, other, scale, shift):
    half, width = mine.shape
    block = half // 2
    part = vmem((block, width), lambda i: (i, 0))
    return pl.pallas_call(
        functools.partial(second_norm_kernel, docs),
        grid=(2,),
        in_specs=[
            vmem((block, 1), lambda i: (i, 0)),
            part,
            part,
            part,
            vmem(scale.shape),
            vmem(shift.shape),
        ],
        out_specs=[part, part],
        out_shape=[
            jax.ShapeDtypeStruct((half, width), f32),
            jax.ShapeDtypeStruct((half, width), bf16),
        ],
        compiler_params=pltpu.CompilerParams(vmem_limit_bytes=32 << 20),
        cost_estimate=estimate(2 * half * width * 128, 12 * half * width),
        name="second_norm",
    )(document, stream_zero, mine, other, scale, shift)


def add_up(target, value):
    @pl.when(pl.program_id(0) == 0)
    def _():
        target[...] = value

    @pl.when(pl.program_id(0) > 0)
    def _():
        target[...] += value


def back_through_norm(docs, grad, value, which, scale):
    normal, inverse = normal_of(value)
    inner = grad * (1.0 + row_mods(which, scale, docs))
    back = inverse * (
        inner
        - jnp.mean(inner, axis=-1, keepdims=True)
        - normal * jnp.mean(inner * normal, axis=-1, keepdims=True)
    )
    lane = lax.broadcasted_iota(jnp.int32, (which.shape[0], 8), 1)
    member = (lane == which).astype(bf16)
    by_scale = dot(member, (grad * normal).astype(bf16), COLUMNS_OF_BOTH)
    by_shift = dot(member, grad.astype(bf16), COLUMNS_OF_BOTH)
    return back, by_scale, by_shift


def second_back_kernel(
    docs, document, stream, mine, other, scale, cotangent, stream_grad, low, by_scale, by_shift
):
    grad = mine[...].astype(f32) + other[...].astype(f32)
    back, for_scale, for_shift = back_through_norm(
        docs, grad, stream[...], document[...], scale[...]
    )
    add_up(by_scale, for_scale)
    add_up(by_shift, for_shift)
    total = cotangent[...].astype(f32) + back
    stream_grad[...] = total
    low[...] = total.astype(bf16)


def second_back(docs, document, stream, mine, other, scale, cotangent):
    half, width = mine.shape
    block = half // 2
    part = vmem((block, width), lambda i: (i, 0))
    sums = vmem((8, width))
    return pl.pallas_call(
        functools.partial(second_back_kernel, docs),
        grid=(2,),
        in_specs=[
            vmem((block, 1), lambda i: (i, 0)),
            part,
            part,
            part,
            vmem(scale.shape),
            part,
        ],
        out_specs=[part, part, sums, sums],
        out_shape=[
            jax.ShapeDtypeStruct((half, width), f32),
            jax.ShapeDtypeStruct((half, width), bf16),
            jax.ShapeDtypeStruct((8, width), f32),
            jax.ShapeDtypeStruct((8, width), f32),
        ],
        compiler_params=pltpu.CompilerParams(vmem_limit_bytes=32 << 20),
        cost_estimate=estimate(2 * half * width * 128, 16 * half * width),
        name="second_back",
    )(document, stream, mine, other, scale, cotangent)


def first_back_kernel(
    docs, flag, document, both, far, weight, project, grad_projected, scale, above, own, other,
    grad_weight, by_scale, by_shift,
):
    at = pl.program_id(0)
    rows = grad_projected.shape[0]
    embed = jnp.where(at < 2, both[0, :rows], far[0, :rows])
    value = dot(embed, weight[...])
    grad = dot(grad_projected[...], project[...], ROWS_OF_BOTH)
    back, for_scale, for_shift = back_through_norm(docs, grad, value, document[...], scale[...])
    add_up(by_scale, for_scale)
    add_up(by_shift, for_shift)
    counts = jnp.where(at < 2, flag[0], 0).astype(f32)
    low = (back + counts * above[...]).astype(bf16)
    grad_embed = dot(low, weight[...], ROWS_OF_BOTH)

    @pl.when(at < 2)
    def _():
        own[...] = grad_embed

    @pl.when(at >= 2)
    def _():
        other[...] = grad_embed.astype(bf16)

    add_up(grad_weight, dot(embed, low, COLUMNS_OF_BOTH))


def first_back(docs, flag, document, both, far, weight, project, grad_projected, scale, above):
    emb, width = weight.shape
    rows = document.shape[0]
    quarter = rows // 4
    message = both.shape[1]
    sums = vmem((8, width))
    early = lambda i: (jnp.minimum(i, 1), 0)
    late = lambda i: (jnp.maximum(i - 2, 0), 0)
    return pl.pallas_call(
        functools.partial(first_back_kernel, docs),
        grid=(4,),
        in_specs=[
            SMEM_SPEC,
            vmem((quarter, 1), lambda i: (i, 0)),
            vmem((1, message, emb), lambda i: (jnp.minimum(i, 1), 0, 0)),
            vmem((1, message, emb), lambda i: (jnp.maximum(i - 2, 0), 0, 0)),
            vmem(weight.shape),
            vmem(project.shape),
            vmem((quarter, project.shape[1]), lambda i: (i, 0)),
            vmem(scale.shape),
            vmem((quarter, width), early),
        ],
        out_specs=[
            vmem((quarter, emb), early),
            vmem((quarter, emb), late),
            vmem((emb, width)),
            sums,
            sums,
        ],
        out_shape=[
            jax.ShapeDtypeStruct((rows // 2, emb), f32),
            jax.ShapeDtypeStruct((rows // 2, emb), bf16),
            jax.ShapeDtypeStruct((emb, width), f32),
            jax.ShapeDtypeStruct((8, width), f32),
            jax.ShapeDtypeStruct((8, width), f32),
        ],
        compiler_params=pltpu.CompilerParams(vmem_limit_bytes=32 << 20),
        cost_estimate=estimate(2 * rows * width * (3 * emb + project.shape[1]), 16 * rows * width),
        name="first_back",
    )(flag, document, both, far, weight, project, grad_projected, scale, above)


def local_sums_kernel(spots, weight, *refs):
    mods, (far_embed, own, other) = refs[:4], refs[4:]
    emb = weight.shape[0]
    per = weight.shape[1] // 8
    share = emb + 32
    flag = spots[9].astype(f32)
    for target, core in ((own, spots[8]), (other, 1 - spots[8])):
        for x in range(2):
            column = 2 * x + core
            base = x * share
            for j in range(2):
                start = pl.multiple_of(spots[column * 2 + j] * per, per)
                target[base : base + emb, j * per : (j + 1) * per] = weight[
                    :, pl.ds(start, per)
                ].astype(target.dtype)
            for q in range(4):
                halves = []
                for j in range(2):
                    start = pl.multiple_of(spots[2 * q + j] * per, per)
                    total = mods[2 * x][:, pl.ds(start, per)]
                    total = jnp.where(core == 0, total, mods[2 * x + 1][:, pl.ds(start, per)])
                    halves.append(total if x == 0 else total * flag)
                block = jnp.concatenate(halves, axis=1)
                target[base + emb + q * 8 : base + emb + (q + 1) * 8] = block.astype(target.dtype)
    other[2 * share :] = far_embed[...]


def local_sums(spots, weight, mods, far_embed):
    emb = weight.shape[0]
    rows = 2 * (emb + 32)
    return pl.pallas_call(
        local_sums_kernel,
        in_specs=[SMEM_SPEC] + [VMEM_SPEC] * 6,
        out_specs=[VMEM_SPEC] * 2,
        out_shape=[
            jax.ShapeDtypeStruct((rows, emb), f32),
            jax.ShapeDtypeStruct((rows + far_embed.shape[0], emb), bf16),
        ],
        compiler_params=pltpu.CompilerParams(vmem_limit_bytes=32 << 20),
        cost_estimate=estimate(0, 0),
        name="local_sums",
    )(spots, weight, *mods, far_embed)


def chip_sums_kernel(spots, own, received, own_embed, keep, send):
    share = own.shape[0] // 2
    quarter = own_embed.shape[0] // 2
    for target, x in ((keep, spots[0]), (send, 1 - spots[0])):
        start = pl.multiple_of(x * share, share)
        total = own[pl.ds(start, share)] + received[pl.ds(start, share)].astype(f32)
        target[:share] = total.astype(target.dtype)
        rows = pl.multiple_of(x * quarter, quarter)
        far = received[pl.ds(pl.multiple_of(2 * share + rows, 64), quarter)]
        total = own_embed[pl.ds(rows, quarter)] + far.astype(f32)
        target[share:] = total.astype(target.dtype)


def chip_sums(spots, own, received, own_embed):
    emb = own.shape[1]
    rows = own.shape[0] // 2 + own_embed.shape[0] // 2
    return pl.pallas_call(
        chip_sums_kernel,
        in_specs=[SMEM_SPEC] + [VMEM_SPEC] * 3,
        out_specs=[VMEM_SPEC] * 2,
        out_shape=[
            jax.ShapeDtypeStruct((rows, emb), f32),
            jax.ShapeDtypeStruct((rows, emb), bf16),
        ],
        cost_estimate=estimate(0, 0),
        name="chip_sums",
    )(spots, own, received, own_embed)


def outgoing_kernel(spots, own, other, *refs):
    *messages, low = refs
    emb = own.shape[1]
    total = (own[...] + other[...].astype(f32)).astype(bf16)
    low[...] = total[:emb]
    piece = emb // 8
    mods = total[emb : emb + 32]
    rows = total.shape[0] - emb - 32
    base = rows + 32
    for k, message in enumerate(messages):
        message[:rows] = total[emb + 32 :]
        message[rows:base] = mods
        for j in range(2):
            start = pl.multiple_of(spots[2 * k + j] * piece, piece)
            message[base + j * piece : base + (j + 1) * piece] = low[pl.ds(start, piece)]


def outgoing(spots, own, other):
    emb = own.shape[1]
    rows = own.shape[0] - emb + 2 * (emb // 8)
    return pl.pallas_call(
        outgoing_kernel,
        in_specs=[SMEM_SPEC] + [VMEM_SPEC] * 2,
        out_specs=[VMEM_SPEC] * 4,
        out_shape=[jax.ShapeDtypeStruct((rows, emb), bf16)] * 4,
        scratch_shapes=[pltpu.VMEM((emb, emb), bf16)],
        cost_estimate=estimate(0, 0),
        name="outgoing",
    )(spots, own, other)


def relay_kernel(share, piece, *refs):
    *arrived, message, keep = refs
    for k, ref in enumerate(arrived):
        message[k * share : (k + 1) * share] = ref[:share]
    for j, target in ((0, keep), (1, message)):
        begin = share + j * piece
        total = sum(ref[begin : begin + piece].astype(f32) for ref in arrived)
        if j:
            message[4 * share :] = total.astype(bf16)
        else:
            keep[...] = total


def relay(share, piece, arrived):
    emb = arrived[0].shape[1]
    return pl.pallas_call(
        functools.partial(relay_kernel, share, piece),
        in_specs=[VMEM_SPEC] * 4,
        out_specs=[VMEM_SPEC] * 2,
        out_shape=[
            jax.ShapeDtypeStruct((4 * share + piece, emb), bf16),
            jax.ShapeDtypeStruct((piece, emb), f32),
        ],
        cost_estimate=estimate(0, 0),
        name="relay",
    )(*arrived)


def landed_kernel(share, rows, features, near, far, keep, small):
    width = small.shape[1] - keep.shape[1]
    total = jnp.zeros((features.shape[1], width), f32)
    for k in range(8):
        source, begin = (near, far)[k // 4], k % 4 * share + rows
        mods = jnp.concatenate(
            [source[begin + q * 8 : begin + q * 8 + 8] for q in range(4)], axis=1
        )
        total += dot(features[k * 8 : (k + 1) * 8], mods, COLUMNS_OF_BOTH)
    small[:, :width] = total
    small[:, width:] = keep[...] + far[4 * share :].astype(f32)


def landed(docs, share, rows, width, features, near, far, keep):
    return pl.pallas_call(
        functools.partial(landed_kernel, share, rows),
        in_specs=[VMEM_SPEC] * 4,
        out_specs=VMEM_SPEC,
        out_shape=jax.ShapeDtypeStruct((features.shape[1], width + keep.shape[1]), f32),
        cost_estimate=estimate(0, 0),
        name="landed",
    )(features, near, far, keep)


def per_device(
    token_ids,
    lengths,
    time_steps,
    embed_table,
    input_weight,
    time_weight,
    project_weight,
    output_weight,
    up_weight,
    down_weight,
    cotangent,
):
    rows = token_ids.shape[0]
    half, quarter = rows // 2, rows // 4
    count = lax.axis_size("dp")
    groups = lax.axis_size("tensor")
    me = lax.axis_index("dp")
    place = lax.axis_index("tensor")
    x, c = place // 2, place % 2
    width = cotangent.shape[1]
    docs = lengths.shape[0]
    shard = embed_table.shape[0]
    emb_rows = input_weight.shape[0]
    head_width = project_weight.shape[1]
    heads = head_width // (3 * HD)
    third = heads * HD
    per = width // count
    dp = Direct(count)

    my_ids = lax.dynamic_slice_in_dim(token_ids, (c * 2 + x) * quarter, quarter)
    heard = jnp.concatenate([my_ids, time_steps])[None]
    table = embed_table.astype(f32)
    rscale = lax.rsqrt(jnp.mean(table * table, axis=1, keepdims=True) + table_eps)
    normed = (table * rscale).astype(bf16)
    crossed = swap_x(normed)
    heard = jnp.concatenate([heard, dp.swap(after(heard, normed), 4)], axis=0)

    packed, small = pack_first(scalars([c]), project_weight, input_weight, output_weight)
    packed = lax.all_gather(packed, "dp")
    small_z2 = dp.swap(small, 4)
    gathered = lax.all_gather(pack_second(up_weight, down_weight), "dp")
    heard = jnp.concatenate([heard, dp.swap(heard, 2)], axis=0)
    heard = jnp.concatenate([heard, dp.swap(heard, 1)], axis=0)

    pair = jnp.concatenate([normed, crossed], axis=0)
    shards = jnp.concatenate([pair, swap_core(pair)], axis=0)
    entry = jnp.arange(4 * shard, dtype=jnp.int32)
    which = entry // shard
    owner = (x ^ (which & 1)) * 2 + (c ^ (which >> 1))
    vocab = (me * groups + owner) * shard + entry % shard

    feature = me * emb_rows + jnp.arange(emb_rows, dtype=jnp.int32)
    part = EMB // 2
    frequency = jnp.exp(-math.log(10000.0) * (feature % part).astype(f32) / part)
    angles = heard[:, quarter:].astype(f32)[:, :, None] * frequency[None, None, :]
    features = jnp.where(feature[None, None, :] < part, jnp.sin(angles), jnp.cos(angles))
    features = features.astype(bf16)
    time_part = lax.dynamic_slice_in_dim(time_weight, place * width, width, 1)
    found_mods = dot(features.reshape(count * docs, emb_rows), time_part)
    found_mods = found_mods.reshape(count, docs, 4, EMB).transpose(0, 2, 1, 3)
    found_mods = jnp.concatenate(split_two(found_mods.reshape(count, 4 * docs, EMB)), axis=1)

    def look_up(begin, end):
        names = heard[begin:end, :quarter].reshape(-1)
        onehot = (names[:, None] == vocab[None, :]).astype(bf16)
        found = dot(onehot, shards).astype(bf16).reshape(end - begin, quarter, EMB)
        return jnp.concatenate([found, found_mods[begin:end]], axis=1)

    looked_up = look_up(4, 8)
    crossed = dp.swap(looked_up, 1)
    small = jnp.concatenate([small, after(small_z2, looked_up)], axis=0)
    small_z1 = dp.swap(small, 2)
    near = look_up(0, 4)
    crossed, small_z1 = join(crossed, small_z1)
    near = near.astype(f32) + crossed.astype(f32)
    mods = near[:, quarter : quarter + 4 * docs] + near[:, quarter + 4 * docs :]
    near = jnp.concatenate([near[:, :quarter].astype(bf16), *split_two(mods)], axis=1)

    small = jnp.concatenate([small, small_z1], axis=0)
    small_far = dp.swap(small, 1)
    arrived = [near[0]] + [dp.swap(near[k], ORDER[k]) for k in (1, 2, 3)]
    arrived[3], small_far = join(arrived[3], small_far)
    mine = finish(True, docs, dp.places, arrived)
    project, output, input_half = unpack(
        scalars(dp.places), after(packed, mine), small, small_far, EMB
    )
    input_other = swap_core(input_half)
    input_full = jnp.concatenate(
        [jnp.where(c == 0, input_half, input_other), jnp.where(c == 0, input_other, input_half)],
        axis=1,
    )
    input_full = permute(input_full, [0], dp.places)
    other = swap_x(mine)
    both = jnp.stack([jnp.where(x == 0, mine, other), jnp.where(x == 0, other, mine)])
    far = swap_core(both)
    own_mods, far_mods = both[:, quarter:], far[:, quarter:]
    scale_one, scale_two = jnp.where(c == 0, own_mods, far_mods)
    shift_one, shift_two = jnp.where(c == 0, far_mods, own_mods)

    position = jnp.arange(rows, dtype=jnp.int32) ^ (c * half)
    ends = jnp.cumsum(lengths)
    document = jnp.sum((position[:, None] >= ends[None, :]).astype(jnp.int32), axis=1)
    column = document[:, None]
    cot = permute(after(cotangent, heard), [c, 1 - c], dp.places)

    hidden_one, query, keys, values, stream_zero = front(
        docs, column, both, far, input_full, project, scale_one, shift_one
    )

    def reduce_core(own, far, weight, dims=((1,), (0,))):
        sent = swap_core(dot(far, weight, dims).astype(bf16))
        return (dot(own, weight, dims) + sent.astype(f32)).astype(bf16)

    def over_rows(left, right):
        return dot(left[0], right[0], COLUMNS_OF_BOTH) + dot(left[1], right[1], COLUMNS_OF_BOTH)

    attended, logsum = attention(document, query, keys, values)
    attention_sum = reduce_core(attended[:half], attended[half:], output)
    crossed = swap_x(attention_sum)
    crossed, cot = join(crossed, cot)
    up, down = spread(scalars(dp.places), after(gathered, attention_sum))
    stream_one, hidden = second_norm(
        docs, column, stream_zero, attention_sum, crossed, scale_two, shift_two
    )
    hidden_two = (hidden, swap_core(hidden))
    cot_two = (cot[:half], cot[half:])
    activated, grad_upward = [], []
    for at in range(2):
        upward = dot(hidden_two[at], up)
        phi = 0.5 * (1.0 + lax.erf(upward * math.sqrt(0.5)))
        activated.append((upward * phi).astype(bf16))
        slope = phi + upward * (math.sqrt(0.5 / math.pi) * jnp.exp(-0.5 * upward * upward))
        grad_active = dot(cot_two[at], down)
        grad_upward.append((grad_active * slope).astype(bf16))
    grad_two = reduce_core(*grad_upward, up, ROWS_OF_BOTH)
    crossed = swap_x(grad_two)
    bundled = weight_grads(
        scalars(dp.places), hidden_two, [after(part, grad_two) for part in grad_upward], cot, activated
    )
    reduced = lax.psum_scatter(bundled, "dp", scatter_dimension=0, tiled=False)
    crossed, bundled = join(crossed, bundled)
    grad_one, low, *by_two = second_back(
        docs, column, stream_one, grad_two, crossed, scale_two, cot
    )
    grad_attn = (low, swap_core(low))
    grad_attended = jnp.concatenate(
        [dot(part, output, ROWS_OF_BOTH).astype(bf16) for part in grad_attn], axis=0
    )
    grad_projected = attention_back(
        document, query, keys, values, grad_attended, attended, logsum
    )
    flag = jnp.where(x == 0, 1, 0)
    own_embed, far_embed, grad_input, *by_one = first_back(
        docs,
        scalars([flag]),
        column,
        both,
        far,
        input_full,
        project,
        grad_projected,
        scale_one,
        grad_one,
    )
    share = quarter + 32
    own_sums, far_sums = local_sums(
        scalars(dp.inverse + [c, flag]), grad_input, [*by_one, *by_two], far_embed
    )
    received = swap_core(far_sums)
    keep, send = chip_sums(scalars([x]), own_sums, received, own_embed)
    crossed = swap_x(send)
    grad_project = dot(hidden_one, after(grad_projected, send), COLUMNS_OF_BOTH)
    grad_output = over_rows((attended[:half], attended[half:]), grad_attn)
    grad_output = jnp.concatenate(
        [unfold(grad_output[:, k * per : (k + 1) * per], 2) for k in range(count)], axis=0
    )
    grad_packed = jnp.concatenate([grad_project, grad_output], axis=1).astype(bf16)
    branch_sum = reduce_core(*[after(part, send) for part in activated], down, ROWS_OF_BOTH)
    crossed, grad_packed, branch_sum = join(crossed, grad_packed, branch_sum)
    packed_first = dp.swap(grad_packed[width // 2 :], 1)
    branch_crossed = swap_x(after(branch_sum, crossed))
    messages = outgoing(scalars([me ^ v ^ j for v in ORDER[:4] for j in range(2)]), keep, crossed)
    arrived = [messages[0]] + [dp.swap(messages[k], ORDER[k]) for k in (1, 2, 3)]
    arrived[3], packed_first, reduced = join(arrived[3], packed_first, reduced)
    near, keep = relay(share, emb_rows, arrived)
    far = dp.swap(near, 1)
    packed_first = after(packed_first, near)
    branch_crossed = after(branch_crossed, near)
    packed_sum = grad_packed[: width // 2].astype(f32) + packed_first.astype(f32)
    packed_second = dp.swap(packed_sum[2 * per :].astype(bf16), 2)

    names = jnp.pad(heard[:, :quarter], ((0, 0), (0, share - quarter)), constant_values=-1)
    near_ids, far_ids = names[:4].reshape(-1), names[4:].reshape(-1)
    near_ids, far_ids = (
        jnp.pad(part, (0, emb_rows), constant_values=-1) for part in (near_ids, far_ids)
    )

    def table_part(first, last, tokens, names):
        onehot = (vocab[first * shard : last * shard, None] == names[None, :]).astype(bf16)
        return dot(onehot, tokens)

    near_low = table_part(0, 4, near, near_ids).astype(bf16)
    block = branch_sum.astype(f32) + branch_crossed.astype(f32)
    block = (stream_one + block).astype(bf16)
    block_out = jnp.concatenate([block, swap_core(block)], axis=0)
    block_out = permute(block_out, [c, 1 - c], dp.inverse)
    summed_down = reduced.reshape(2 * per, -1)[per:].T.astype(f32)
    far, packed_second, block_out, near_low, summed_down = join(
        far, packed_second, block_out, near_low, summed_down
    )
    theirs = near_low[2 * shard :] + table_part(2, 4, far, far_ids)
    theirs = swap_core(theirs.astype(bf16)).astype(f32)
    sent = near_low[shard : 2 * shard] + table_part(1, 2, far, far_ids)
    sent_low = (sent + theirs[shard:]).astype(bf16)
    sent = swap_x(sent_low)
    kept = near_low[:shard] + table_part(0, 1, far, far_ids) + theirs[:shard]

    features = jnp.pad(features, ((0, 0), (0, 8 - docs), (0, 0))).reshape(8 * count, emb_rows)
    small = landed(docs, share, quarter, width, features, near, far, after(keep, sent_low))
    packed_sum = packed_sum[: 2 * per] + after(packed_second, sent_low).astype(f32)
    packed_third = dp.swap(packed_sum[per:].astype(bf16), 4)
    other = swap_x(small)

    reduced = reduced.astype(f32)
    summed_up = reduced[:per]
    summed_packed = packed_sum[:per] + after(packed_third, kept).astype(f32)
    summed_project = summed_packed[:, :head_width]
    summed_output = fold(summed_packed[:, head_width:], per)
    summed_project = (
        summed_project.reshape(per, 3, heads, HD).transpose(0, 2, 1, 3).reshape(per, head_width)
    )
    sent, kept, summed_up = join(sent, kept, summed_up)
    other = after(other, sent)
    both = jnp.stack([jnp.where(x == 0, small, other), jnp.where(x == 0, other, small)])
    far = swap_core(both)
    pieces = []
    for at in range(2):
        pieces += [jnp.where(c == 0, both[at], far[at]), jnp.where(c == 0, far[at], both[at])]
    summed_time = jnp.concatenate([piece[:, :width] for piece in pieces], axis=1)
    summed_input = jnp.concatenate([piece[:, width:] for piece in pieces], axis=1)
    grad_normed = kept + sent.astype(f32)
    grad_table = rscale * grad_normed - table * (
        rscale * rscale * rscale * jnp.mean(grad_normed * table, axis=1, keepdims=True)
    )
    return (
        block_out,
        grad_table,
        summed_input,
        summed_time,
        summed_project,
        summed_output,
        summed_up,
        summed_down,
    )


def normalize(table_rows):
    return table_rows * lax.rsqrt(
        jnp.mean(table_rows * table_rows, axis=1, keepdims=True) + table_eps
    )


def layer_norm(value, scale, shift):
    centred = value - jnp.mean(value, axis=-1, keepdims=True)
    return (
        centred
        * lax.rsqrt(jnp.mean(centred * centred, axis=-1, keepdims=True) + norm_eps)
        * (1.0 + scale)
        + shift
    )


def time_features(step_index, width):
    half = width // 2
    frequency = jnp.exp(-math.log(10000.0) * jnp.arange(half).astype(jnp.float32) / half)
    angles = step_index.astype(jnp.float32)[:, None] * frequency[None, :]
    return jnp.concatenate([jnp.sin(angles), jnp.cos(angles)], axis=1)


def gelu_exact(value):
    return jax.nn.gelu(value, approximate=False)


def whole_collectives(
    token_ids,
    lengths,
    time_steps,
    embed_table,
    input_weight,
    time_weight,
    project_weight,
    output_weight,
    up_weight,
    down_weight,
    cotangent,
):
    rows = token_ids.shape[0]
    groups = lax.axis_size("tensor")
    tensor_place = lax.axis_index("tensor")
    shard_rows = embed_table.shape[0]
    factor = 1.0 / math.sqrt(HD)
    normed, normed_back = jax.vjp(normalize, embed_table.astype(jnp.float32))
    normed_low = normed.astype(jnp.bfloat16)
    gathered = (
        lax.all_gather(input_weight, "dp", axis=0, tiled=True),
        lax.all_gather(time_weight, "dp", axis=0, tiled=True),
        lax.all_gather(project_weight, "dp", axis=0, tiled=True),
        lax.all_gather(output_weight, "dp", axis=1, tiled=True),
        lax.all_gather(up_weight, "dp", axis=0, tiled=True),
        lax.all_gather(down_weight, "dp", axis=1, tiled=True),
    )
    input_full, time_full, project_full, output_full, up_full, down_full = gathered

    def vocab_rows(count):
        flat_index = jnp.arange(count, dtype=jnp.int32)
        return (
            flat_index // shard_rows * groups + tensor_place
        ) * shard_rows + flat_index % shard_rows

    token_block = min(256, rows)
    piece = lax.all_gather(normed_low, "dp", axis=0, tiled=True)
    vocab = vocab_rows(piece.shape[0])
    parts = []
    for add_begin in range(0, rows, token_block):
        add_onehot = (
            token_ids[add_begin : add_begin + token_block, None] == vocab[None, :]
        ).astype(jnp.bfloat16)
        parts.append(jnp.dot(add_onehot, piece, preferred_element_type=jnp.float32))
    partial_embed = jnp.concatenate(parts, axis=0)
    embed = lax.psum(partial_embed.astype(jnp.bfloat16), "tensor")
    stream_zero = jnp.dot(embed, input_full, preferred_element_type=jnp.float32)
    ends = jnp.cumsum(lengths)
    position = jnp.arange(rows, dtype=jnp.int32)
    document = jnp.sum((position[:, None] >= ends[None, :]).astype(jnp.int32), axis=1)
    member = (document[:, None] == jnp.arange(lengths.shape[0], dtype=jnp.int32)[None, :]).astype(
        jnp.float32
    )
    features = time_features(time_steps, EMB).astype(jnp.bfloat16)
    modulation = jnp.dot(features, time_full, preferred_element_type=jnp.float32)
    row_mods = jnp.dot(member, modulation, precision=highest)
    scale_one, shift_one, scale_two, shift_two = jnp.split(row_mods, 4, axis=1)
    normed_one, norm_one_back = jax.vjp(layer_norm, stream_zero, scale_one, shift_one)
    hidden_one = normed_one.astype(jnp.bfloat16)
    projected = jnp.dot(hidden_one, project_full, preferred_element_type=jnp.float32).astype(
        jnp.bfloat16
    )
    heads_here = projected.shape[1] // (3 * HD)
    projected = projected.reshape(rows, heads_here, 3, HD)
    query = jnp.transpose(projected[:, :, 0], (1, 0, 2))
    keys = jnp.transpose(projected[:, :, 1], (1, 0, 2))
    values = jnp.transpose(projected[:, :, 2], (1, 0, 2))
    query_block = min(512, rows)

    def scores_of(begin):
        block_query = query[:, begin : begin + query_block]
        plain = (
            jnp.einsum("hqd,hkd->hqk", block_query, keys, preferred_element_type=jnp.float32)
            * factor
        )
        allowed = document[begin : begin + query_block, None] == document[None, :]
        return (jnp.where(allowed[None], plain, masked_score), block_query)

    outputs = []
    logsums = []
    kept_probs = []
    for begin in range(0, rows, query_block):
        scores, block_query = scores_of(begin)
        peak = jnp.max(scores, axis=2, keepdims=True)
        expo = jnp.exp(scores - peak)
        total = jnp.sum(expo, axis=2, keepdims=True)
        logsums.append(peak + jnp.log(total))
        probs_low = (expo / total).astype(jnp.bfloat16)
        kept_probs.append(probs_low)
        outputs.append(
            jnp.einsum("hqk,hkd->hqd", probs_low, values, preferred_element_type=jnp.float32)
        )
    attended = (
        jnp.transpose(jnp.concatenate(outputs, axis=1), (1, 0, 2))
        .reshape(rows, heads_here * HD)
        .astype(jnp.bfloat16)
    )
    attention_sum = lax.psum(
        jnp.dot(attended, output_full, preferred_element_type=jnp.float32), "tensor"
    )
    stream_one_rows = stream_zero + attention_sum
    normed_two, norm_two_back = jax.vjp(layer_norm, stream_one_rows, scale_two, shift_two)
    hidden_two = normed_two.astype(jnp.bfloat16)
    upward = jnp.dot(hidden_two, up_full, preferred_element_type=jnp.float32)
    activated, gelu_back = jax.vjp(gelu_exact, upward)
    activated_low = activated.astype(jnp.bfloat16)
    branch = lax.psum(
        jnp.dot(activated_low, down_full, preferred_element_type=jnp.float32), "tensor"
    )
    block_out = (stream_one_rows + branch).astype(jnp.bfloat16)
    grad_down = jnp.dot(activated_low.T, cotangent, preferred_element_type=jnp.float32)
    grad_active = jnp.dot(cotangent, down_full.T, preferred_element_type=jnp.float32)
    grad_upward = gelu_back(grad_active)[0].astype(jnp.bfloat16)
    grad_up = jnp.dot(hidden_two.T, grad_upward, preferred_element_type=jnp.float32)
    grad_hidden_two = lax.psum(
        jnp.dot(grad_upward, up_full.T, preferred_element_type=jnp.float32), "tensor"
    )
    grad_stream_rows, grad_scale_two, grad_shift_two = norm_two_back(grad_hidden_two)
    grad_stream_rows = grad_stream_rows + cotangent.astype(jnp.float32)
    grad_attn_rows = grad_stream_rows.astype(jnp.bfloat16)
    grad_output = jnp.dot(attended.T, grad_attn_rows, preferred_element_type=jnp.float32)
    grad_attended = jnp.dot(
        grad_attn_rows, output_full.T, preferred_element_type=jnp.float32
    ).astype(jnp.bfloat16)
    grad_attended = jnp.transpose(grad_attended.reshape(rows, heads_here, HD), (1, 0, 2))
    query_grads = []
    grad_keys = jnp.zeros(keys.shape, jnp.float32)
    grad_values = jnp.zeros(values.shape, jnp.float32)
    for number, begin in enumerate(range(0, rows, query_block)):
        scores, block_query = scores_of(begin)
        probs = jnp.exp(scores - logsums[number])
        block_grad = grad_attended[:, begin : begin + query_block]
        grad_probs = jnp.einsum(
            "hqd,hkd->hqk", block_grad, values, preferred_element_type=jnp.float32
        )
        inner = jnp.sum(probs * grad_probs, axis=2, keepdims=True)
        grad_scores = (probs * (grad_probs - inner)).astype(jnp.bfloat16)
        query_grads.append(
            jnp.einsum("hqk,hkd->hqd", grad_scores, keys, preferred_element_type=jnp.float32)
            * factor
        )
        grad_keys = (
            grad_keys
            + jnp.einsum(
                "hqk,hqd->hkd", grad_scores, block_query, preferred_element_type=jnp.float32
            )
            * factor
        )
        grad_values = grad_values + jnp.einsum(
            "hqk,hqd->hkd", kept_probs[number], block_grad, preferred_element_type=jnp.float32
        )
    grad_query = jnp.concatenate(query_grads, axis=1)
    grad_projected = jnp.stack([grad_query, grad_keys, grad_values], axis=2)
    grad_projected = (
        jnp.transpose(grad_projected, (1, 0, 2, 3))
        .reshape(rows, heads_here * 3 * HD)
        .astype(jnp.bfloat16)
    )
    grad_project = jnp.dot(hidden_one.T, grad_projected, preferred_element_type=jnp.float32)
    grad_hidden_one = lax.psum(
        jnp.dot(grad_projected, project_full.T, preferred_element_type=jnp.float32), "tensor"
    )
    grad_stream_zero, grad_scale_one, grad_shift_one = norm_one_back(grad_hidden_one)
    grad_zero_low = (grad_stream_zero + grad_stream_rows).astype(jnp.bfloat16)
    grad_rows = jnp.concatenate(
        [grad_scale_one, grad_shift_one, grad_scale_two, grad_shift_two], axis=1
    )
    partial_modulation = jnp.dot(member.T, grad_rows, precision=highest)
    grad_stream_zero = grad_zero_low
    grad_input = jnp.dot(embed.T, grad_stream_zero, preferred_element_type=jnp.float32)
    grad_embed = jnp.dot(grad_stream_zero, input_full.T, preferred_element_type=jnp.float32).astype(
        jnp.bfloat16
    )
    grad_time = jnp.dot(features.astype(jnp.float32).T, partial_modulation, precision=highest)
    every_row = shard_rows * lax.axis_size("dp")
    vocab_all = vocab_rows(every_row)
    grad_normed = jnp.zeros((every_row, EMB), jnp.float32)
    for begin in range(0, rows, token_block):
        onehot = (token_ids[begin : begin + token_block, None] == vocab_all[None, :]).astype(
            jnp.bfloat16
        )
        grad_normed = grad_normed + jnp.einsum(
            "tv,te->ve",
            onehot,
            grad_embed[begin : begin + token_block],
            preferred_element_type=jnp.float32,
        )
    (
        summed_input,
        summed_time,
        summed_project,
        summed_output,
        summed_up,
        summed_down,
        summed_table,
    ) = (
        lax.psum_scatter(grad_input, "dp", scatter_dimension=0, tiled=True),
        lax.psum_scatter(grad_time, "dp", scatter_dimension=0, tiled=True),
        lax.psum_scatter(grad_project, "dp", scatter_dimension=0, tiled=True),
        lax.psum_scatter(grad_output, "dp", scatter_dimension=1, tiled=True),
        lax.psum_scatter(grad_up, "dp", scatter_dimension=0, tiled=True),
        lax.psum_scatter(grad_down, "dp", scatter_dimension=1, tiled=True),
        lax.psum_scatter(grad_normed, "dp", scatter_dimension=0, tiled=True),
    )
    grad_table = normed_back(summed_table)[0]
    return (
        block_out,
        grad_table,
        summed_input,
        summed_time,
        summed_project,
        summed_output,
        summed_up,
        summed_down,
    )


def solution(mesh):
    count, groups = mesh.shape["dp"], mesh.shape["tensor"]
    return jax.shard_map(
        per_device if count == len(ORDER) and groups == 4 else whole_collectives,
        mesh=mesh,
        in_specs=(
            P("dp"),
            P("dp"),
            P("dp"),
            P(("dp", "tensor"), None),
            P("dp", None),
            P("dp", None),
            P("dp", "tensor"),
            P("tensor", "dp"),
            P("dp", "tensor"),
            P("tensor", "dp"),
            P("dp", None),
        ),
        out_specs=(
            P("dp", None),
            P(("dp", "tensor"), None),
            P("dp", None),
            P("dp", None),
            P("dp", "tensor"),
            P("tensor", "dp"),
            P("dp", "tensor"),
            P("tensor", "dp"),
        ),
        check_vma=False,
    )
```

```python
import functools
import math

import jax
import jax.numpy as jnp
from jax import lax
from jax.experimental import pallas as pl
from jax.experimental.pallas import tpu as pltpu
from jax.sharding import PartitionSpec as P

HD = 64
EMB = 256

table_eps = 1e-06
norm_eps = 1e-05
masked_score = -1e30
highest = lax.Precision.HIGHEST
bf16 = jnp.bfloat16
f32 = jnp.float32


def dot(left, right, dims=((1,), (0,))):
    return lax.dot_general(left, right, (dims, ((), ())), preferred_element_type=f32)


def join(*values):
    return lax.optimization_barrier(values)


def after(value, *others):
    return lax.optimization_barrier((value,) + others)[0]


SWAP_CORE = [(0, 1), (1, 0), (2, 3), (3, 2)]
SWAP_X = [(0, 2), (2, 0), (1, 3), (3, 1)]


def swap_core(value):
    return lax.ppermute(value, "tensor", SWAP_CORE)


def swap_x(value):
    return lax.ppermute(value, "tensor", SWAP_X)


ROWS_OF_BOTH = ((1,), (1,))
COLUMNS_OF_BOTH = ((0,), (0,))
ORDER = (0, 4, 2, 6, 1, 5, 3, 7)


class Direct:
    def __init__(self, count):
        self.count = count
        self.me = lax.axis_index("dp")
        self.places = [self.me ^ v for v in ORDER]
        self.inverse = [
            sum(jnp.where(self.places[k] == a, k, 0) for k in range(count)) for a in range(count)
        ]

    def swap(self, value, v):
        return lax.ppermute(value, "dp", [(i, i ^ v) for i in range(self.count)])

    def spread_small(self, value):
        value = value[None]
        for v in (4, 2, 1):
            value = jnp.concatenate([value, self.swap(value, v)], axis=0)
        return value


def picked(value, places, axis):
    size = value.shape[axis] // len(ORDER)
    return jnp.concatenate(
        [lax.slice_in_dim(value, p * size, (p + 1) * size, axis=axis) for p in places], axis=axis
    )


def split_two(value):
    high = value.astype(bf16)
    return high, (value - high.astype(f32)).astype(bf16)


def fold(value, width):
    return jnp.concatenate(jnp.split(value, value.shape[1] // width, axis=1), axis=0)


def unfold(value, count):
    return jnp.concatenate(jnp.split(value, count, axis=0), axis=1)


def permute_kernel(row_places, column_places, source, target):
    rows = source.shape[0] // row_places.shape[0]
    columns = source.shape[1] // column_places.shape[0]
    for i in range(row_places.shape[0]):
        for j in range(column_places.shape[0]):
            first = pl.multiple_of(row_places[i] * rows, rows)
            second = pl.multiple_of(column_places[j] * columns, columns)
            target[i * rows : (i + 1) * rows, j * columns : (j + 1) * columns] = source[
                pl.ds(first, rows), pl.ds(second, columns)
            ]


def permute(value, row_places, column_places):
    lists = [jnp.stack([jnp.int32(p) for p in places]) for places in (row_places, column_places)]
    return pl.pallas_call(
        permute_kernel,
        out_shape=jax.ShapeDtypeStruct(value.shape, value.dtype),
        in_specs=[pl.BlockSpec(memory_space=pltpu.SMEM)] * 2
        + [pl.BlockSpec(memory_space=pltpu.VMEM)],
        out_specs=pl.BlockSpec(memory_space=pltpu.VMEM),
        compiler_params=pltpu.CompilerParams(vmem_limit_bytes=32 << 20),
        cost_estimate=estimate(0, 0),
        name="permute",
    )(*lists, value)


def attention_kernel(heads, same_row, same_column, query, keys, values, attended, logsum):
    same = same_row[...] == same_column[...]
    q, k, v = query[...], keys[...], values[...]
    head = lax.broadcasted_iota(jnp.int32, q.shape, 1) // HD
    total_out = jnp.zeros(q.shape, f32)
    for h in range(heads):
        scores = dot(jnp.where(head == h, q, jnp.zeros_like(q)), k, ROWS_OF_BOTH)
        scores = jnp.where(same, scores, -1e30)
        peak = jnp.max(scores, axis=1, keepdims=True)
        expo = jnp.exp(scores - peak)
        total = jnp.sum(expo, axis=1, keepdims=True)
        total_out = jnp.where(head == h, dot(expo.astype(bf16), v) / total, total_out)
        logsum[:, h : h + 1] = peak + jnp.log(total)
    attended[...] = total_out.astype(bf16)


def attention(document, query, keys, values):
    rows, width = query.shape
    heads = width // HD
    block = rows // 2
    part = pl.BlockSpec((block, width), lambda i: (i, 0))
    whole = pl.BlockSpec((rows, width), lambda i: (0, 0))
    return pl.pallas_call(
        functools.partial(attention_kernel, heads),
        grid=(2,),
        in_specs=[
            pl.BlockSpec((block, 1), lambda i: (i, 0)),
            pl.BlockSpec((1, rows), lambda i: (0, 0)),
            part,
            whole,
            whole,
        ],
        out_specs=[part, pl.BlockSpec((block, heads), lambda i: (i, 0))],
        out_shape=[
            jax.ShapeDtypeStruct((rows, width), bf16),
            jax.ShapeDtypeStruct((rows, heads), f32),
        ],
        compiler_params=pltpu.CompilerParams(vmem_limit_bytes=32 << 20),
        cost_estimate=pl.CostEstimate(
            flops=4 * rows * rows * width * 4, bytes_accessed=8 * rows * width, transcendentals=0
        ),
        name="attention",
    )(document[:, None], document[None, :], query, keys, values)


def attention_back_kernel(
    count,
    same_row,
    same_column,
    query,
    keys,
    values,
    grad_attended,
    attended,
    logsum,
    grad_projected,
    sum_keys,
    sum_values,
):
    pair, at = pl.program_id(0), pl.program_id(1)
    same = same_row[...] == same_column[...]
    q, k, v, g = query[...], keys[...], values[...], grad_attended[...]
    rows, lanes = q.shape
    head = lax.broadcasted_iota(jnp.int32, q.shape, 1) // HD
    product = g.astype(f32) * attended[...].astype(f32)
    logs = logsum[...]
    lane = lax.broadcasted_iota(jnp.int32, logs.shape, 1)

    @pl.when(at == 0)
    def _():
        sum_keys[...] = jnp.zeros_like(sum_keys)
        sum_values[...] = jnp.zeros_like(sum_values)

    out = jnp.zeros(q.shape, f32)
    for h in range(lanes // HD):
        here = head == h
        q_head = jnp.where(here, q, jnp.zeros_like(q))
        g_head = jnp.where(here, g, jnp.zeros_like(g))
        log = jnp.sum(jnp.where(lane == pair * (lanes // HD) + h, logs, 0.0), 1, keepdims=True)
        scores = jnp.where(same, dot(q_head, k, ROWS_OF_BOTH), -1e30)
        probs = jnp.exp(scores - log)
        inner = jnp.sum(jnp.where(here, product, 0.0), axis=1, keepdims=True)
        grad_scores = probs * (dot(g_head, v, ROWS_OF_BOTH) - inner)
        grad_scores = grad_scores.astype(bf16)
        out = jnp.where(here, dot(grad_scores, k), out)
        sum_keys[...] += dot(grad_scores, q_head, COLUMNS_OF_BOTH)
        sum_values[...] += dot(probs.astype(bf16), g_head, COLUMNS_OF_BOTH)
    third = grad_projected.shape[1] // 3
    first = pl.multiple_of(at * rows, rows)
    grad_projected[pl.ds(first, rows), pl.ds(pl.multiple_of(pair * lanes, lanes), lanes)] = (
        out * (1.0 / math.sqrt(HD))
    ).astype(bf16)

    @pl.when(at == count - 1)
    def _():
        for which, total in ((1, sum_keys), (2, sum_values)):
            start = pl.multiple_of(which * third + pair * lanes, lanes)
            grad_projected[:, pl.ds(start, lanes)] = total[...].astype(bf16)


def attention_back(document, query, keys, values, grad_attended, attended, logsum):
    rows, width = query.shape
    heads = width // HD
    block, lanes = rows, 2 * HD
    part = pl.BlockSpec((block, lanes), lambda p, i: (i, p))
    whole = pl.BlockSpec((rows, lanes), lambda p, i: (0, p))
    return pl.pallas_call(
        functools.partial(attention_back_kernel, rows // block),
        grid=(width // lanes, rows // block),
        in_specs=[
            pl.BlockSpec((block, 1), lambda p, i: (i, 0)),
            pl.BlockSpec((1, rows), lambda p, i: (0, 0)),
            part,
            whole,
            whole,
            part,
            part,
            pl.BlockSpec((block, heads), lambda p, i: (i, 0)),
        ],
        out_specs=pl.BlockSpec((rows, 3 * width), lambda p, i: (0, 0)),
        out_shape=jax.ShapeDtypeStruct((rows, 3 * width), bf16),
        scratch_shapes=[pltpu.VMEM((rows, lanes), f32)] * 2,
        compiler_params=pltpu.CompilerParams(vmem_limit_bytes=32 << 20),
        cost_estimate=pl.CostEstimate(
            flops=60 * rows * rows * width, bytes_accessed=16 * rows * width, transcendentals=0
        ),
        name="attention_back",
    )(document[:, None], document[None, :], query, keys, values, grad_attended, attended, logsum)


SMEM_SPEC = pl.BlockSpec(memory_space=pltpu.SMEM)
VMEM_SPEC = pl.BlockSpec(memory_space=pltpu.VMEM)


def scalars(values):
    return jnp.stack([jnp.int32(value) for value in values])


def vmem(shape, index=None):
    if index is None:
        return pl.BlockSpec(shape, lambda *_: (0,) * len(shape))
    return pl.BlockSpec(shape, index)


def estimate(flops, moved):
    return pl.CostEstimate(flops=flops, bytes_accessed=moved, transcendentals=0)


def finish_kernel(direct, docs, places, *refs):
    *arrived, target = refs
    rows = arrived[0].shape[0] - 8 * docs
    total = arrived[0][:rows].astype(f32)
    high = arrived[0][rows : rows + 4 * docs].astype(f32)
    low = arrived[0][rows + 4 * docs :].astype(f32)
    for ref in arrived[1:]:
        total += ref[:rows].astype(f32)
        high += ref[rows : rows + 4 * docs].astype(f32)
        low += ref[rows + 4 * docs :].astype(f32)
    target[:rows] = total.astype(bf16)
    mods = high + low
    if direct:
        lanes = mods.shape[1] // 2
        blocks = [
            mods[(a // 2) * docs : (a // 2 + 1) * docs, (a % 2) * lanes : (a % 2 + 1) * lanes]
            for a in range(8)
        ]
        ordered = []
        for p in range(8):
            block = jnp.zeros_like(blocks[0])
            for a in range(8):
                block = jnp.where(places[p] == a, blocks[a], block)
            ordered.append(block)
        mods = jnp.concatenate(
            [jnp.concatenate(ordered[2 * q : 2 * q + 2], axis=1) for q in range(4)], axis=0
        )
    first = mods.astype(bf16)
    target[rows:] = jnp.concatenate(
        [first, (mods - first.astype(f32)).astype(bf16)], axis=0
    )


def finish(direct, docs, places, arrived):
    return pl.pallas_call(
        functools.partial(finish_kernel, direct, docs),
        in_specs=[pl.BlockSpec(memory_space=pltpu.SMEM)]
        + [pl.BlockSpec(memory_space=pltpu.VMEM)] * len(arrived),
        out_specs=pl.BlockSpec(memory_space=pltpu.VMEM),
        out_shape=jax.ShapeDtypeStruct(arrived[0].shape, bf16),
        cost_estimate=estimate(0, 0),
        name="finish",
    )(jnp.stack([jnp.int32(p) for p in places]), *arrived)


def row_mods(document, folded, docs):
    lane = lax.broadcasted_iota(jnp.int32, (document.shape[0], 8 * docs), 1)
    return jnp.concatenate(
        [
            dot((lane % (4 * docs) == document + q * docs).astype(bf16), folded)
            for q in range(4)
        ],
        axis=1,
    )


def normal_of(value):
    centred = value - jnp.mean(value, axis=-1, keepdims=True)
    inverse = lax.rsqrt(jnp.mean(centred * centred, axis=-1, keepdims=True) + norm_eps)
    return centred * inverse, inverse


def front_kernel(docs, document, both, far, weight, project, scale, shift, *outs):
    hidden, query, keys, values, stream = outs
    at = pl.program_id(0)
    rows = hidden.shape[0]
    embed = jnp.where(at < 2, both[0, :rows], far[0, :rows])
    value = dot(embed, weight[...])

    @pl.when(at < 2)
    def _():
        stream[...] = value

    normal, _ = normal_of(value)
    which = document[...]
    scaled = normal * (1.0 + row_mods(which, scale[...], docs)) + row_mods(which, shift[...], docs)
    low = scaled.astype(bf16)
    hidden[...] = low
    projected = dot(low, project[...]).astype(bf16)
    third = projected.shape[1] // 3
    query[...] = projected[:, :third] * jnp.asarray(1.0 / math.sqrt(HD), bf16)
    keys[...] = projected[:, third : 2 * third]
    values[...] = projected[:, 2 * third :]


def front(docs, document, both, far, weight, project, scale, shift):
    emb, width = weight.shape
    rows = document.shape[0]
    quarter = rows // 4
    third = project.shape[1] // 3
    message = both.shape[1]
    part = vmem((quarter, third), lambda i: (i, 0))
    return pl.pallas_call(
        functools.partial(front_kernel, docs),
        grid=(4,),
        in_specs=[
            vmem((quarter, 1), lambda i: (i, 0)),
            vmem((1, message, emb), lambda i: (jnp.minimum(i, 1), 0, 0)),
            vmem((1, message, emb), lambda i: (jnp.maximum(i - 2, 0), 0, 0)),
            vmem(weight.shape),
            vmem(project.shape),
            vmem(scale.shape),
            vmem(shift.shape),
        ],
        out_specs=[
            vmem((quarter, width), lambda i: (i, 0)),
            part,
            part,
            part,
            vmem((quarter, width), lambda i: (jnp.minimum(i, 1), 0)),
        ],
        out_shape=[jax.ShapeDtypeStruct((rows, width), bf16)]
        + [jax.ShapeDtypeStruct((rows, third), bf16)] * 3
        + [jax.ShapeDtypeStruct((rows // 2, width), f32)],
        compiler_params=pltpu.CompilerParams(vmem_limit_bytes=32 << 20),
        cost_estimate=estimate(2 * rows * width * (emb + 3 * third), 8 * rows * width),
        name="front",
    )(document, both, far, weight, project, scale, shift)


def pack_first_kernel(spots, project, weight, output, target, small):
    depth, columns = project.shape
    third = columns // 3
    for head in range(third // HD):
        for which in range(3):
            target[:, which * third + head * HD : which * third + (head + 1) * HD] = project[
                :, (3 * head + which) * HD : (3 * head + which + 1) * HD
            ]
    emb = weight.shape[0]
    for q in range(depth // emb):
        start = spots[0] * (weight.shape[1] // 2) + q * depth
        small[q * emb : (q + 1) * emb, :depth] = weight[
            :, pl.ds(pl.multiple_of(start, depth), depth)
        ]
    for j in range(2):
        small[:, (1 + j) * depth : (2 + j) * depth] = output[j * depth : (j + 1) * depth]


def pack_first(spots, project, weight, output):
    depth, columns = project.shape
    return pl.pallas_call(
        pack_first_kernel,
        in_specs=[SMEM_SPEC] + [VMEM_SPEC] * 3,
        out_specs=[VMEM_SPEC] * 2,
        out_shape=[
            jax.ShapeDtypeStruct((depth, columns), bf16),
            jax.ShapeDtypeStruct((depth, 3 * depth), bf16),
        ],
        name="pack_first",
    )(spots, project, weight, output)


def pack_second_kernel(up, down, target):
    per = up.shape[0]
    target[:per] = up[...]
    target[per:] = down[...].T


def pack_second(up, down):
    per, units = up.shape
    return pl.pallas_call(
        pack_second_kernel,
        in_specs=[VMEM_SPEC] * 2,
        out_specs=VMEM_SPEC,
        out_shape=jax.ShapeDtypeStruct((2 * per, units), bf16),
        name="pack_second",
    )(up, down)


def unpack_kernel(places, gathered, near, far, project, output, weight):
    depth = project.shape[0] // 8
    emb = weight.shape[0] // 8
    for p in range(8):
        rows = slice(p * depth, (p + 1) * depth)
        project[rows] = gathered[places[p]]
        source, begin = (near, far)[p // 4], p % 4 * depth
        for j in range(2):
            output[j * depth : (j + 1) * depth, rows] = source[
                begin : begin + depth, (1 + j) * depth : (2 + j) * depth
            ]
        first = pl.multiple_of(places[p] * emb, emb)
        for q in range(depth // emb):
            weight[pl.ds(first, emb), q * depth : (q + 1) * depth] = source[
                begin + q * emb : begin + (q + 1) * emb, :depth
            ]


def unpack(places, gathered, near, far, emb):
    count, depth, columns = gathered.shape
    return pl.pallas_call(
        unpack_kernel,
        in_specs=[SMEM_SPEC] + [VMEM_SPEC] * 3,
        out_specs=[VMEM_SPEC] * 3,
        out_shape=[
            jax.ShapeDtypeStruct((count * depth, columns), bf16),
            jax.ShapeDtypeStruct((2 * depth, count * depth), bf16),
            jax.ShapeDtypeStruct((emb, depth * depth // (emb // count)), bf16),
        ],
        compiler_params=pltpu.CompilerParams(vmem_limit_bytes=32 << 20),
        cost_estimate=estimate(0, 0),
        name="unpack",
    )(places, gathered, near, far)


def spread_kernel(places, gathered, up, down):
    per = up.shape[0] // 8
    for p in range(8):
        up[p * per : (p + 1) * per] = gathered[places[p], :per]
        down[p * per : (p + 1) * per] = gathered[places[p], per:]


def spread(places, gathered):
    width = gathered.shape[2]
    return pl.pallas_call(
        spread_kernel,
        in_specs=[SMEM_SPEC, VMEM_SPEC],
        out_specs=[VMEM_SPEC] * 2,
        out_shape=[jax.ShapeDtypeStruct((width, width), bf16)] * 2,
        compiler_params=pltpu.CompilerParams(vmem_limit_bytes=32 << 20),
        cost_estimate=estimate(0, 0),
        name="spread",
    )(places, gathered)


def weight_grads_kernel(
    places, hidden, hidden_far, grad, grad_far, cotangent, active, active_far, target
):
    at = pl.program_id(0)
    half = hidden.shape[0]
    per = target.shape[1] // 2
    up = dot(hidden[...], grad[...], COLUMNS_OF_BOTH)
    up += dot(hidden_far[...], grad_far[...], COLUMNS_OF_BOTH)
    down = dot(cotangent[:half], active[...], COLUMNS_OF_BOTH)
    down += dot(cotangent[half:], active_far[...], COLUMNS_OF_BOTH)
    for j in range(2):
        place = places[2 * at + j]
        target[place, :per] = up[j * per : (j + 1) * per].astype(bf16)
        target[place, per:] = down[j * per : (j + 1) * per].astype(bf16)


def weight_grads(places, hidden, grad, cotangent, active):
    half, width = hidden[0].shape
    units = grad[0].shape[1]
    per = width // len(ORDER)
    tall = vmem((half, 2 * per), lambda i: (0, i))
    whole = vmem((half, units))
    return pl.pallas_call(
        weight_grads_kernel,
        grid=(len(ORDER) // 2,),
        in_specs=[
            SMEM_SPEC,
            tall,
            tall,
            whole,
            whole,
            vmem((2 * half, 2 * per), lambda i: (0, i)),
            whole,
            whole,
        ],
        out_specs=vmem((len(ORDER), 2 * per, units)),
        out_shape=jax.ShapeDtypeStruct((len(ORDER), 2 * per, units), bf16),
        compiler_params=pltpu.CompilerParams(vmem_limit_bytes=40 << 20),
        cost_estimate=estimate(0, 0),
        name="weight_grads",
    )(places, *hidden, *grad, cotangent, *active)


def second_norm_kernel(docs, document, stream_zero, mine, other, scale, shift, stream, hidden):
    value = stream_zero[...] + (mine[...].astype(f32) + other[...].astype(f32))
    stream[...] = value
    normal, _ = normal_of(value)
    which = document[...]
    hidden[...] = (
        normal * (1.0 + row_mods(which, scale[...], docs)) + row_mods(which, shift[...], docs)
    ).astype(bf16)


def second_norm(docs, document, stream_zero, mine, other, scale, shift):
    half, width = mine.shape
    block = half // 2
    part = vmem((block, width), lambda i: (i, 0))
    return pl.pallas_call(
        functools.partial(second_norm_kernel, docs),
        grid=(2,),
        in_specs=[
            vmem((block, 1), lambda i: (i, 0)),
            part,
            part,
            part,
            vmem(scale.shape),
            vmem(shift.shape),
        ],
        out_specs=[part, part],
        out_shape=[
            jax.ShapeDtypeStruct((half, width), f32),
            jax.ShapeDtypeStruct((half, width), bf16),
        ],
        compiler_params=pltpu.CompilerParams(vmem_limit_bytes=32 << 20),
        cost_estimate=estimate(2 * half * width * 128, 12 * half * width),
        name="second_norm",
    )(document, stream_zero, mine, other, scale, shift)


def add_up(target, value):
    @pl.when(pl.program_id(0) == 0)
    def _():
        target[...] = value

    @pl.when(pl.program_id(0) > 0)
    def _():
        target[...] += value


def back_through_norm(docs, grad, value, which, scale):
    normal, inverse = normal_of(value)
    inner = grad * (1.0 + row_mods(which, scale, docs))
    back = inverse * (
        inner
        - jnp.mean(inner, axis=-1, keepdims=True)
        - normal * jnp.mean(inner * normal, axis=-1, keepdims=True)
    )
    lane = lax.broadcasted_iota(jnp.int32, (which.shape[0], 8), 1)
    member = (lane == which).astype(bf16)
    by_scale = dot(member, (grad * normal).astype(bf16), COLUMNS_OF_BOTH)
    by_shift = dot(member, grad.astype(bf16), COLUMNS_OF_BOTH)
    return back, by_scale, by_shift


def second_back_kernel(
    docs, document, stream, mine, other, scale, cotangent, stream_grad, low, by_scale, by_shift
):
    grad = mine[...].astype(f32) + other[...].astype(f32)
    back, for_scale, for_shift = back_through_norm(
        docs, grad, stream[...], document[...], scale[...]
    )
    add_up(by_scale, for_scale)
    add_up(by_shift, for_shift)
    total = cotangent[...].astype(f32) + back
    stream_grad[...] = total
    low[...] = total.astype(bf16)


def second_back(docs, document, stream, mine, other, scale, cotangent):
    half, width = mine.shape
    block = half // 2
    part = vmem((block, width), lambda i: (i, 0))
    sums = vmem((8, width))
    return pl.pallas_call(
        functools.partial(second_back_kernel, docs),
        grid=(2,),
        in_specs=[
            vmem((block, 1), lambda i: (i, 0)),
            part,
            part,
            part,
            vmem(scale.shape),
            part,
        ],
        out_specs=[part, part, sums, sums],
        out_shape=[
            jax.ShapeDtypeStruct((half, width), f32),
            jax.ShapeDtypeStruct((half, width), bf16),
            jax.ShapeDtypeStruct((8, width), f32),
            jax.ShapeDtypeStruct((8, width), f32),
        ],
        compiler_params=pltpu.CompilerParams(vmem_limit_bytes=32 << 20),
        cost_estimate=estimate(2 * half * width * 128, 16 * half * width),
        name="second_back",
    )(document, stream, mine, other, scale, cotangent)


def first_back_kernel(
    docs, flag, document, both, far, weight, project, grad_projected, scale, above, own, other,
    grad_weight, by_scale, by_shift,
):
    at = pl.program_id(0)
    rows = grad_projected.shape[0]
    embed = jnp.where(at < 2, both[0, :rows], far[0, :rows])
    value = dot(embed, weight[...])
    grad = dot(grad_projected[...], project[...], ROWS_OF_BOTH)
    back, for_scale, for_shift = back_through_norm(docs, grad, value, document[...], scale[...])
    add_up(by_scale, for_scale)
    add_up(by_shift, for_shift)
    counts = jnp.where(at < 2, flag[0], 0).astype(f32)
    low = (back + counts * above[...]).astype(bf16)
    grad_embed = dot(low, weight[...], ROWS_OF_BOTH)

    @pl.when(at < 2)
    def _():
        own[...] = grad_embed

    @pl.when(at >= 2)
    def _():
        other[...] = grad_embed.astype(bf16)

    add_up(grad_weight, dot(embed, low, COLUMNS_OF_BOTH))


def first_back(docs, flag, document, both, far, weight, project, grad_projected, scale, above):
    emb, width = weight.shape
    rows = document.shape[0]
    quarter = rows // 4
    message = both.shape[1]
    sums = vmem((8, width))
    early = lambda i: (jnp.minimum(i, 1), 0)
    late = lambda i: (jnp.maximum(i - 2, 0), 0)
    return pl.pallas_call(
        functools.partial(first_back_kernel, docs),
        grid=(4,),
        in_specs=[
            SMEM_SPEC,
            vmem((quarter, 1), lambda i: (i, 0)),
            vmem((1, message, emb), lambda i: (jnp.minimum(i, 1), 0, 0)),
            vmem((1, message, emb), lambda i: (jnp.maximum(i - 2, 0), 0, 0)),
            vmem(weight.shape),
            vmem(project.shape),
            vmem((quarter, project.shape[1]), lambda i: (i, 0)),
            vmem(scale.shape),
            vmem((quarter, width), early),
        ],
        out_specs=[
            vmem((quarter, emb), early),
            vmem((quarter, emb), late),
            vmem((emb, width)),
            sums,
            sums,
        ],
        out_shape=[
            jax.ShapeDtypeStruct((rows // 2, emb), f32),
            jax.ShapeDtypeStruct((rows // 2, emb), bf16),
            jax.ShapeDtypeStruct((emb, width), f32),
            jax.ShapeDtypeStruct((8, width), f32),
            jax.ShapeDtypeStruct((8, width), f32),
        ],
        compiler_params=pltpu.CompilerParams(vmem_limit_bytes=32 << 20),
        cost_estimate=estimate(2 * rows * width * (3 * emb + project.shape[1]), 16 * rows * width),
        name="first_back",
    )(flag, document, both, far, weight, project, grad_projected, scale, above)


def local_sums_kernel(spots, weight, *refs):
    mods, (far_embed, own, other) = refs[:4], refs[4:]
    emb = weight.shape[0]
    per = weight.shape[1] // 8
    share = emb + 32
    flag = spots[9].astype(f32)
    for target, core in ((own, spots[8]), (other, 1 - spots[8])):
        for x in range(2):
            column = 2 * x + core
            base = x * share
            for j in range(2):
                start = pl.multiple_of(spots[column * 2 + j] * per, per)
                target[base : base + emb, j * per : (j + 1) * per] = weight[
                    :, pl.ds(start, per)
                ].astype(target.dtype)
            for q in range(4):
                halves = []
                for j in range(2):
                    start = pl.multiple_of(spots[2 * q + j] * per, per)
                    total = mods[2 * x][:, pl.ds(start, per)]
                    total = jnp.where(core == 0, total, mods[2 * x + 1][:, pl.ds(start, per)])
                    halves.append(total if x == 0 else total * flag)
                block = jnp.concatenate(halves, axis=1)
                target[base + emb + q * 8 : base + emb + (q + 1) * 8] = block.astype(target.dtype)
    other[2 * share :] = far_embed[...]


def local_sums(spots, weight, mods, far_embed):
    emb = weight.shape[0]
    rows = 2 * (emb + 32)
    return pl.pallas_call(
        local_sums_kernel,
        in_specs=[SMEM_SPEC] + [VMEM_SPEC] * 6,
        out_specs=[VMEM_SPEC] * 2,
        out_shape=[
            jax.ShapeDtypeStruct((rows, emb), f32),
            jax.ShapeDtypeStruct((rows + far_embed.shape[0], emb), bf16),
        ],
        compiler_params=pltpu.CompilerParams(vmem_limit_bytes=32 << 20),
        cost_estimate=estimate(0, 0),
        name="local_sums",
    )(spots, weight, *mods, far_embed)


def chip_sums_kernel(spots, own, received, own_embed, keep, send):
    share = own.shape[0] // 2
    quarter = own_embed.shape[0] // 2
    for target, x in ((keep, spots[0]), (send, 1 - spots[0])):
        start = pl.multiple_of(x * share, share)
        total = own[pl.ds(start, share)] + received[pl.ds(start, share)].astype(f32)
        target[:share] = total.astype(target.dtype)
        rows = pl.multiple_of(x * quarter, quarter)
        far = received[pl.ds(pl.multiple_of(2 * share + rows, 64), quarter)]
        total = own_embed[pl.ds(rows, quarter)] + far.astype(f32)
        target[share:] = total.astype(target.dtype)


def chip_sums(spots, own, received, own_embed):
    emb = own.shape[1]
    rows = own.shape[0] // 2 + own_embed.shape[0] // 2
    return pl.pallas_call(
        chip_sums_kernel,
        in_specs=[SMEM_SPEC] + [VMEM_SPEC] * 3,
        out_specs=[VMEM_SPEC] * 2,
        out_shape=[
            jax.ShapeDtypeStruct((rows, emb), f32),
            jax.ShapeDtypeStruct((rows, emb), bf16),
        ],
        cost_estimate=estimate(0, 0),
        name="chip_sums",
    )(spots, own, received, own_embed)


def outgoing_kernel(spots, own, other, *refs):
    *messages, low = refs
    emb = own.shape[1]
    total = (own[...] + other[...].astype(f32)).astype(bf16)
    low[...] = total[:emb]
    piece = emb // 8
    mods = total[emb : emb + 32]
    rows = total.shape[0] - emb - 32
    base = rows + 32
    for k, message in enumerate(messages):
        message[:rows] = total[emb + 32 :]
        message[rows:base] = mods
        for j in range(2):
            start = pl.multiple_of(spots[2 * k + j] * piece, piece)
            message[base + j * piece : base + (j + 1) * piece] = low[pl.ds(start, piece)]


def outgoing(spots, own, other):
    emb = own.shape[1]
    rows = own.shape[0] - emb + 2 * (emb // 8)
    return pl.pallas_call(
        outgoing_kernel,
        in_specs=[SMEM_SPEC] + [VMEM_SPEC] * 2,
        out_specs=[VMEM_SPEC] * 4,
        out_shape=[jax.ShapeDtypeStruct((rows, emb), bf16)] * 4,
        scratch_shapes=[pltpu.VMEM((emb, emb), bf16)],
        cost_estimate=estimate(0, 0),
        name="outgoing",
    )(spots, own, other)


def relay_kernel(share, piece, *refs):
    *arrived, message, keep = refs
    for k, ref in enumerate(arrived):
        message[k * share : (k + 1) * share] = ref[:share]
    for j, target in ((0, keep), (1, message)):
        begin = share + j * piece
        total = sum(ref[begin : begin + piece].astype(f32) for ref in arrived)
        if j:
            message[4 * share :] = total.astype(bf16)
        else:
            keep[...] = total


def relay(share, piece, arrived):
    emb = arrived[0].shape[1]
    return pl.pallas_call(
        functools.partial(relay_kernel, share, piece),
        in_specs=[VMEM_SPEC] * 4,
        out_specs=[VMEM_SPEC] * 2,
        out_shape=[
            jax.ShapeDtypeStruct((4 * share + piece, emb), bf16),
            jax.ShapeDtypeStruct((piece, emb), f32),
        ],
        cost_estimate=estimate(0, 0),
        name="relay",
    )(*arrived)


def landed_kernel(share, rows, features, near, far, keep, small):
    width = small.shape[1] - keep.shape[1]
    total = jnp.zeros((features.shape[1], width), f32)
    for k in range(8):
        source, begin = (near, far)[k // 4], k % 4 * share + rows
        mods = jnp.concatenate(
            [source[begin + q * 8 : begin + q * 8 + 8] for q in range(4)], axis=1
        )
        total += dot(features[k * 8 : (k + 1) * 8], mods, COLUMNS_OF_BOTH)
    small[:, :width] = total
    small[:, width:] = keep[...] + far[4 * share :].astype(f32)


def landed(docs, share, rows, width, features, near, far, keep):
    return pl.pallas_call(
        functools.partial(landed_kernel, share, rows),
        in_specs=[VMEM_SPEC] * 4,
        out_specs=VMEM_SPEC,
        out_shape=jax.ShapeDtypeStruct((features.shape[1], width + keep.shape[1]), f32),
        cost_estimate=estimate(0, 0),
        name="landed",
    )(features, near, far, keep)


def per_device(
    token_ids,
    lengths,
    time_steps,
    embed_table,
    input_weight,
    time_weight,
    project_weight,
    output_weight,
    up_weight,
    down_weight,
    cotangent,
):
    rows = token_ids.shape[0]
    half, quarter = rows // 2, rows // 4
    count = lax.axis_size("dp")
    groups = lax.axis_size("tensor")
    me = lax.axis_index("dp")
    place = lax.axis_index("tensor")
    x, c = place // 2, place % 2
    width = cotangent.shape[1]
    docs = lengths.shape[0]
    shard = embed_table.shape[0]
    emb_rows = input_weight.shape[0]
    head_width = project_weight.shape[1]
    heads = head_width // (3 * HD)
    third = heads * HD
    per = width // count
    dp = Direct(count)

    my_ids = lax.dynamic_slice_in_dim(token_ids, (c * 2 + x) * quarter, quarter)
    heard = jnp.concatenate([my_ids, time_steps])[None]
    table = embed_table.astype(f32)
    rscale = lax.rsqrt(jnp.mean(table * table, axis=1, keepdims=True) + table_eps)
    normed = (table * rscale).astype(bf16)
    crossed = swap_x(normed)
    heard = jnp.concatenate([heard, dp.swap(after(heard, normed), 4)], axis=0)

    packed, small = pack_first(scalars([c]), project_weight, input_weight, output_weight)
    packed = lax.all_gather(packed, "dp")
    small_z2 = dp.swap(small, 4)
    gathered = lax.all_gather(pack_second(up_weight, down_weight), "dp")
    heard = jnp.concatenate([heard, dp.swap(heard, 2)], axis=0)
    heard = jnp.concatenate([heard, dp.swap(heard, 1)], axis=0)

    pair = jnp.concatenate([normed, crossed], axis=0)
    shards = jnp.concatenate([pair, swap_core(pair)], axis=0)
    entry = jnp.arange(4 * shard, dtype=jnp.int32)
    which = entry // shard
    owner = (x ^ (which & 1)) * 2 + (c ^ (which >> 1))
    vocab = (me * groups + owner) * shard + entry % shard

    feature = me * emb_rows + jnp.arange(emb_rows, dtype=jnp.int32)
    part = EMB // 2
    frequency = jnp.exp(-math.log(10000.0) * (feature % part).astype(f32) / part)
    angles = heard[:, quarter:].astype(f32)[:, :, None] * frequency[None, None, :]
    features = jnp.where(feature[None, None, :] < part, jnp.sin(angles), jnp.cos(angles))
    features = features.astype(bf16)
    time_part = lax.dynamic_slice_in_dim(time_weight, place * width, width, 1)
    found_mods = dot(features.reshape(count * docs, emb_rows), time_part)
    found_mods = found_mods.reshape(count, docs, 4, EMB).transpose(0, 2, 1, 3)
    found_mods = jnp.concatenate(split_two(found_mods.reshape(count, 4 * docs, EMB)), axis=1)

    def look_up(begin, end):
        names = heard[begin:end, :quarter].reshape(-1)
        onehot = (names[:, None] == vocab[None, :]).astype(bf16)
        found = dot(onehot, shards).astype(bf16).reshape(end - begin, quarter, EMB)
        return jnp.concatenate([found, found_mods[begin:end]], axis=1)

    looked_up = look_up(4, 8)
    crossed = dp.swap(looked_up, 1)
    small = jnp.concatenate([small, after(small_z2, looked_up)], axis=0)
    small_z1 = dp.swap(small, 2)
    near = look_up(0, 4)
    crossed, small_z1 = join(crossed, small_z1)
    near = near.astype(f32) + crossed.astype(f32)
    mods = near[:, quarter : quarter + 4 * docs] + near[:, quarter + 4 * docs :]
    near = jnp.concatenate([near[:, :quarter].astype(bf16), *split_two(mods)], axis=1)

    small = jnp.concatenate([small, small_z1], axis=0)
    small_far = dp.swap(small, 1)
    arrived = [near[0]] + [dp.swap(near[k], ORDER[k]) for k in (1, 2, 3)]
    arrived[3], small_far = join(arrived[3], small_far)
    mine = finish(True, docs, dp.places, arrived)
    project, output, input_half = unpack(
        scalars(dp.places), after(packed, mine), small, small_far, EMB
    )
    input_other = swap_core(input_half)
    input_full = jnp.concatenate(
        [jnp.where(c == 0, input_half, input_other), jnp.where(c == 0, input_other, input_half)],
        axis=1,
    )
    input_full = permute(input_full, [0], dp.places)
    other = swap_x(mine)
    both = jnp.stack([jnp.where(x == 0, mine, other), jnp.where(x == 0, other, mine)])
    far = swap_core(both)
    own_mods, far_mods = both[:, quarter:], far[:, quarter:]
    scale_one, scale_two = jnp.where(c == 0, own_mods, far_mods)
    shift_one, shift_two = jnp.where(c == 0, far_mods, own_mods)

    position = jnp.arange(rows, dtype=jnp.int32) ^ (c * half)
    ends = jnp.cumsum(lengths)
    document = jnp.sum((position[:, None] >= ends[None, :]).astype(jnp.int32), axis=1)
    column = document[:, None]
    cot = permute(after(cotangent, heard), [c, 1 - c], dp.places)

    hidden_one, query, keys, values, stream_zero = front(
        docs, column, both, far, input_full, project, scale_one, shift_one
    )

    def reduce_core(own, far, weight, dims=((1,), (0,))):
        sent = swap_core(dot(far, weight, dims).astype(bf16))
        return (dot(own, weight, dims) + sent.astype(f32)).astype(bf16)

    def over_rows(left, right):
        return dot(left[0], right[0], COLUMNS_OF_BOTH) + dot(left[1], right[1], COLUMNS_OF_BOTH)

    attended, logsum = attention(document, query, keys, values)
    attention_sum = reduce_core(attended[:half], attended[half:], output)
    crossed = swap_x(attention_sum)
    crossed, cot = join(crossed, cot)
    up, down = spread(scalars(dp.places), after(gathered, attention_sum))
    stream_one, hidden = second_norm(
        docs, column, stream_zero, attention_sum, crossed, scale_two, shift_two
    )
    hidden_two = (hidden, swap_core(hidden))
    cot_two = (cot[:half], cot[half:])
    activated, grad_upward = [], []
    for at in range(2):
        upward = dot(hidden_two[at], up)
        phi = 0.5 * (1.0 + lax.erf(upward * math.sqrt(0.5)))
        activated.append((upward * phi).astype(bf16))
        slope = phi + upward * (math.sqrt(0.5 / math.pi) * jnp.exp(-0.5 * upward * upward))
        grad_active = dot(cot_two[at], down)
        grad_upward.append((grad_active * slope).astype(bf16))
    grad_two = reduce_core(*grad_upward, up, ROWS_OF_BOTH)
    crossed = swap_x(grad_two)
    bundled = weight_grads(
        scalars(dp.places), hidden_two, [after(part, grad_two) for part in grad_upward], cot, activated
    )
    reduced = lax.psum_scatter(bundled, "dp", scatter_dimension=0, tiled=False)
    crossed, bundled = join(crossed, bundled)
    grad_one, low, *by_two = second_back(
        docs, column, stream_one, grad_two, crossed, scale_two, cot
    )
    grad_attn = (low, swap_core(low))
    grad_attended = jnp.concatenate(
        [dot(part, output, ROWS_OF_BOTH).astype(bf16) for part in grad_attn], axis=0
    )
    grad_projected = attention_back(
        document, query, keys, values, grad_attended, attended, logsum
    )
    flag = jnp.where(x == 0, 1, 0)
    own_embed, far_embed, grad_input, *by_one = first_back(
        docs,
        scalars([flag]),
        column,
        both,
        far,
        input_full,
        project,
        grad_projected,
        scale_one,
        grad_one,
    )
    share = quarter + 32
    own_sums, far_sums = local_sums(
        scalars(dp.inverse + [c, flag]), grad_input, [*by_one, *by_two], far_embed
    )
    received = swap_core(far_sums)
    keep, send = chip_sums(scalars([x]), own_sums, received, own_embed)
    crossed = swap_x(send)
    grad_project = dot(hidden_one, after(grad_projected, send), COLUMNS_OF_BOTH)
    grad_output = over_rows((attended[:half], attended[half:]), grad_attn)
    grad_output = jnp.concatenate(
        [unfold(grad_output[:, k * per : (k + 1) * per], 2) for k in range(count)], axis=0
    )
    grad_packed = jnp.concatenate([grad_project, grad_output], axis=1).astype(bf16)
    branch_sum = reduce_core(*[after(part, send) for part in activated], down, ROWS_OF_BOTH)
    crossed, grad_packed, branch_sum = join(crossed, grad_packed, branch_sum)
    packed_first = dp.swap(grad_packed[width // 2 :], 1)
    branch_crossed = swap_x(after(branch_sum, crossed))
    messages = outgoing(scalars([me ^ v ^ j for v in ORDER[:4] for j in range(2)]), keep, crossed)
    arrived = [messages[0]] + [dp.swap(messages[k], ORDER[k]) for k in (1, 2, 3)]
    arrived[3], packed_first, reduced = join(arrived[3], packed_first, reduced)
    near, keep = relay(share, emb_rows, arrived)
    far = dp.swap(near, 1)
    packed_first = after(packed_first, near)
    branch_crossed = after(branch_crossed, near)
    packed_sum = grad_packed[: width // 2].astype(f32) + packed_first.astype(f32)
    packed_second = dp.swap(packed_sum[2 * per :].astype(bf16), 2)

    names = jnp.pad(heard[:, :quarter], ((0, 0), (0, share - quarter)), constant_values=-1)
    near_ids, far_ids = names[:4].reshape(-1), names[4:].reshape(-1)
    near_ids, far_ids = (
        jnp.pad(part, (0, emb_rows), constant_values=-1) for part in (near_ids, far_ids)
    )

    def table_part(first, last, tokens, names):
        onehot = (vocab[first * shard : last * shard, None] == names[None, :]).astype(bf16)
        return dot(onehot, tokens)

    near_low = table_part(0, 4, near, near_ids).astype(bf16)
    block = branch_sum.astype(f32) + branch_crossed.astype(f32)
    block = (stream_one + block).astype(bf16)
    block_out = jnp.concatenate([block, swap_core(block)], axis=0)
    block_out = permute(block_out, [c, 1 - c], dp.inverse)
    summed_down = reduced.reshape(2 * per, -1)[per:].T.astype(f32)
    far, packed_second, block_out, near_low, summed_down = join(
        far, packed_second, block_out, near_low, summed_down
    )
    theirs = near_low[2 * shard :] + table_part(2, 4, far, far_ids)
    theirs = swap_core(theirs.astype(bf16)).astype(f32)
    sent = near_low[shard : 2 * shard] + table_part(1, 2, far, far_ids)
    sent_low = (sent + theirs[shard:]).astype(bf16)
    sent = swap_x(sent_low)
    kept = near_low[:shard] + table_part(0, 1, far, far_ids) + theirs[:shard]

    features = jnp.pad(features, ((0, 0), (0, 8 - docs), (0, 0))).reshape(8 * count, emb_rows)
    small = landed(docs, share, quarter, width, features, near, far, after(keep, sent_low))
    packed_sum = packed_sum[: 2 * per] + after(packed_second, sent_low).astype(f32)
    packed_third = dp.swap(packed_sum[per:].astype(bf16), 4)
    other = swap_x(small)

    reduced = reduced.astype(f32)
    summed_up = reduced[:per]
    summed_packed = packed_sum[:per] + after(packed_third, kept).astype(f32)
    summed_project = summed_packed[:, :head_width]
    summed_output = fold(summed_packed[:, head_width:], per)
    summed_project = (
        summed_project.reshape(per, 3, heads, HD).transpose(0, 2, 1, 3).reshape(per, head_width)
    )
    sent, kept, summed_up = join(sent, kept, summed_up)
    other = after(other, sent)
    both = jnp.stack([jnp.where(x == 0, small, other), jnp.where(x == 0, other, small)])
    far = swap_core(both)
    pieces = []
    for at in range(2):
        pieces += [jnp.where(c == 0, both[at], far[at]), jnp.where(c == 0, far[at], both[at])]
    summed_time = jnp.concatenate([piece[:, :width] for piece in pieces], axis=1)
    summed_input = jnp.concatenate([piece[:, width:] for piece in pieces], axis=1)
    grad_normed = kept + sent.astype(f32)
    grad_table = rscale * grad_normed - table * (
        rscale * rscale * rscale * jnp.mean(grad_normed * table, axis=1, keepdims=True)
    )
    return (
        block_out,
        grad_table,
        summed_input,
        summed_time,
        summed_project,
        summed_output,
        summed_up,
        summed_down,
    )


def normalize(table_rows):
    return table_rows * lax.rsqrt(
        jnp.mean(table_rows * table_rows, axis=1, keepdims=True) + table_eps
    )


def layer_norm(value, scale, shift):
    centred = value - jnp.mean(value, axis=-1, keepdims=True)
    return (
        centred
        * lax.rsqrt(jnp.mean(centred * centred, axis=-1, keepdims=True) + norm_eps)
        * (1.0 + scale)
        + shift
    )


def time_features(step_index, width):
    half = width // 2
    frequency = jnp.exp(-math.log(10000.0) * jnp.arange(half).astype(jnp.float32) / half)
    angles = step_index.astype(jnp.float32)[:, None] * frequency[None, :]
    return jnp.concatenate([jnp.sin(angles), jnp.cos(angles)], axis=1)


def gelu_exact(value):
    return jax.nn.gelu(value, approximate=False)


def whole_collectives(
    token_ids,
    lengths,
    time_steps,
    embed_table,
    input_weight,
    time_weight,
    project_weight,
    output_weight,
    up_weight,
    down_weight,
    cotangent,
):
    rows = token_ids.shape[0]
    groups = lax.axis_size("tensor")
    tensor_place = lax.axis_index("tensor")
    shard_rows = embed_table.shape[0]
    factor = 1.0 / math.sqrt(HD)
    normed, normed_back = jax.vjp(normalize, embed_table.astype(jnp.float32))
    normed_low = normed.astype(jnp.bfloat16)
    gathered = (
        lax.all_gather(input_weight, "dp", axis=0, tiled=True),
        lax.all_gather(time_weight, "dp", axis=0, tiled=True),
        lax.all_gather(project_weight, "dp", axis=0, tiled=True),
        lax.all_gather(output_weight, "dp", axis=1, tiled=True),
        lax.all_gather(up_weight, "dp", axis=0, tiled=True),
        lax.all_gather(down_weight, "dp", axis=1, tiled=True),
    )
    input_full, time_full, project_full, output_full, up_full, down_full = gathered

    def vocab_rows(count):
        flat_index = jnp.arange(count, dtype=jnp.int32)
        return (
            flat_index // shard_rows * groups + tensor_place
        ) * shard_rows + flat_index % shard_rows

    token_block = min(256, rows)
    piece = lax.all_gather(normed_low, "dp", axis=0, tiled=True)
    vocab = vocab_rows(piece.shape[0])
    parts = []
    for add_begin in range(0, rows, token_block):
        add_onehot = (
            token_ids[add_begin : add_begin + token_block, None] == vocab[None, :]
        ).astype(jnp.bfloat16)
        parts.append(jnp.dot(add_onehot, piece, preferred_element_type=jnp.float32))
    partial_embed = jnp.concatenate(parts, axis=0)
    embed = lax.psum(partial_embed.astype(jnp.bfloat16), "tensor")
    stream_zero = jnp.dot(embed, input_full, preferred_element_type=jnp.float32)
    ends = jnp.cumsum(lengths)
    position = jnp.arange(rows, dtype=jnp.int32)
    document = jnp.sum((position[:, None] >= ends[None, :]).astype(jnp.int32), axis=1)
    member = (document[:, None] == jnp.arange(lengths.shape[0], dtype=jnp.int32)[None, :]).astype(
        jnp.float32
    )
    features = time_features(time_steps, EMB).astype(jnp.bfloat16)
    modulation = jnp.dot(features, time_full, preferred_element_type=jnp.float32)
    row_mods = jnp.dot(member, modulation, precision=highest)
    scale_one, shift_one, scale_two, shift_two = jnp.split(row_mods, 4, axis=1)
    normed_one, norm_one_back = jax.vjp(layer_norm, stream_zero, scale_one, shift_one)
    hidden_one = normed_one.astype(jnp.bfloat16)
    projected = jnp.dot(hidden_one, project_full, preferred_element_type=jnp.float32).astype(
        jnp.bfloat16
    )
    heads_here = projected.shape[1] // (3 * HD)
    projected = projected.reshape(rows, heads_here, 3, HD)
    query = jnp.transpose(projected[:, :, 0], (1, 0, 2))
    keys = jnp.transpose(projected[:, :, 1], (1, 0, 2))
    values = jnp.transpose(projected[:, :, 2], (1, 0, 2))
    query_block = min(512, rows)

    def scores_of(begin):
        block_query = query[:, begin : begin + query_block]
        plain = (
            jnp.einsum("hqd,hkd->hqk", block_query, keys, preferred_element_type=jnp.float32)
            * factor
        )
        allowed = document[begin : begin + query_block, None] == document[None, :]
        return (jnp.where(allowed[None], plain, masked_score), block_query)

    outputs = []
    logsums = []
    kept_probs = []
    for begin in range(0, rows, query_block):
        scores, block_query = scores_of(begin)
        peak = jnp.max(scores, axis=2, keepdims=True)
        expo = jnp.exp(scores - peak)
        total = jnp.sum(expo, axis=2, keepdims=True)
        logsums.append(peak + jnp.log(total))
        probs_low = (expo / total).astype(jnp.bfloat16)
        kept_probs.append(probs_low)
        outputs.append(
            jnp.einsum("hqk,hkd->hqd", probs_low, values, preferred_element_type=jnp.float32)
        )
    attended = (
        jnp.transpose(jnp.concatenate(outputs, axis=1), (1, 0, 2))
        .reshape(rows, heads_here * HD)
        .astype(jnp.bfloat16)
    )
    attention_sum = lax.psum(
        jnp.dot(attended, output_full, preferred_element_type=jnp.float32), "tensor"
    )
    stream_one_rows = stream_zero + attention_sum
    normed_two, norm_two_back = jax.vjp(layer_norm, stream_one_rows, scale_two, shift_two)
    hidden_two = normed_two.astype(jnp.bfloat16)
    upward = jnp.dot(hidden_two, up_full, preferred_element_type=jnp.float32)
    activated, gelu_back = jax.vjp(gelu_exact, upward)
    activated_low = activated.astype(jnp.bfloat16)
    branch = lax.psum(
        jnp.dot(activated_low, down_full, preferred_element_type=jnp.float32), "tensor"
    )
    block_out = (stream_one_rows + branch).astype(jnp.bfloat16)
    grad_down = jnp.dot(activated_low.T, cotangent, preferred_element_type=jnp.float32)
    grad_active = jnp.dot(cotangent, down_full.T, preferred_element_type=jnp.float32)
    grad_upward = gelu_back(grad_active)[0].astype(jnp.bfloat16)
    grad_up = jnp.dot(hidden_two.T, grad_upward, preferred_element_type=jnp.float32)
    grad_hidden_two = lax.psum(
        jnp.dot(grad_upward, up_full.T, preferred_element_type=jnp.float32), "tensor"
    )
    grad_stream_rows, grad_scale_two, grad_shift_two = norm_two_back(grad_hidden_two)
    grad_stream_rows = grad_stream_rows + cotangent.astype(jnp.float32)
    grad_attn_rows = grad_stream_rows.astype(jnp.bfloat16)
    grad_output = jnp.dot(attended.T, grad_attn_rows, preferred_element_type=jnp.float32)
    grad_attended = jnp.dot(
        grad_attn_rows, output_full.T, preferred_element_type=jnp.float32
    ).astype(jnp.bfloat16)
    grad_attended = jnp.transpose(grad_attended.reshape(rows, heads_here, HD), (1, 0, 2))
    query_grads = []
    grad_keys = jnp.zeros(keys.shape, jnp.float32)
    grad_values = jnp.zeros(values.shape, jnp.float32)
    for number, begin in enumerate(range(0, rows, query_block)):
        scores, block_query = scores_of(begin)
        probs = jnp.exp(scores - logsums[number])
        block_grad = grad_attended[:, begin : begin + query_block]
        grad_probs = jnp.einsum(
            "hqd,hkd->hqk", block_grad, values, preferred_element_type=jnp.float32
        )
        inner = jnp.sum(probs * grad_probs, axis=2, keepdims=True)
        grad_scores = (probs * (grad_probs - inner)).astype(jnp.bfloat16)
        query_grads.append(
            jnp.einsum("hqk,hkd->hqd", grad_scores, keys, preferred_element_type=jnp.float32)
            * factor
        )
        grad_keys = (
            grad_keys
            + jnp.einsum(
                "hqk,hqd->hkd", grad_scores, block_query, preferred_element_type=jnp.float32
            )
            * factor
        )
        grad_values = grad_values + jnp.einsum(
            "hqk,hqd->hkd", kept_probs[number], block_grad, preferred_element_type=jnp.float32
        )
    grad_query = jnp.concatenate(query_grads, axis=1)
    grad_projected = jnp.stack([grad_query, grad_keys, grad_values], axis=2)
    grad_projected = (
        jnp.transpose(grad_projected, (1, 0, 2, 3))
        .reshape(rows, heads_here * 3 * HD)
        .astype(jnp.bfloat16)
    )
    grad_project = jnp.dot(hidden_one.T, grad_projected, preferred_element_type=jnp.float32)
    grad_hidden_one = lax.psum(
        jnp.dot(grad_projected, project_full.T, preferred_element_type=jnp.float32), "tensor"
    )
    grad_stream_zero, grad_scale_one, grad_shift_one = norm_one_back(grad_hidden_one)
    grad_zero_low = (grad_stream_zero + grad_stream_rows).astype(jnp.bfloat16)
    grad_rows = jnp.concatenate(
        [grad_scale_one, grad_shift_one, grad_scale_two, grad_shift_two], axis=1
    )
    partial_modulation = jnp.dot(member.T, grad_rows, precision=highest)
    grad_stream_zero = grad_zero_low
    grad_input = jnp.dot(embed.T, grad_stream_zero, preferred_element_type=jnp.float32)
    grad_embed = jnp.dot(grad_stream_zero, input_full.T, preferred_element_type=jnp.float32).astype(
        jnp.bfloat16
    )
    grad_time = jnp.dot(features.astype(jnp.float32).T, partial_modulation, precision=highest)
    every_row = shard_rows * lax.axis_size("dp")
    vocab_all = vocab_rows(every_row)
    grad_normed = jnp.zeros((every_row, EMB), jnp.float32)
    for begin in range(0, rows, token_block):
        onehot = (token_ids[begin : begin + token_block, None] == vocab_all[None, :]).astype(
            jnp.bfloat16
        )
        grad_normed = grad_normed + jnp.einsum(
            "tv,te->ve",
            onehot,
            grad_embed[begin : begin + token_block],
            preferred_element_type=jnp.float32,
        )
    (
        summed_input,
        summed_time,
        summed_project,
        summed_output,
        summed_up,
        summed_down,
        summed_table,
    ) = (
        lax.psum_scatter(grad_input, "dp", scatter_dimension=0, tiled=True),
        lax.psum_scatter(grad_time, "dp", scatter_dimension=0, tiled=True),
        lax.psum_scatter(grad_project, "dp", scatter_dimension=0, tiled=True),
        lax.psum_scatter(grad_output, "dp", scatter_dimension=1, tiled=True),
        lax.psum_scatter(grad_up, "dp", scatter_dimension=0, tiled=True),
        lax.psum_scatter(grad_down, "dp", scatter_dimension=1, tiled=True),
        lax.psum_scatter(grad_normed, "dp", scatter_dimension=0, tiled=True),
    )
    grad_table = normed_back(summed_table)[0]
    return (
        block_out,
        grad_table,
        summed_input,
        summed_time,
        summed_project,
        summed_output,
        summed_up,
        summed_down,
    )


def solution(mesh):
    count, groups = mesh.shape["dp"], mesh.shape["tensor"]
    return jax.shard_map(
        per_device if count == len(ORDER) and groups == 4 else whole_collectives,
        mesh=mesh,
        in_specs=(
            P("dp"),
            P("dp"),
            P("dp"),
            P(("dp", "tensor"), None),
            P("dp", None),
            P("dp", None),
            P("dp", "tensor"),
            P("tensor", "dp"),
            P("dp", "tensor"),
            P("tensor", "dp"),
            P("dp", None),
        ),
        out_specs=(
            P("dp", None),
            P(("dp", "tensor"), None),
            P("dp", None),
            P("dp", None),
            P("dp", "tensor"),
            P("tensor", "dp"),
            P("dp", "tensor"),
            P("tensor", "dp"),
        ),
        check_vma=False,
    )
```
